32 devices in a mesh: dp: 4 (over y, x), head: 8 (over z, core).
Axes of the slice: x: 2, y: 2, z: 4, core: 2. Of those that a mesh axis runs over, the one named last changes fastest.
Arguments:
- stream: bfloat16 [8192, 2048], P(('dp', 'head')), may hold values from -4 to 4
- doc_lengths: int32 [4, 8], P('dp'), may hold values from 1 to 1024, 2048 in all within a row
- premix_gain: bfloat16 [2048], replicated, may hold values from 0.099609375 to 1.8984375
- branch_weight: bfloat16 [2048, 2736], P(None, 'head'), may hold values from -0.125 to 0.125
- input_weight: bfloat16 [2048, 2736], P(None, 'head'), may hold values from -0.125 to 0.125
- conv_kernel: bfloat16 [4, 2736], P(None, 'head'), may hold values from -3 to 3
- conv_bias: bfloat16 [2736], P('head'), may hold values from -3 to 3
- rate_weight: bfloat16 [16, 171, 171], P('head'), may hold values from -0.4375 to 0.4375
- rate_bias: bfloat16 [16, 171], P('head'), may hold values from -3 to 3
- entry_weight: bfloat16 [16, 171, 171], P('head'), may hold values from -0.4375 to 0.4375
- entry_bias: bfloat16 [16, 171], P('head'), may hold values from -3 to 3
- decay_param: bfloat16 [2736], P('head'), may hold values from -9 to -3
- output_weight: bfloat16 [2736, 2048], P('head'), may hold values from -0.625 to 0.625
- preffn_gain: bfloat16 [2048], replicated, may hold values from 0.099609375 to 1.8984375
- ffn_gate: bfloat16 [2048, 6144], P(None, 'head'), may hold values from -0.125 to 0.125
- ffn_upward: bfloat16 [2048, 6144], P(None, 'head'), may hold values from -1 to 1
- ffn_down: bfloat16 [2048, 6144], P(None, 'head'), may hold values from -1 to 1
- cotangent: bfloat16 [8192, 2048], P(('dp', 'head')), may hold values from -4 to 4
Outputs:
- layer_out: bfloat16 [8192, 2048], P(('dp', 'head'))
- stream_grad: bfloat16 [8192, 2048], P(('dp', 'head'))
- premix_grad: float32 [2048], replicated
- branch_grad: float32 [2048, 2736], P(None, 'head')
- input_grad: float32 [2048, 2736], P(None, 'head')
- kernel_grad: float32 [4, 2736], P(None, 'head')
- convbias_grad: float32 [2736], P('head')
- rate_grad: float32 [16, 171, 171], P('head')
- ratebias_grad: float32 [16, 171], P('head')
- entry_grad: float32 [16, 171, 171], P('head')
- entrybias_grad: float32 [16, 171], P('head')
- decay_grad: float32 [2736], P('head')
- output_grad: float32 [2736, 2048], P('head')
- preffn_grad: float32 [2048], replicated
- ffngate_grad: float32 [2048, 6144], P('dp', 'head')
- ffnupward_grad: float32 [2048, 6144], P('dp', 'head')
- ffndown_grad: float32 [2048, 6144], P('dp', 'head')
The draws below stay inside these ranges and needn't reach their ends.
Inputs may be any that keep to these rules, and one draw needn't show every extreme that they name: `doc_lengths`: each row's 8 document lengths add up to 2048, and the longest is exactly 1024.
All inputs are finite; a program needn't handle non-finite values.
Results may differ from the reference program's by a relative error of at most 0.025.
Values may be sent and summed in bfloat16 or wider, within the bound.
A program may use at most 576 MiB of HBM per device.

```python
import math
import jax
import jax.numpy as jnp
import numpy as np
from jax import lax

D = 2048
FF = 6144
R = 2736
HEADS = 16
CONVW = 4
SEQ = 2048
NDOC = 8
ROWS_DEV = 1
HS = 171
MOST = 1024
ROWS = 4
TOKENS = 8192


def token_common(key):
    return jnp.clip(jax.random.normal(jax.random.fold_in(key, 101), (TOKENS, D), jnp.float32), -4.0, 4.0)


def weight_common(key):
    return jnp.clip(jax.random.normal(jax.random.fold_in(key, 202), (D, FF), jnp.float32), -4.0, 4.0)


def draw_stream(key, part):
    shared = token_common(key)
    return shared.astype(jnp.bfloat16)


def draw_cotangent(key, part):
    shared = token_common(key)
    key = jax.random.fold_in(key, 2)
    own = jnp.clip(jax.random.normal(key, (TOKENS, D), jnp.float32), -4.0, 4.0)
    return jnp.clip(0.6 * shared + 0.8 * own, -4.0, 4.0).astype(jnp.bfloat16)


def draw_ffn_upward(key, part):
    shared = weight_common(key)
    factor = D ** (-0.5)
    return (shared * factor).astype(jnp.bfloat16)


def draw_ffn_down(key, part):
    shared = weight_common(key)
    key = jax.random.fold_in(key, 4)
    own = jnp.clip(jax.random.normal(key, (D, FF), jnp.float32), -4.0, 4.0)
    factor = (2.0 / FF) ** 0.5
    return ((0.75 * shared + 0.66 * own) * factor).astype(jnp.bfloat16)


def block_levels(stream_key, shape, split, low, largest):
    loudness, own = 1.0, jax.random.fold_in(stream_key, 6)
    for position, shards_of in split:
        draws = jnp.exp(jax.random.uniform(jax.random.fold_in(own, position), (shards_of,), jnp.float32, low / len(split), largest / len(split)))
        loudness = loudness * jnp.repeat(draws, shape[position] // shards_of).reshape([-1 if axis == position else 1 for axis in range(len(shape))])
    return loudness


def length_profile(number_of, total, limit, slope):
    portions = [(1 << 20) // math.isqrt(rank ** slope) + 1 for rank in range(2, number_of + 1)]
    spare, given = total - limit - (number_of - 1), [1] * (number_of - 1)
    while spare > 0:
        movable = [i for i in range(number_of - 1) if given[i] < limit]
        mass, left = sum([portions[i] for i in movable]), spare
        for i in movable:
            addition = min(limit - given[i], max(1, left * portions[i] // mass), spare)
            given[i] = given[i] + addition
            spare = spare - addition
    return np.array([limit] + given)


def ragged(stream_key, amount, total, reach, skew):
    if amount == 2:
        one = jax.random.randint(stream_key, (), max(1, total - reach), min(reach, total - 1) + 1)
        return jnp.stack([one, total - one])
    sizes = jnp.asarray(length_profile(amount, total, reach, skew), jnp.int32)
    twos = (amount - 1) // 2
    giver, receiver = sizes[1:1 + 2 * twos:2], sizes[2:2 + 2 * twos:2]
    room = jnp.minimum(giver - 1, reach - receiver)
    moved = jax.random.randint(jax.random.fold_in(stream_key, 1), (twos,), 0, 1 << 20) % (room + 1)
    sizes = sizes.at[1:1 + 2 * twos:2].set(giver - moved).at[2:2 + 2 * twos:2].set(receiver + moved)
    return sizes[jax.random.permutation(jax.random.fold_in(stream_key, 2), amount)]


def bell_draw(rng, shape, scale, limit, pieces=(), held_as=jnp.bfloat16):
    factor_of = block_levels(rng, shape, pieces, -0.22, 0.18) if pieces else 1.0
    drawn = jax.random.normal(rng, shape, jnp.float32) * scale * factor_of
    return jnp.minimum(jnp.maximum(drawn, -limit), limit).astype(held_as)


def setup_inputs(seed: int = 0) -> dict:
    streams_of = jax.random.split(jax.random.key(seed), 19)
    return {
        "stream": draw_stream(jax.random.fold_in(streams_of[18], 71), 0),
        "doc_lengths": jax.vmap(lambda own: ragged(own, NDOC, SEQ, MOST, 2))(jax.random.split(streams_of[1], ROWS)).reshape((ROWS, NDOC)).astype(jnp.int32),
        "premix_gain": jnp.clip(1.0 + 0.18 * jax.random.normal(streams_of[2], (D,), jnp.float32), 0.099609375, 1.8984375).astype(jnp.bfloat16),
        "branch_weight": bell_draw(streams_of[3], (D, R), D ** -0.5, 0.125, ((1, 8),)),
        "input_weight": bell_draw(streams_of[4], (D, R), D ** -0.5, 0.125, ((1, 8),)),
        "conv_kernel": bell_draw(streams_of[5], (CONVW, R), CONVW ** -0.5, 3.0, ((1, 8),)),
        "conv_bias": bell_draw(streams_of[6], (R,), 0.5, 3.0, ((0, 8),)),
        "rate_weight": bell_draw(streams_of[7], (HEADS, HS, HS), HS ** -0.5, 0.4375, ((0, 8),)),
        "rate_bias": bell_draw(streams_of[8], (HEADS, HS), 1.0, 3.0, ((0, 8),)),
        "entry_weight": bell_draw(streams_of[9], (HEADS, HS, HS), HS ** -0.5, 0.4375, ((0, 8),)),
        "entry_bias": bell_draw(streams_of[10], (HEADS, HS), 1.0, 3.0, ((0, 8),)),
        "decay_param": jnp.clip(-9.0 + 6.0 * jax.random.uniform(streams_of[11], (R,), jnp.float32) ** block_levels(streams_of[11], (R,), ((0, 8),), -0.2, 0.2), -9.0, -3.0).astype(jnp.bfloat16),
        "output_weight": bell_draw(streams_of[12], (R, D), (R // 32) ** -0.5, 0.625, ((0, 8),)),
        "preffn_gain": jnp.clip(1.0 + 0.18 * jax.random.normal(streams_of[13], (D,), jnp.float32), 0.099609375, 1.8984375).astype(jnp.bfloat16),
        "ffn_gate": bell_draw(streams_of[14], (D, FF), D ** -0.5, 0.125, ((1, 8),)),
        "ffn_upward": draw_ffn_upward(jax.random.fold_in(streams_of[18], 71), 0),
        "ffn_down": draw_ffn_down(jax.random.fold_in(streams_of[18], 71), 0),
        "cotangent": draw_cotangent(jax.random.fold_in(streams_of[18], 71), 0),
    }


EPSILON = 1e-06
HIGHEST = lax.Precision.HIGHEST
DECAY_SCALE = 8.0

@jax.custom_vjp
def low(v):
    return lax.optimization_barrier(v.astype(jnp.bfloat16)).astype(jnp.float32)

@jax.custom_vjp
def low_back(v):
    return v

def low_keep(v):
    return (low(v), None)

def low_pass(kept, grad):
    return (grad,)

def back_keep(v):
    return (v, None)

def back_low(kept, grad):
    return (low(grad),)
low.defvjp(low_keep, low_pass)
low_back.defvjp(back_keep, back_low)

def rms_norm(values, scales):
    return values * lax.rsqrt(lax.optimization_barrier(jnp.mean(values * values, axis=-1, keepdims=True)) + EPSILON) * scales

def gated_unit(gate_pre, upward_pre):
    return jax.nn.gelu(gate_pre) * upward_pre

def doc_masks(lengths, length):
    starts = jnp.cumsum(lengths, axis=1) - lengths
    places = jnp.arange(length, dtype=jnp.int32)
    resets = jnp.any(starts[:, :, None] == places[None, None, :], axis=1)
    earlier = jnp.where(starts[:, :, None] <= places[None, None, :], starts[:, :, None], 0)
    begins = lax.optimization_barrier(jnp.max(earlier, axis=1))
    shifts = jnp.arange(CONVW, dtype=jnp.int32)
    inside = places[None, :, None] - shifts[None, None, :] >= begins[:, :, None]
    return (resets, inside.astype(jnp.float32))

def pair_combine(earlier, latter):
    return (earlier[0] * latter[0], latter[0] * earlier[1] + latter[1])

def recurrence(branch_pre, input_pre, kernel, kernel_bias, rate_weight, rate_bias, entry_weight, entry_bias, decay_param, resets, inside):
    length = input_pre.shape[1]
    convolved = kernel_bias + kernel[0] * input_pre
    for offset in range(1, kernel.shape[0]):
        shifted = jnp.pad(input_pre, ((0, 0), (offset, 0), (0, 0)))[:, :length]
        convolved = convolved + kernel[offset] * shifted * inside[:, :, offset:offset + 1]
    blocks = convolved.reshape(convolved.shape[0], length, rate_weight.shape[0], rate_weight.shape[1])
    rate_gate = jax.nn.sigmoid(jnp.einsum('rthc,hcd->rthd', blocks, rate_weight, precision=HIGHEST) + rate_bias).reshape(convolved.shape)
    entry_gate = jax.nn.sigmoid(jnp.einsum('rthc,hcd->rthd', blocks, entry_weight, precision=HIGHEST) + entry_bias).reshape(convolved.shape)
    log_decay = -DECAY_SCALE * jax.nn.softplus(decay_param) * rate_gate
    scaling = jnp.where(resets[:, :, None], 1.0, jnp.sqrt(-jnp.expm1(2.0 * log_decay)))
    carried = jnp.where(resets[:, :, None], 0.0, jnp.exp(log_decay))
    _, states = lax.associative_scan(pair_combine, (carried, scaling * entry_gate * convolved), axis=1)
    return states * jax.nn.gelu(branch_pre)

def matmul(leading, trailing):
    return jnp.dot(leading, trailing, precision=HIGHEST)

def block_forward(params, inflow, resets, inside):
    premix_gain, branch_weight, input_weight, conv_kernel, conv_bias, rate_weight, rate_bias, entry_weight, entry_bias, decay_param, output_weight, preffn_gain, ffn_gate, ffn_upward, ffn_down = params
    row_count = resets.shape[0]
    normed = low(rms_norm(inflow, premix_gain))
    branch_pre = low_back(matmul(normed, branch_weight)).reshape(row_count, SEQ, R)
    input_pre = low_back(matmul(normed, input_weight)).reshape(row_count, SEQ, R)
    mixer_core = jax.checkpoint(recurrence)
    gated_out = low(mixer_core(branch_pre, input_pre, conv_kernel, conv_bias, rate_weight, rate_bias, entry_weight, entry_bias, decay_param, resets, inside).reshape(-1, R))
    hidden_in = inflow + low_back(matmul(gated_out, output_weight))
    ffn_normed = low(rms_norm(hidden_in, preffn_gain))
    gate_pre = low_back(matmul(ffn_normed, ffn_gate))
    upward_pre = low_back(matmul(ffn_normed, ffn_upward))
    hidden_low = low(gated_unit(gate_pre, upward_pre))
    ffn_out = low_back(jnp.dot(hidden_low, ffn_down.T, precision=HIGHEST))
    return hidden_in + ffn_out

def reference(stream, doc_lengths, premix_gain, branch_weight, input_weight, conv_kernel, conv_bias, rate_weight, rate_bias, entry_weight, entry_bias, decay_param, output_weight, preffn_gain, ffn_gate, ffn_upward, ffn_down, cotangent):
    params = tuple((tensor.astype(jnp.float32) for tensor in (premix_gain, branch_weight, input_weight, conv_kernel, conv_bias, rate_weight, rate_bias, entry_weight, entry_bias, decay_param, output_weight, preffn_gain, ffn_gate, ffn_upward, ffn_down)))
    groups = doc_lengths.shape[0] // ROWS_DEV
    inflows = stream.astype(jnp.float32).reshape(groups, ROWS_DEV * SEQ, D)
    upstreams = cotangent.astype(jnp.float32).reshape(groups, ROWS_DEV * SEQ, D)
    lengths = doc_lengths.reshape(groups, ROWS_DEV, NDOC)

    def group_step(totals, entries):
        inflow, upstream, group_lengths = entries
        resets, inside = doc_masks(group_lengths, SEQ)

        def forward(params_in, inflow_in):
            return block_forward(params_in, inflow_in, resets, inside)
        result, backward = jax.vjp(forward, params, inflow)
        param_grads, inflow_grad = backward(upstream)
        totals = jax.tree.map(jnp.add, totals, param_grads)
        return (totals, (result, inflow_grad))
    totals, (results, inflow_grads) = lax.scan(group_step, jax.tree.map(jnp.zeros_like, params), (inflows, upstreams, lengths))
    return (results.reshape(-1, D).astype(jnp.bfloat16), inflow_grads.reshape(-1, D).astype(jnp.bfloat16), totals[0], totals[1], totals[2], totals[3], totals[4], totals[5], totals[6], totals[7], totals[8], totals[9], totals[10], totals[11], totals[12], totals[13], totals[14])
```

```python
import functools
import math

import jax
import jax.numpy as jnp
from jax import lax
from jax.experimental import pallas as pl
from jax.experimental.pallas import tpu as pltpu
from jax.sharding import PartitionSpec as P

CONVW = 4
SEQ = 2048
CHUNK = 256
BLOCK = 64
LANES = 128
HALO = 8

EPSILON = 1e-06
DECAY_SCALE = 8.0
GELU_A = math.sqrt(2.0 / math.pi)
GELU_B = 0.044715

BIAS, TAP, RATE_B, ENTRY_B, DECAY = 0, 1, 5, 6, 7
PARAMS = 8
G_BIAS, G_TAP, G_RATE, G_ENTRY, G_DECAY = 0, 1, 5, 6, 7


def rms_parts(values):
    rinv = lax.rsqrt(jnp.mean(values * values, axis=-1, keepdims=True) + EPSILON)
    return rinv, values * rinv


def norm_back(unit, rinv, gain, grad):
    q = gain * grad
    return rinv * (q - unit * jnp.mean(q * unit, axis=-1, keepdims=True))


def contract_cols(leading, trailing):
    return lax.dot_general(
        leading, trailing, (((1,), (1,)), ((), ())), preferred_element_type=jnp.float32
    )


def contract_rows(leading, trailing):
    return lax.dot_general(
        leading, trailing, (((0,), (0,)), ((), ())), preferred_element_type=jnp.float32
    )


def gelu_pair(v):
    sq = v * v
    th = jnp.tanh(GELU_A * v * (1.0 + GELU_B * sq))
    half = 0.5 * (1.0 + th)
    slope = half + 0.5 * v * (1.0 - th * th) * (GELU_A * (1.0 + 3.0 * GELU_B * sq))
    return v * half, slope


def gelu(v):
    return v * (0.5 * (1.0 + jnp.tanh(GELU_A * v * (1.0 + GELU_B * v * v))))


def decay_terms(rate_gate, slope, fresh):
    log_decay = slope * rate_gate
    c = jnp.exp(log_decay)
    y = 2.0 * log_decay
    series = 1.0 + y * (1.0 / 7.0)
    for n in (6, 5, 4, 3, 2):
        series = 1.0 + (y * (1.0 / n)) * series
    sq = c * c
    q = jnp.where(y > -0.5, -y * series, 1.0 - sq)
    rsq = lax.rsqrt(jnp.maximum(q, 1e-37))
    return (
        jnp.where(fresh, 0.0, c),
        jnp.where(fresh, 1.0, q * rsq),
        jnp.where(fresh, 0.0, sq * rsq),
    )


def rec_fwd_kernel(pre, pos, wg, par, u_out, r_out, e_out, h_out, gated, xbuf, z, carry):
    width = u_out.shape[1]
    tiles = width // LANES

    @pl.when(pl.program_id(0) == 0)
    def _():
        xbuf[0:HALO, :] = jnp.zeros((HALO, width), jnp.float32)
        carry[...] = jnp.zeros_like(carry)

    @pl.when(pl.program_id(0) > 0)
    def _():
        xbuf[0:HALO, :] = xbuf[CHUNK : CHUNK + HALO, :]

    xbuf[HALO : HALO + CHUNK, :] = pre[:, width:]

    def conv_step(i, _):
        row = pl.multiple_of(i * BLOCK, BLOCK)
        place = pos[pl.ds(row, BLOCK), :]
        for t in range(tiles):
            cols = pl.ds(t * LANES, LANES)
            xs = xbuf[pl.ds(row, BLOCK + HALO), cols]
            total = par[BIAS : BIAS + 1, cols] + par[TAP : TAP + 1, cols] * xs[HALO:]
            for k in range(1, CONVW):
                term = par[TAP + k : TAP + k + 1, cols] * xs[HALO - k : HALO - k + BLOCK]
                total = total + jnp.where(place >= k, term, 0.0)
            u_out[pl.ds(row, BLOCK), cols] = total
        return 0

    lax.fori_loop(0, CHUNK // BLOCK, conv_step, 0)
    z[...] = jnp.dot(u_out[...].astype(jnp.bfloat16), wg[...], preferred_element_type=jnp.float32)

    def scan_step(i, _):
        row = pl.multiple_of(i * BLOCK, BLOCK)
        rows = pl.ds(row, BLOCK)
        fresh = pos[rows, :] == 0
        inner = lax.broadcasted_iota(jnp.int32, (BLOCK, LANES), 0) % 8
        for t in range(tiles):
            cols = pl.ds(t * LANES, LANES)
            other = pl.ds(width + t * LANES, LANES)
            r = jax.nn.sigmoid(z[rows, cols] + par[RATE_B : RATE_B + 1, cols])
            e = jax.nn.sigmoid(z[rows, other] + par[ENTRY_B : ENTRY_B + 1, cols])
            u = u_out[rows, cols]
            c, m, _ = decay_terms(r, par[DECAY : DECAY + 1, cols], fresh)
            r_out[rows, cols] = r
            e_out[rows, cols] = e
            b = m * e * u
            for d in (1, 2, 4):
                near = inner >= d
                b = b + c * jnp.where(near, pltpu.roll(b, d, 0), 0.0)
                c = c * jnp.where(near, pltpu.roll(c, d, 0), 1.0)
            last = carry[0:1, cols]
            pieces = []
            for g in range(BLOCK // 8):
                part = slice(g * 8, g * 8 + 8)
                state = b[part] + c[part] * last
                last = state[7:8]
                pieces.append(state)
            carry[0:1, cols] = last
            h = jnp.concatenate(pieces, axis=0)
            h_out[rows, cols] = h
            gated[rows, cols] = (h * gelu(pre[rows, cols])).astype(jnp.bfloat16)
        return 0

    lax.fori_loop(0, CHUNK // BLOCK, scan_step, 0)


def rec_fwd(pre, pos, wg, par):
    length, width = pre.shape[0], pre.shape[1] // 2
    rows = lambda cols: pl.BlockSpec((CHUNK, cols), lambda i: (i, 0))
    whole = lambda a: pl.BlockSpec(a.shape, lambda i: (0,) * a.ndim)
    wide = jax.ShapeDtypeStruct((length, width), jnp.float32)
    return pl.pallas_call(
        rec_fwd_kernel,
        grid=(length // CHUNK,),
        out_shape=(wide, wide, wide, wide, jax.ShapeDtypeStruct((length, width), jnp.bfloat16)),
        in_specs=[rows(2 * width), rows(LANES), whole(wg), whole(par)],
        out_specs=[rows(width)] * 5,
        scratch_shapes=[
            pltpu.VMEM((CHUNK + HALO, width), jnp.float32),
            pltpu.VMEM((CHUNK, 2 * width), jnp.float32),
            pltpu.VMEM((8, width), jnp.float32),
        ],
        compiler_params=pltpu.CompilerParams(vmem_limit_bytes=40 * 2**20),
        name="recurrence_forward",
    )(pre, pos, wg, par)


def rec_bwd_kernel(
    gg, pre, pre_halo, pos, u_in, r_in, e_in, h_in, h_halo, wg, par,
    dpre, dgate, dpar, dz, du, pbuf, carry,
):
    width = u_in.shape[1]
    tiles = width // LANES
    step = pl.program_id(0)

    @pl.when(step == 0)
    def _():
        du[CHUNK:, :] = jnp.zeros((HALO, width), jnp.float32)
        pbuf[CHUNK:, :] = jnp.zeros((HALO, LANES), jnp.int32)
        carry[...] = jnp.zeros_like(carry)
        dgate[...] = jnp.zeros_like(dgate)
        dpar[...] = jnp.zeros_like(dpar)

    @pl.when(step > 0)
    def _():
        du[CHUNK:, :] = du[0:HALO, :]
        pbuf[CHUNK:, :] = pbuf[0:HALO, :]

    pbuf[0:CHUNK, :] = pos[...]

    def total(v):
        return jnp.sum(v, axis=0, keepdims=True)

    def scan_step(j, _):
        i = CHUNK // BLOCK - 1 - j
        row = pl.multiple_of(i * BLOCK, BLOCK)
        rows = pl.ds(row, BLOCK)
        fresh = pos[rows, :] == 0
        place = lax.broadcasted_iota(jnp.int32, (BLOCK, LANES), 0)
        inner = place % 8
        before = pl.multiple_of(jnp.maximum(row - 8, 0), 8)
        for t in range(tiles):
            cols = pl.ds(t * LANES, LANES)
            other = pl.ds(width + t * LANES, LANES)
            r, e, u, h = r_in[rows, cols], e_in[rows, cols], u_in[rows, cols], h_in[rows, cols]
            grad = gg[rows, cols]
            act, slope = gelu_pair(pre[rows, cols])
            dpre[rows, cols] = (grad * h * slope).astype(jnp.bfloat16)
            dh = grad * act
            decay = par[DECAY : DECAY + 1, cols]
            c, m, ratio = decay_terms(r, decay, fresh)
            b, a = c * dh, c
            for d in (1, 2, 4):
                near = inner < 8 - d
                b = b + a * jnp.where(near, pltpu.roll(b, BLOCK - d, 0), 0.0)
                a = a * jnp.where(near, pltpu.roll(a, BLOCK - d, 0), 1.0)
            later = carry[0:1, cols]
            pieces = []
            first = later
            for g in reversed(range(BLOCK // 8)):
                part = slice(g * 8, g * 8 + 8)
                state = b[part] + a[part] * first
                first = state[0:1]
                pieces.append(state)
            carry[0:1, cols] = first
            mu = jnp.concatenate(pieces[::-1], axis=0)
            adj = dh + jnp.where(place == BLOCK - 1, later, pltpu.roll(mu, BLOCK - 1, 0))
            edge = jnp.where(i == 0, h_halo[7:8, cols], h_in[pl.ds(before, 8), cols][7:8])
            prior = jnp.where(place == 0, edge, pltpu.roll(h, 1, 0))
            eu = e * u
            dlog = adj * (prior * c - eu * ratio)
            dpar[G_DECAY : G_DECAY + 1, cols] += total(dlog * r)
            dzr = decay * dlog * (r * (1.0 - r))
            dze = adj * m * eu * (1.0 - e)
            dpar[G_RATE : G_RATE + 1, cols] += total(dzr)
            dpar[G_ENTRY : G_ENTRY + 1, cols] += total(dze)
            dz[rows, cols] = dzr.astype(jnp.bfloat16)
            dz[rows, other] = dze.astype(jnp.bfloat16)
            du[rows, cols] = adj * m * e
        return 0

    lax.fori_loop(0, CHUNK // BLOCK, scan_step, 0)
    du[0:CHUNK, :] += contract_cols(dz[...], wg[...])
    dgate[...] += contract_rows(u_in[...].astype(jnp.bfloat16), dz[...])

    def conv_step(i, _):
        row = pl.multiple_of(i * BLOCK, BLOCK)
        rows = pl.ds(row, BLOCK)
        before = pl.multiple_of(jnp.maximum(row - 8, 0), 8)
        place = pbuf[pl.ds(row, BLOCK + HALO), :]
        for t in range(tiles):
            cols = pl.ds(t * LANES, LANES)
            other = pl.ds(width + t * LANES, LANES)
            ds = du[pl.ds(row, BLOCK + HALO), cols]
            near = ds[0:BLOCK]
            x = pre[rows, other]
            head = jnp.where(i == 0, pre_halo[:, other], pre[pl.ds(before, 8), other])
            xs = jnp.concatenate([head, x], axis=0)
            dx = par[TAP : TAP + 1, cols] * near
            dpar[G_BIAS : G_BIAS + 1, cols] += total(near)
            dpar[G_TAP : G_TAP + 1, cols] += total(near * x)
            for k in range(1, CONVW):
                inside = jnp.where(place >= k, ds, 0.0)
                dx = dx + par[TAP + k : TAP + k + 1, cols] * inside[k : k + BLOCK]
                dpar[G_TAP + k : G_TAP + k + 1, cols] += total(
                    inside[0:BLOCK] * xs[HALO - k : HALO - k + BLOCK]
                )
            dpre[rows, other] = dx.astype(jnp.bfloat16)
        return 0

    lax.fori_loop(0, CHUNK // BLOCK, conv_step, 0)


def rec_bwd(gg, pre, pos, u, r, e, h, wg, par):
    length, width = u.shape
    count = length // CHUNK
    rows = lambda cols: pl.BlockSpec((CHUNK, cols), lambda i: (count - 1 - i, 0))
    halo = lambda cols: pl.BlockSpec(
        (HALO, cols), lambda i: (jnp.maximum((count - 1 - i) * (CHUNK // HALO) - 1, 0), 0)
    )
    whole = lambda shape: pl.BlockSpec(shape, lambda i: (0,) * len(shape))
    return pl.pallas_call(
        rec_bwd_kernel,
        grid=(count,),
        out_shape=(
            jax.ShapeDtypeStruct((length, 2 * width), jnp.bfloat16),
            jax.ShapeDtypeStruct((width, 2 * width), jnp.float32),
            jax.ShapeDtypeStruct((PARAMS, width), jnp.float32),
        ),
        in_specs=[
            rows(width), rows(2 * width), halo(2 * width), rows(LANES),
            rows(width), rows(width), rows(width), rows(width), halo(width),
            whole(wg.shape), whole(par.shape),
        ],
        out_specs=[rows(2 * width), whole((width, 2 * width)), whole((PARAMS, width))],
        scratch_shapes=[
            pltpu.VMEM((CHUNK, 2 * width), jnp.bfloat16),
            pltpu.VMEM((CHUNK + HALO, width), jnp.float32),
            pltpu.VMEM((CHUNK + HALO, LANES), jnp.int32),
            pltpu.VMEM((8, width), jnp.float32),
        ],
        compiler_params=pltpu.CompilerParams(vmem_limit_bytes=40 * 2**20),
        name="recurrence_backward",
    )(gg, pre, pre, pos, u, r, e, h, h, wg, par)


def places(lengths):
    starts = jnp.cumsum(lengths, axis=1) - lengths
    spots = jnp.arange(SEQ, dtype=jnp.int32)
    earlier = jnp.where(starts[:, :, None] <= spots[None, None, :], starts[:, :, None], 0)
    return (spots[None, :] - jnp.max(earlier, axis=1))[0]


def widen(values, width):
    return jnp.pad(values, ((0, 0), (0, width - values.shape[1])))


def block_diagonal(weights, width):
    heads, size = weights.shape[0], weights.shape[1]
    placed = [
        jnp.pad(weights[i], ((i * size, width - (i + 1) * size),) * 2) for i in range(heads)
    ]
    return functools.reduce(jnp.add, placed)


def diagonal_blocks(dense, heads, size):
    return jnp.stack(
        [dense[i * size : (i + 1) * size, i * size : (i + 1) * size] for i in range(heads)]
    )


def shards(
    stream, doc_lengths, premix_gain, branch_weight, input_weight, conv_kernel, conv_bias,
    rate_weight, rate_bias, entry_weight, entry_bias, decay_param, output_weight, preffn_gain,
    ffn_gate, ffn_upward, ffn_down, cotangent,
):
    f32, bf16 = jnp.float32, jnp.bfloat16
    heads, size = rate_bias.shape
    chans = branch_weight.shape[1]
    width = -(-chans // LANES) * LANES
    group = lax.axis_size("dp")

    pos = jnp.broadcast_to(places(doc_lengths)[:, None], (SEQ, LANES))
    slope = -DECAY_SCALE * jax.nn.softplus(decay_param.astype(f32))
    par = jnp.concatenate(
        [
            conv_bias[None].astype(f32),
            conv_kernel.astype(f32),
            rate_bias.reshape(1, -1).astype(f32),
            entry_bias.reshape(1, -1).astype(f32),
            slope[None],
        ]
    )
    par = jnp.pad(par, ((0, 0), (0, width - chans)), constant_values=-1.0)
    par = jnp.where((jnp.arange(width)[None] < chans) | (jnp.arange(PARAMS)[:, None] == DECAY), par, 0.0)
    wg = jnp.concatenate(
        [block_diagonal(rate_weight, width), block_diagonal(entry_weight, width)], axis=1
    )
    wbi = jnp.concatenate([widen(branch_weight, width), widen(input_weight, width)], axis=1)
    wo = jnp.pad(output_weight, ((0, width - chans), (0, 0)))

    inflow = stream.astype(f32)
    premix = premix_gain.astype(f32)
    rinv1, unit1 = rms_parts(inflow)
    normed = (unit1 * premix).astype(bf16)
    normed_rows = lax.all_gather(normed, "head", axis=0, tiled=True)
    pre = jnp.dot(normed_rows, wbi, preferred_element_type=f32)
    u, r, e, h, gated = rec_fwd(pre, pos, wg, par)
    mixer_out = lax.psum_scatter(
        jnp.dot(gated, wo, preferred_element_type=f32).astype(bf16),
        "head", scatter_dimension=0, tiled=True,
    )
    hidden_in = inflow + mixer_out.astype(f32)

    preffn = preffn_gain.astype(f32)
    rinv2, unit2 = rms_parts(hidden_in)
    ffn_low = (unit2 * preffn).astype(bf16)
    cot_rows = lax.all_gather(cotangent, "head", axis=0, tiled=True)
    ffn_rows = lax.all_gather(ffn_low, "head", axis=0, tiled=True)
    gate_pre = jnp.dot(ffn_rows, ffn_gate, preferred_element_type=f32)
    upward_pre = jnp.dot(ffn_rows, ffn_upward, preferred_element_type=f32)
    hidden_grad = jnp.dot(cot_rows, ffn_down, preferred_element_type=f32)
    act, act_slope = gelu_pair(gate_pre)
    hidden_low = (act * upward_pre).astype(bf16)
    gate_low = (hidden_grad * upward_pre * act_slope).astype(bf16)
    upward_low = (hidden_grad * act).astype(bf16)
    back = contract_cols(gate_low, ffn_gate) + contract_cols(upward_low, ffn_upward)
    ffn_grad = lax.psum_scatter(
        back.astype(bf16), "head", scatter_dimension=0, tiled=True
    ).astype(f32)
    ffn_out = lax.psum_scatter(
        contract_cols(hidden_low, ffn_down).astype(bf16), "head", scatter_dimension=0, tiled=True
    )
    layer_out = (hidden_in + ffn_out.astype(f32)).astype(bf16)
    terms = jnp.stack(
        [
            contract_rows(gate_low, ffn_rows),
            contract_rows(upward_low, ffn_rows),
            contract_rows(hidden_low, cot_rows),
        ]
    ).astype(bf16)
    terms = jnp.moveaxis(terms.reshape(3, terms.shape[1], group, -1), 2, 0)
    ffn_sums = lax.psum_scatter(terms, "dp", scatter_dimension=0, tiled=False).astype(f32)

    preffn_grad = jnp.sum(ffn_grad * unit2, axis=0)
    resid_grad = cotangent.astype(f32) + norm_back(unit2, rinv2, preffn, ffn_grad)
    resid_low = resid_grad.astype(bf16)

    grad_rows = lax.all_gather(resid_low, "head", axis=0, tiled=True)
    gated_grad = contract_cols(grad_rows, wo)
    output_grad = contract_rows(gated, grad_rows)[:chans]
    dpre, dgate, dpar = rec_bwd(gated_grad, pre, pos, u, r, e, h, wg, par)
    normed_grad = lax.psum_scatter(
        contract_cols(dpre, wbi).astype(bf16), "head", scatter_dimension=0, tiled=True
    ).astype(f32)
    dwbi = contract_rows(normed_rows, dpre)
    premix_grad = jnp.sum(normed_grad * unit1, axis=0)
    stream_grad = (resid_grad + norm_back(unit1, rinv1, premix, normed_grad)).astype(bf16)

    sums = lax.psum(
        tuple(
            v.astype(bf16)
            for v in (
                dwbi[:, :chans],
                dwbi[:, width : width + chans],
                output_grad,
                diagonal_blocks(dgate[:, :width], heads, size),
                diagonal_blocks(dgate[:, width:], heads, size),
                dpar[:, :chans],
            )
        ),
        "dp",
    )
    branch_grad, input_grad, output_grad, rate_grad, entry_grad, dpar = (
        v.astype(f32) for v in sums
    )
    premix_grad, preffn_grad = lax.psum((premix_grad, preffn_grad), ("dp", "head"))
    decay_grad = dpar[G_DECAY] * (-DECAY_SCALE * jax.nn.sigmoid(decay_param.astype(f32)))
    return (
        layer_out,
        stream_grad,
        premix_grad,
        branch_grad,
        input_grad,
        dpar[G_TAP : G_TAP + CONVW],
        dpar[G_BIAS],
        rate_grad,
        dpar[G_RATE].reshape(heads, size),
        entry_grad,
        dpar[G_ENTRY].reshape(heads, size),
        decay_grad,
        output_grad,
        preffn_grad,
        ffn_sums[0].T,
        ffn_sums[1].T,
        ffn_sums[2].T,
    )


def solution(mesh):
    placed = (
        P(("dp", "head"), None),
        P("dp", None),
        P(),
        P(None, "head"),
        P(None, "head"),
        P(None, "head"),
        P("head"),
        P("head", None, None),
        P("head", None),
        P("head", None, None),
        P("head", None),
        P("head"),
        P("head", None),
        P(),
        P(None, "head"),
        P(None, "head"),
        P(None, "head"),
        P(("dp", "head"), None),
    )
    return jax.shard_map(
        shards,
        mesh=mesh,
        in_specs=placed,
        out_specs=(
            P(("dp", "head"), None),
            P(("dp", "head"), None),
            P(),
            P(None, "head"),
            P(None, "head"),
            P(None, "head"),
            P("head"),
            P("head", None, None),
            P("head", None),
            P("head", None, None),
            P("head", None),
            P("head"),
            P("head", None),
            P(),
            P("dp", "head"),
            P("dp", "head"),
            P("dp", "head"),
        ),
        check_vma=False,
    )
```

```python
import functools
import math

import jax
import jax.numpy as jnp
from jax import lax
from jax.experimental import pallas as pl
from jax.experimental.pallas import tpu as pltpu
from jax.sharding import PartitionSpec as P

CONVW = 4
SEQ = 2048
CHUNK = 256
BLOCK = 64
LANES = 128
HALO = 8
PARTS = 2
VMEM_BYTES = 62 * 2**20

EPSILON = 1e-06
DECAY_SCALE = 8.0
GELU_A = math.sqrt(2.0 / math.pi)
GELU_B = 0.044715

BIAS, TAP, RATE_B, ENTRY_B, DECAY = 0, 1, 5, 6, 7
PARAMS = 8
G_BIAS, G_TAP, G_RATE, G_ENTRY, G_DECAY = 0, 1, 5, 6, 7


def rms_parts(values):
    rinv = lax.rsqrt(jnp.mean(values * values, axis=-1, keepdims=True) + EPSILON)
    return rinv, values * rinv


def norm_back(unit, rinv, gain, grad):
    q = gain * grad
    return rinv * (q - unit * jnp.mean(q * unit, axis=-1, keepdims=True))


def contract_cols(leading, trailing):
    return lax.dot_general(
        leading, trailing, (((1,), (1,)), ((), ())), preferred_element_type=jnp.float32
    )


def contract_rows(leading, trailing):
    return lax.dot_general(
        leading, trailing, (((0,), (0,)), ((), ())), preferred_element_type=jnp.float32
    )


def gelu_pair(v):
    sq = v * v
    th = jnp.tanh(GELU_A * v * (1.0 + GELU_B * sq))
    half = 0.5 * (1.0 + th)
    slope = half + 0.5 * v * (1.0 - th * th) * (GELU_A * (1.0 + 3.0 * GELU_B * sq))
    return v * half, slope


def gelu(v):
    return v * (0.5 * (1.0 + jnp.tanh(GELU_A * v * (1.0 + GELU_B * v * v))))


def decay_terms(rate_gate, slope, fresh):
    log_decay = slope * rate_gate
    c = jnp.exp(log_decay)
    y = 2.0 * log_decay
    series = 1.0 + y * (1.0 / 7.0)
    for n in (6, 5, 4, 3, 2):
        series = 1.0 + (y * (1.0 / n)) * series
    sq = c * c
    q = jnp.where(y > -0.5, -y * series, 1.0 - sq)
    rsq = lax.rsqrt(jnp.maximum(q, 1e-37))
    return (
        jnp.where(fresh, 0.0, c),
        jnp.where(fresh, 1.0, q * rsq),
        jnp.where(fresh, 0.0, sq * rsq),
    )


def rec_fwd_kernel(pre, pos, wg, par, u_out, r_out, e_out, h_out, gated, xbuf, z, carry):
    width = u_out.shape[1]
    tiles = width // LANES

    @pl.when(pl.program_id(0) == 0)
    def _():
        xbuf[0:HALO, :] = jnp.zeros((HALO, width), jnp.float32)
        carry[...] = jnp.zeros_like(carry)

    @pl.when(pl.program_id(0) > 0)
    def _():
        xbuf[0:HALO, :] = xbuf[CHUNK : CHUNK + HALO, :]

    xbuf[HALO : HALO + CHUNK, :] = pre[:, width:]

    def conv_step(i, _):
        row = pl.multiple_of(i * BLOCK, BLOCK)
        place = pos[pl.ds(row, BLOCK), :]
        for t in range(tiles):
            cols = pl.ds(t * LANES, LANES)
            xs = xbuf[pl.ds(row, BLOCK + HALO), cols]
            total = par[BIAS : BIAS + 1, cols] + par[TAP : TAP + 1, cols] * xs[HALO:]
            for k in range(1, CONVW):
                term = par[TAP + k : TAP + k + 1, cols] * xs[HALO - k : HALO - k + BLOCK]
                total = total + jnp.where(place >= k, term, 0.0)
            u_out[pl.ds(row, BLOCK), cols] = total
        return 0

    lax.fori_loop(0, CHUNK // BLOCK, conv_step, 0)
    z[...] = jnp.dot(u_out[...].astype(jnp.bfloat16), wg[...], preferred_element_type=jnp.float32)

    def scan_step(i, _):
        row = pl.multiple_of(i * BLOCK, BLOCK)
        rows = pl.ds(row, BLOCK)
        fresh = pos[rows, :] == 0
        inner = lax.broadcasted_iota(jnp.int32, (BLOCK, LANES), 0) % 8
        for t in range(tiles):
            cols = pl.ds(t * LANES, LANES)
            other = pl.ds(width + t * LANES, LANES)
            r = jax.nn.sigmoid(z[rows, cols] + par[RATE_B : RATE_B + 1, cols])
            e = jax.nn.sigmoid(z[rows, other] + par[ENTRY_B : ENTRY_B + 1, cols])
            u = u_out[rows, cols]
            c, m, _ = decay_terms(r, par[DECAY : DECAY + 1, cols], fresh)
            r_out[rows, cols] = r
            e_out[rows, cols] = e
            b = m * e * u
            for d in (1, 2, 4):
                near = inner >= d
                b = b + c * jnp.where(near, pltpu.roll(b, d, 0), 0.0)
                c = c * jnp.where(near, pltpu.roll(c, d, 0), 1.0)
            last = carry[0:1, cols]
            pieces = []
            for g in range(BLOCK // 8):
                part = slice(g * 8, g * 8 + 8)
                state = b[part] + c[part] * last
                last = state[7:8]
                pieces.append(state)
            carry[0:1, cols] = last
            h = jnp.concatenate(pieces, axis=0)
            h_out[rows, cols] = h
            gated[rows, cols] = (h * gelu(pre[rows, cols])).astype(jnp.bfloat16)
        return 0

    lax.fori_loop(0, CHUNK // BLOCK, scan_step, 0)


def rec_fwd(pre, pos, wg, par):
    length, width = pre.shape[0], pre.shape[1] // 2
    rows = lambda cols: pl.BlockSpec((CHUNK, cols), lambda i: (i, 0))
    whole = lambda a: pl.BlockSpec(a.shape, lambda i: (0,) * a.ndim)
    wide = jax.ShapeDtypeStruct((length, width), jnp.float32)
    return pl.pallas_call(
        rec_fwd_kernel,
        grid=(length // CHUNK,),
        out_shape=(wide, wide, wide, wide, jax.ShapeDtypeStruct((length, width), jnp.bfloat16)),
        in_specs=[rows(2 * width), rows(LANES), whole(wg), whole(par)],
        out_specs=[rows(width)] * 5,
        scratch_shapes=[
            pltpu.VMEM((CHUNK + HALO, width), jnp.float32),
            pltpu.VMEM((CHUNK, 2 * width), jnp.float32),
            pltpu.VMEM((8, width), jnp.float32),
        ],
        compiler_params=pltpu.CompilerParams(vmem_limit_bytes=40 * 2**20),
        name="recurrence_forward",
    )(pre, pos, wg, par)


def rec_bwd_kernel(
    gg, pre, pre_halo, pos, u_in, r_in, e_in, h_in, h_halo, wg, par,
    dpre, dgate, dpar, dz, du, pbuf, carry,
):
    width = u_in.shape[1]
    tiles = width // LANES
    step = pl.program_id(0)

    @pl.when(step == 0)
    def _():
        du[CHUNK:, :] = jnp.zeros((HALO, width), jnp.float32)
        pbuf[CHUNK:, :] = jnp.zeros((HALO, LANES), jnp.int32)
        carry[...] = jnp.zeros_like(carry)
        dgate[...] = jnp.zeros_like(dgate)
        dpar[...] = jnp.zeros_like(dpar)

    @pl.when(step > 0)
    def _():
        du[CHUNK:, :] = du[0:HALO, :]
        pbuf[CHUNK:, :] = pbuf[0:HALO, :]

    pbuf[0:CHUNK, :] = pos[...]

    def total(v):
        return jnp.sum(v, axis=0, keepdims=True)

    def scan_step(j, _):
        i = CHUNK // BLOCK - 1 - j
        row = pl.multiple_of(i * BLOCK, BLOCK)
        rows = pl.ds(row, BLOCK)
        fresh = pos[rows, :] == 0
        place = lax.broadcasted_iota(jnp.int32, (BLOCK, LANES), 0)
        inner = place % 8
        before = pl.multiple_of(jnp.maximum(row - 8, 0), 8)
        for t in range(tiles):
            cols = pl.ds(t * LANES, LANES)
            other = pl.ds(width + t * LANES, LANES)
            r, e, u, h = r_in[rows, cols], e_in[rows, cols], u_in[rows, cols], h_in[rows, cols]
            grad = gg[rows, cols]
            act, slope = gelu_pair(pre[rows, cols])
            dpre[rows, cols] = (grad * h * slope).astype(jnp.bfloat16)
            dh = grad * act
            decay = par[DECAY : DECAY + 1, cols]
            c, m, ratio = decay_terms(r, decay, fresh)
            b, a = c * dh, c
            for d in (1, 2, 4):
                near = inner < 8 - d
                b = b + a * jnp.where(near, pltpu.roll(b, BLOCK - d, 0), 0.0)
                a = a * jnp.where(near, pltpu.roll(a, BLOCK - d, 0), 1.0)
            later = carry[0:1, cols]
            pieces = []
            first = later
            for g in reversed(range(BLOCK // 8)):
                part = slice(g * 8, g * 8 + 8)
                state = b[part] + a[part] * first
                first = state[0:1]
                pieces.append(state)
            carry[0:1, cols] = first
            mu = jnp.concatenate(pieces[::-1], axis=0)
            adj = dh + jnp.where(place == BLOCK - 1, later, pltpu.roll(mu, BLOCK - 1, 0))
            edge = jnp.where(i == 0, h_halo[7:8, cols], h_in[pl.ds(before, 8), cols][7:8])
            prior = jnp.where(place == 0, edge, pltpu.roll(h, 1, 0))
            eu = e * u
            dlog = adj * (prior * c - eu * ratio)
            dpar[G_DECAY : G_DECAY + 1, cols] += total(dlog * r)
            dzr = decay * dlog * (r * (1.0 - r))
            dze = adj * m * eu * (1.0 - e)
            dpar[G_RATE : G_RATE + 1, cols] += total(dzr)
            dpar[G_ENTRY : G_ENTRY + 1, cols] += total(dze)
            dz[rows, cols] = dzr.astype(jnp.bfloat16)
            dz[rows, other] = dze.astype(jnp.bfloat16)
            du[rows, cols] = adj * m * e
        return 0

    lax.fori_loop(0, CHUNK // BLOCK, scan_step, 0)
    du[0:CHUNK, :] += contract_cols(dz[...], wg[...])
    dgate[...] += contract_rows(u_in[...].astype(jnp.bfloat16), dz[...])

    def conv_step(i, _):
        row = pl.multiple_of(i * BLOCK, BLOCK)
        rows = pl.ds(row, BLOCK)
        before = pl.multiple_of(jnp.maximum(row - 8, 0), 8)
        place = pbuf[pl.ds(row, BLOCK + HALO), :]
        for t in range(tiles):
            cols = pl.ds(t * LANES, LANES)
            other = pl.ds(width + t * LANES, LANES)
            ds = du[pl.ds(row, BLOCK + HALO), cols]
            near = ds[0:BLOCK]
            x = pre[rows, other]
            head = jnp.where(i == 0, pre_halo[:, other], pre[pl.ds(before, 8), other])
            xs = jnp.concatenate([head, x], axis=0)
            dx = par[TAP : TAP + 1, cols] * near
            dpar[G_BIAS : G_BIAS + 1, cols] += total(near)
            dpar[G_TAP : G_TAP + 1, cols] += total(near * x)
            for k in range(1, CONVW):
                inside = jnp.where(place >= k, ds, 0.0)
                dx = dx + par[TAP + k : TAP + k + 1, cols] * inside[k : k + BLOCK]
                dpar[G_TAP + k : G_TAP + k + 1, cols] += total(
                    inside[0:BLOCK] * xs[HALO - k : HALO - k + BLOCK]
                )
            dpre[rows, other] = dx.astype(jnp.bfloat16)
        return 0

    lax.fori_loop(0, CHUNK // BLOCK, conv_step, 0)


def rec_bwd(gg, pre, pos, u, r, e, h, wg, par):
    length, width = u.shape
    count = length // CHUNK
    rows = lambda cols: pl.BlockSpec((CHUNK, cols), lambda i: (count - 1 - i, 0))
    halo = lambda cols: pl.BlockSpec(
        (HALO, cols), lambda i: (jnp.maximum((count - 1 - i) * (CHUNK // HALO) - 1, 0), 0)
    )
    whole = lambda shape: pl.BlockSpec(shape, lambda i: (0,) * len(shape))
    return pl.pallas_call(
        rec_bwd_kernel,
        grid=(count,),
        out_shape=(
            jax.ShapeDtypeStruct((length, 2 * width), jnp.bfloat16),
            jax.ShapeDtypeStruct((width, 2 * width), jnp.float32),
            jax.ShapeDtypeStruct((PARAMS, width), jnp.float32),
        ),
        in_specs=[
            rows(width), rows(2 * width), halo(2 * width), rows(LANES),
            rows(width), rows(width), rows(width), rows(width), halo(width),
            whole(wg.shape), whole(par.shape),
        ],
        out_specs=[rows(2 * width), whole((width, 2 * width)), whole((PARAMS, width))],
        scratch_shapes=[
            pltpu.VMEM((CHUNK, 2 * width), jnp.bfloat16),
            pltpu.VMEM((CHUNK + HALO, width), jnp.float32),
            pltpu.VMEM((CHUNK + HALO, LANES), jnp.int32),
            pltpu.VMEM((8, width), jnp.float32),
        ],
        compiler_params=pltpu.CompilerParams(vmem_limit_bytes=40 * 2**20),
        name="recurrence_backward",
    )(gg, pre, pre, pos, u, r, e, h, h, wg, par)

def each(count, body):
    def step(i, _):
        body(i)
        return 0

    lax.fori_loop(0, count, step, 0)


def line_place():
    return lax.axis_index("head"), lax.axis_size("head")


def line_barrier(j, n):
    barrier = pltpu.get_barrier_semaphore()
    for side in (-1, 1):

        @pl.when((j + side >= 0) & (j + side < n))
        def _():
            pl.semaphore_signal(
                barrier, inc=1, device_id={"head": j + side}, device_id_type=pl.DeviceIdType.MESH
            )

    inside = (j > 0) & (j < n - 1)

    @pl.when(inside)
    def _():
        pl.semaphore_wait(barrier, 2)

    @pl.when(jnp.logical_not(inside))
    def _():
        pl.semaphore_wait(barrier, 1)


class Gather:
    def __init__(self, j, n, buf, send, recv):
        self.j, self.n, self.buf, self.send, self.recv = j, n, buf, send, recv
        self.span = buf.shape[1] // PARTS

    def copy(self, block, s, side, source=None):
        part = pl.ds(s * self.span, self.span)
        target = self.buf.at[block, part]
        return pltpu.make_async_remote_copy(
            src_ref=target if source is None else source.at[part],
            dst_ref=target,
            send_sem=self.send.at[(side + 1) // 2, block, s],
            recv_sem=self.recv.at[block, s],
            device_id={"head": self.j + side},
            device_id_type=pl.DeviceIdType.MESH,
        )

    def there(self, side):
        return (self.j + side >= 0) & (self.j + side < self.n)

    def flows(self, t):
        for side in (1, -1):
            block = self.j - side * t
            yield side, block, (block >= 0) & (block < self.n)

    def start(self, source):
        for s in range(PARTS):
            for side in (1, -1):

                @pl.when(self.there(side))
                def _():
                    self.copy(self.j, s, side, source).start()

    def step(self, t):
        for s in range(PARTS):
            for side, block, live in self.flows(t):

                @pl.when(live)
                def _():
                    self.copy(block, s, -side).wait_recv()

                @pl.when(live & self.there(side))
                def _():
                    self.copy(block, s, side).start()

    def finish(self):
        def drain(t):
            for s in range(PARTS):
                for side, block, live in self.flows(t):

                    @pl.when(live & self.there(side))
                    def _():
                        self.copy(block, s, side).wait_send()

        each(self.n, drain)


class Scatter:
    def __init__(self, j, n, own, held, send, recv):
        self.j, self.n, self.own, self.held, self.send, self.recv = j, n, own, held, send, recv
        self.span = own.shape[1] // PARTS

    def rows(self, s):
        return pl.ds(s * self.span, self.span)

    def slot(self, block, side, at):
        return block if side == 1 else jnp.where(block == at, self.n, block)

    def arrival(self, slot, s):
        return pltpu.make_async_copy(
            self.held.at[slot, self.rows(s)], self.held.at[slot, self.rows(s)], self.recv.at[slot, s]
        )

    def flows(self, t):
        for side in (1, -1):
            lag = self.j if side == 1 else self.n - 1 - self.j
            block = self.n - 1 - (t - lag) if side == 1 else t - lag
            yield side, block, (t >= lag) & (t <= self.n - 2)

    def copy(self, source, block, s, side):
        slot = self.slot(block, side, self.j + side)
        return pltpu.make_async_remote_copy(
            src_ref=source.at[block, self.rows(s)],
            dst_ref=self.held.at[slot, self.rows(s)],
            send_sem=self.send.at[block, s],
            recv_sem=self.recv.at[slot, s],
            device_id={"head": self.j + side},
            device_id_type=pl.DeviceIdType.MESH,
        )

    def step(self, t):
        for s in range(PARTS):
            for side, block, live in self.flows(t):
                behind = (self.j - side >= 0) & (self.j - side < self.n)

                @pl.when(live & jnp.logical_not(behind))
                def _():
                    self.copy(self.own, block, s, side).start()

                @pl.when(live & behind)
                def _():
                    self.arrival(block, s).wait()
                    self.add(block, s)
                    self.copy(self.held, block, s, side).start()

    def add(self, block, s):
        def add_rows(i):
            rows = pl.ds(pl.multiple_of(s * self.span + i * 16, 16), 16)
            total = self.own[block, rows, :].astype(jnp.float32) + self.held[
                block, rows, :
            ].astype(jnp.float32)
            self.held[block, rows, :] = total.astype(jnp.bfloat16)

        each(self.span // 16, add_rows)

    def arrive(self):
        for s in range(PARTS):

            @pl.when(self.j > 0)
            def _():
                self.arrival(self.j, s).wait()

            @pl.when(self.j < self.n - 1)
            def _():
                self.arrival(self.n, s).wait()

    def result(self, rows):
        total = self.own[self.j, rows, :].astype(jnp.float32)
        left = self.held[self.j, rows, :].astype(jnp.float32)
        right = self.held[self.n, rows, :].astype(jnp.float32)
        total = total + jnp.where(self.j > 0, left, 0.0)
        return total + jnp.where(self.j < self.n - 1, right, 0.0)

    def finish(self):
        def drain(t):
            for s in range(PARTS):
                for side, block, live in self.flows(t):

                    @pl.when(live)
                    def _():
                        self.copy(self.own, block, s, side).wait_send()

        each(self.n - 1, drain)


def gather_sems(n):
    return [pltpu.SemaphoreType.DMA((2, n, PARTS)), pltpu.SemaphoreType.DMA((n, PARTS))]


def scatter_sems(n):
    return [pltpu.SemaphoreType.DMA((n, PARTS)), pltpu.SemaphoreType.DMA((n + 1, PARTS))]


def line_call(kernel, ident, name, out_shape, in_specs, out_specs, scratch, cost=None):
    return pl.pallas_call(
        kernel,
        out_shape=out_shape,
        in_specs=in_specs,
        out_specs=out_specs,
        scratch_shapes=scratch,
        compiler_params=pltpu.CompilerParams(
            collective_id=ident, has_side_effects=True, vmem_limit_bytes=VMEM_BYTES
        ),
        name=name,
    )


IN_VMEM = pl.BlockSpec(memory_space=pltpu.VMEM)
IN_ANY = pl.BlockSpec(memory_space=pl.ANY)
STRIP = 16


def strips(rows, body):
    each(rows // STRIP, lambda i: body(pl.ds(pl.multiple_of(i * STRIP, STRIP), STRIP)))


def project_kernel(
    stream, gain, wbi, rows_out, pre, normed, rows, send, recv, keep_sem
):
    j, n = line_place()
    line_barrier(j, n)
    local = stream.shape[0]

    def norm(part):
        _, unit = rms_parts(stream[part, :].astype(jnp.float32))
        normed[part, :] = (unit * gain[...]).astype(jnp.bfloat16)

    strips(local, norm)
    gather = Gather(j, n, rows, send, recv)
    gather.start(normed)

    def project(block, source):
        part = pl.ds(pl.multiple_of(block * local, local), local)
        pre[part, :] = jnp.dot(source, wbi[...], preferred_element_type=jnp.float32)

    def keep(source, block):
        return pltpu.make_async_copy(source, rows_out.at[block], keep_sem.at[block])

    keep(normed, j).start()
    project(j, normed[...])

    def visit(v):
        t = v // 2 + 1
        block = jnp.where(v % 2 == 0, j - t, j + t)

        @pl.when(v % 2 == 0)
        def _():
            gather.step(t)

        @pl.when((block >= 0) & (block < n))
        def _():
            keep(rows.at[block], block).start()
            project(block, rows[block])

    each(2 * (n - 1), visit)
    gather.finish()
    keep(normed, j).wait()
    for k in range(1, n):
        other = lax.rem(j + k, n)
        keep(rows.at[other], other).wait()


def project(stream, gain, wbi):
    n = lax.axis_size("head")
    local, depth = stream.shape
    return line_call(
        project_kernel, 0, "gather_project",
        (
            jax.ShapeDtypeStruct((n, local, depth), jnp.bfloat16),
            jax.ShapeDtypeStruct((n * local, wbi.shape[1]), jnp.float32),
        ),
        [IN_VMEM] * 3,
        [IN_ANY, IN_VMEM],
        [
            pltpu.VMEM((local, depth), jnp.bfloat16),
            pltpu.VMEM((n, local, depth), jnp.bfloat16),
            *gather_sems(n),
            pltpu.SemaphoreType.DMA((n,)),
        ],
    )(stream, gain, wbi)


def mixer_out_kernel(
    gated, wo, stream, gain, cot, cot_rows, hidden, low_out, own, held,
    send, recv, gsend, grecv, sem,
):
    j, n = line_place()
    line_barrier(j, n)
    local = stream.shape[0]
    gather = Gather(j, n, cot_rows, gsend, grecv)
    scatter = Scatter(j, n, own, held, send, recv)

    def compute(block):
        part = pl.ds(pl.multiple_of(block * local, local), local)
        own[block] = jnp.dot(
            gated[part, :], wo[...], preferred_element_type=jnp.float32
        ).astype(jnp.bfloat16)

    def ahead(t):
        for _, block, live in scatter.flows(t):
            pl.when(live)(lambda: compute(block))

    ahead(0)
    mine = pltpu.make_async_copy(cot, cot_rows.at[j], sem)
    mine.start()

    def step(t):
        scatter.step(t)

        @pl.when(t == 0)
        def _():
            gather.start(cot)

        ahead(t + 1)

        @pl.when(t == 0)
        def _():
            compute(j)

        @pl.when(t > 0)
        def _():
            gather.step(t)

    each(n - 1, step)
    scatter.arrive()

    def settle(part):
        total = stream[part, :].astype(jnp.float32) + scatter.result(part)
        hidden[part, :] = total
        _, unit = rms_parts(total)
        low_out[part, :] = (unit * gain[...]).astype(jnp.bfloat16)

    strips(local, settle)
    gather.step(n - 1)
    scatter.finish()
    gather.finish()
    mine.wait()


def mixer_out(gated, wo, stream, gain, cot):
    n = lax.axis_size("head")
    local, depth = stream.shape
    return line_call(
        mixer_out_kernel, 1, "mixer_out",
        (
            jax.ShapeDtypeStruct((n, local, depth), jnp.bfloat16),
            jax.ShapeDtypeStruct((local, depth), jnp.float32),
            jax.ShapeDtypeStruct((local, depth), jnp.bfloat16),
        ),
        [IN_VMEM] * 4 + [IN_ANY],
        [IN_ANY, IN_VMEM, IN_VMEM],
        [
            pltpu.VMEM((n, local, depth), jnp.bfloat16),
            pltpu.VMEM((n + 1, local, depth), jnp.bfloat16),
            *scatter_sems(n),
            *gather_sems(n),
            pltpu.SemaphoreType.DMA,
        ],
    )(gated, wo, stream, gain, cot)


def ffn_kernel(
    low, cot_rows, cot, hidden, gain, wg, wu, wd,
    out_part, terms, resid, resid_low, gain_grad,
    rows, cot_unit, kept, own, held, stage, wstage, cot_cols,
    gsend, grecv, send, recv, cot_sem, out_sem, col_sem, term_sem,
):
    j, n = line_place()
    line_barrier(j, n)
    f32, bf16 = jnp.float32, jnp.bfloat16
    local, depth = low.shape
    units = wg.shape[1]
    fstep = 256 if units % 256 == 0 else LANES
    dstep = 512
    gather = Gather(j, n, rows, gsend, grecv)
    scatter = Scatter(j, n, own, held, send, recv)
    gather.start(low)
    rows[j] = low[...]

    def fetch(block):
        return pltpu.make_async_copy(cot_rows.at[block], cot_unit, cot_sem)

    def put(block):
        return pltpu.make_async_copy(stage, out_part.at[block], out_sem)

    def unit(block):
        span = pl.ds(pl.multiple_of(block * local, local), local)
        x = rows.at[block]
        for f in range(0, units, fstep):
            cols = slice(f, f + fstep)
            gate = jnp.dot(x[...], wg[:, cols], preferred_element_type=f32)
            act, slope = gelu_pair(gate)
            up = jnp.dot(x[...], wu[:, cols], preferred_element_type=f32)
            kept[2, span, cols] = (act * up).astype(bf16)
            grad = jnp.dot(cot_unit[...], wd[:, cols], preferred_element_type=f32)
            kept[0, span, cols] = (grad * up * slope).astype(bf16)
            kept[1, span, cols] = (grad * act).astype(bf16)
        for d in range(0, depth, dstep):
            cols = slice(d, d + dstep)
            own[block, :, cols] = (
                contract_cols(kept[0, span, :], wg[cols, :])
                + contract_cols(kept[1, span, :], wu[cols, :])
            ).astype(bf16)
            stage[:, cols] = contract_cols(kept[2, span, :], wd[cols, :]).astype(bf16)

    def visit(v):
        t = (v + 1) // 2
        block = jnp.where(v % 2 == 1, j - t, j + t)
        live = (block >= 0) & (block < n)

        @pl.when(live)
        def _():
            fetch(block).start()

        @pl.when(v % 2 == 1)
        def _():
            gather.step(t)

        @pl.when(live)
        def _():
            fetch(block).wait()

            @pl.when(v > 0)
            def _():
                put(block).wait()

            unit(block)
            put(block).start()

    each(2 * n - 1, visit)
    put(j).wait()

    width = depth // n
    per = depth // terms.shape[0] // width

    def take(b):
        cols = pl.ds(pl.multiple_of(b * width, width), width)
        return pltpu.make_async_copy(cot_rows.at[:, :, cols], cot_cols, col_sem)

    def give(b):
        spot = pl.ds(pl.multiple_of(lax.rem(b, per) * width, width), width)
        return pltpu.make_async_copy(wstage, terms.at[b // per, :, spot, :], term_sem)

    def weights(b):
        cols = pl.ds(pl.multiple_of(b * width, width), width)
        xs = rows[:, :, cols].reshape(n * local, width)
        take(b).wait()

        @pl.when(b > 0)
        def _():
            give(b).wait()

        wstage[0] = contract_rows(xs, kept[0]).astype(bf16)
        wstage[1] = contract_rows(xs, kept[1]).astype(bf16)
        wstage[2] = contract_rows(
            cot_cols[...].reshape(n * local, width), kept[2]
        ).astype(bf16)
        give(b).start()

        @pl.when(b + 1 < n)
        def _():
            take(b + 1).start()

    take(0).start()

    def step(t):
        pl.when(t < n - 1)(lambda: scatter.step(t))
        weights(t)

    each(n, step)
    scatter.arrive()
    gain_grad[...] = jnp.zeros_like(gain_grad)

    def settle(part):
        rinv, u = rms_parts(hidden[part, :])
        grad = scatter.result(part)
        gain_grad[...] += jnp.sum(grad * u, axis=0, keepdims=True)
        total = cot[part, :].astype(f32) + norm_back(u, rinv, gain[...], grad)
        resid[part, :] = total
        resid_low[part, :] = total.astype(bf16)

    strips(local, settle)
    give(0).wait()
    gather.finish()
    scatter.finish()


def feed_forward(low, cot_rows, cot, hidden, gain, wg, wu, wd):
    n, group = lax.axis_size("head"), lax.axis_size("dp")
    local, depth = low.shape
    units = wg.shape[1]
    bf16 = jnp.bfloat16
    return line_call(
        ffn_kernel, 2, "feed_forward",
        (
            jax.ShapeDtypeStruct((n, local, depth), bf16),
            jax.ShapeDtypeStruct((group, 3, depth // group, units), bf16),
            jax.ShapeDtypeStruct((local, depth), jnp.float32),
            jax.ShapeDtypeStruct((local, depth), bf16),
            jax.ShapeDtypeStruct((1, depth), jnp.float32),
        ),
        [IN_VMEM, IN_ANY] + [IN_VMEM] * 6,
        [IN_ANY, IN_ANY, IN_VMEM, IN_VMEM, IN_VMEM],
        [
            pltpu.VMEM((n, local, depth), bf16),
            pltpu.VMEM((local, depth), bf16),
            pltpu.VMEM((3, n * local, units), bf16),
            pltpu.VMEM((n, local, depth), bf16),
            pltpu.VMEM((n + 1, local, depth), bf16),
            pltpu.VMEM((local, depth), bf16),
            pltpu.VMEM((3, depth // n, units), bf16),
            pltpu.VMEM((n, local, depth // n), bf16),
            *gather_sems(n),
            *scatter_sems(n),
            *[pltpu.SemaphoreType.DMA] * 4,
        ],
    )(low, cot_rows, cot, hidden, gain, wg, wu, wd)


def resid_kernel(
    low, out_part, hidden, grad_rows, layer_out, held, send, recv, gsend, grecv, sem
):
    j, n = line_place()
    line_barrier(j, n)
    gather = Gather(j, n, grad_rows, gsend, grecv)
    scatter = Scatter(j, n, out_part, held, send, recv)
    gather.start(low)
    mine = pltpu.make_async_copy(low, grad_rows.at[j], sem)
    mine.start()

    def step(t):
        pl.when(t > 0)(lambda: gather.step(t))
        pl.when(t < n - 1)(lambda: scatter.step(t))

    each(n, step)
    scatter.arrive()

    def settle(part):
        layer_out[part, :] = (hidden[part, :] + scatter.result(part)).astype(jnp.bfloat16)

    strips(low.shape[0], settle)
    gather.finish()
    scatter.finish()
    mine.wait()


def gather_resid(low, out_part, hidden):
    n = lax.axis_size("head")
    local, depth = low.shape
    bf16 = jnp.bfloat16
    return line_call(
        resid_kernel, 3, "gather_resid",
        (jax.ShapeDtypeStruct((n, local, depth), bf16), jax.ShapeDtypeStruct((local, depth), bf16)),
        [IN_VMEM] * 3,
        [IN_ANY, IN_VMEM],
        [
            pltpu.VMEM((n + 1, local, depth), bf16),
            *scatter_sems(n),
            *gather_sems(n),
            pltpu.SemaphoreType.DMA,
        ],
    )(low, out_part, hidden)


def stream_kernel(dpre, wbi, stream, gain, resid, stream_grad, gain_grad, own, held, send, recv):
    j, n = line_place()
    line_barrier(j, n)
    local = stream.shape[0]
    scatter = Scatter(j, n, own, held, send, recv)

    def compute(block):
        part = pl.ds(pl.multiple_of(block * local, local), local)
        own[block] = contract_cols(dpre[part, :], wbi[...]).astype(jnp.bfloat16)

    def ahead(t):
        for _, block, live in scatter.flows(t):
            pl.when(live)(lambda: compute(block))

    ahead(0)

    def step(t):
        scatter.step(t)
        ahead(t + 1)
        pl.when(t == 0)(lambda: compute(j))

    each(n - 1, step)
    scatter.arrive()
    gain_grad[...] = jnp.zeros_like(gain_grad)

    def settle(part):
        rinv, u = rms_parts(stream[part, :].astype(jnp.float32))
        grad = scatter.result(part)
        gain_grad[...] += jnp.sum(grad * u, axis=0, keepdims=True)
        total = resid[part, :] + norm_back(u, rinv, gain[...], grad)
        stream_grad[part, :] = total.astype(jnp.bfloat16)

    strips(local, settle)
    scatter.finish()


def stream_back(dpre, wbi, stream, gain, resid):
    n = lax.axis_size("head")
    local, depth = stream.shape
    return line_call(
        stream_kernel, 4, "stream_back",
        (
            jax.ShapeDtypeStruct((local, depth), jnp.bfloat16),
            jax.ShapeDtypeStruct((1, depth), jnp.float32),
        ),
        [IN_VMEM] * 5,
        [IN_VMEM, IN_VMEM],
        [
            pltpu.VMEM((n, local, depth), jnp.bfloat16),
            pltpu.VMEM((n + 1, local, depth), jnp.bfloat16),
            *scatter_sems(n),
        ],
    )(dpre, wbi, stream, gain, resid)


def places(lengths):
    starts = jnp.cumsum(lengths, axis=1) - lengths
    spots = jnp.arange(SEQ, dtype=jnp.int32)
    earlier = jnp.where(starts[:, :, None] <= spots[None, None, :], starts[:, :, None], 0)
    return (spots[None, :] - jnp.max(earlier, axis=1))[0]


def widen(values, width):
    return jnp.pad(values, ((0, 0), (0, width - values.shape[1])))


def block_diagonal(weights, width):
    heads, size = weights.shape[0], weights.shape[1]
    placed = [
        jnp.pad(weights[i], ((i * size, width - (i + 1) * size),) * 2) for i in range(heads)
    ]
    return functools.reduce(jnp.add, placed)


def diagonal_blocks(dense, heads, size):
    return jnp.stack(
        [dense[i * size : (i + 1) * size, i * size : (i + 1) * size] for i in range(heads)]
    )


def shards(
    stream, doc_lengths, premix_gain, branch_weight, input_weight, conv_kernel, conv_bias,
    rate_weight, rate_bias, entry_weight, entry_bias, decay_param, output_weight, preffn_gain,
    ffn_gate, ffn_upward, ffn_down, cotangent,
):
    f32, bf16 = jnp.float32, jnp.bfloat16
    heads, size = rate_bias.shape
    chans = branch_weight.shape[1]
    width = -(-chans // LANES) * LANES

    pos = jnp.broadcast_to(places(doc_lengths)[:, None], (SEQ, LANES))
    slope = -DECAY_SCALE * jax.nn.softplus(decay_param.astype(f32))
    par = jnp.concatenate(
        [
            conv_bias[None].astype(f32),
            conv_kernel.astype(f32),
            rate_bias.reshape(1, -1).astype(f32),
            entry_bias.reshape(1, -1).astype(f32),
            slope[None],
        ]
    )
    par = jnp.pad(par, ((0, 0), (0, width - chans)), constant_values=-1.0)
    par = jnp.where((jnp.arange(width)[None] < chans) | (jnp.arange(PARAMS)[:, None] == DECAY), par, 0.0)
    wg = jnp.concatenate(
        [block_diagonal(rate_weight, width), block_diagonal(entry_weight, width)], axis=1
    )
    wbi = jnp.concatenate([widen(branch_weight, width), widen(input_weight, width)], axis=1)
    wo = jnp.pad(output_weight, ((0, width - chans), (0, 0)))

    premix = premix_gain.astype(f32)[None]
    preffn = preffn_gain.astype(f32)[None]
    normed_rows, pre = project(stream, premix, wbi)
    u, r, e, h, gated = rec_fwd(pre, pos, wg, par)
    cot_rows, hidden_in, ffn_low = mixer_out(gated, wo, stream, preffn, cotangent)

    out_part, terms, resid_grad, resid_low, preffn_grad = feed_forward(
        ffn_low, cot_rows, cotangent, hidden_in, preffn, ffn_gate, ffn_upward, ffn_down
    )
    ffn_sums = lax.psum_scatter(terms, "dp", scatter_dimension=0, tiled=False).astype(f32)

    grad_rows, layer_out = gather_resid(resid_low, out_part, hidden_in)
    grad_rows = grad_rows.reshape(SEQ, -1)
    gated_grad = contract_cols(grad_rows, wo)
    output_grad = contract_rows(gated, grad_rows)[:chans]
    dpre, dgate, dpar = rec_bwd(gated_grad, pre, pos, u, r, e, h, wg, par)
    dwbi = contract_rows(normed_rows.reshape(SEQ, -1), dpre)
    stream_grad, premix_grad = stream_back(dpre, wbi, stream, premix, resid_grad)

    sums = lax.psum(
        tuple(
            v.astype(bf16)
            for v in (
                dwbi[:, :chans],
                dwbi[:, width : width + chans],
                output_grad,
                diagonal_blocks(dgate[:, :width], heads, size),
                diagonal_blocks(dgate[:, width:], heads, size),
                dpar[:, :chans],
            )
        ),
        "dp",
    )
    branch_grad, input_grad, output_grad, rate_grad, entry_grad, dpar = (
        v.astype(f32) for v in sums
    )
    premix_grad, preffn_grad = lax.psum((premix_grad[0], preffn_grad[0]), ("dp", "head"))
    decay_grad = dpar[G_DECAY] * (-DECAY_SCALE * jax.nn.sigmoid(decay_param.astype(f32)))
    return (
        layer_out,
        stream_grad,
        premix_grad,
        branch_grad,
        input_grad,
        dpar[G_TAP : G_TAP + CONVW],
        dpar[G_BIAS],
        rate_grad,
        dpar[G_RATE].reshape(heads, size),
        entry_grad,
        dpar[G_ENTRY].reshape(heads, size),
        decay_grad,
        output_grad,
        preffn_grad,
        ffn_sums[0],
        ffn_sums[1],
        ffn_sums[2],
    )


def solution(mesh):
    placed = (
        P(("dp", "head"), None),
        P("dp", None),
        P(),
        P(None, "head"),
        P(None, "head"),
        P(None, "head"),
        P("head"),
        P("head", None, None),
        P("head", None),
        P("head", None, None),
        P("head", None),
        P("head"),
        P("head", None),
        P(),
        P(None, "head"),
        P(None, "head"),
        P(None, "head"),
        P(("dp", "head"), None),
    )
    return jax.shard_map(
        shards,
        mesh=mesh,
        in_specs=placed,
        out_specs=(
            P(("dp", "head"), None),
            P(("dp", "head"), None),
            P(),
            P(None, "head"),
            P(None, "head"),
            P(None, "head"),
            P("head"),
            P("head", None, None),
            P("head", None),
            P("head", None, None),
            P("head", None),
            P("head"),
            P("head", None),
            P(),
            P("dp", "head"),
            P("dp", "head"),
            P("dp", "head"),
        ),
        check_vma=False,
    )
```

```python
import functools
import math

import jax
import jax.numpy as jnp
from jax import lax
from jax.experimental import pallas as pl
from jax.experimental.pallas import tpu as pltpu
from jax.sharding import PartitionSpec as P

CONVW = 4
SEQ = 2048
CHUNK = 256
BLOCK = 64
LANES = 128
HALO = 8
PARTS = 2
LAG = 1
VMEM_BYTES = 62 * 2**20
IN_VMEM = pl.BlockSpec(memory_space=pltpu.VMEM)
IN_SMEM = pl.BlockSpec(memory_space=pltpu.SMEM)
IN_ANY = pl.BlockSpec(memory_space=pl.ANY)

EPSILON = 1e-06
DECAY_SCALE = 8.0
GELU_A = math.sqrt(2.0 / math.pi)
GELU_B = 0.044715

BIAS, TAP, RATE_B, ENTRY_B, DECAY = 0, 1, 5, 6, 7
PARAMS = 8
SAVED = 4
G_BIAS, G_TAP, G_RATE, G_ENTRY, G_DECAY = 0, 1, 5, 6, 7


def rms_parts(values):
    rinv = lax.rsqrt(jnp.mean(values * values, axis=-1, keepdims=True) + EPSILON)
    return rinv, values * rinv


def norm_back(unit, rinv, gain, grad):
    q = gain * grad
    return rinv * (q - unit * jnp.mean(q * unit, axis=-1, keepdims=True))


def contract_cols(leading, trailing):
    return lax.dot_general(
        leading, trailing, (((1,), (1,)), ((), ())), preferred_element_type=jnp.float32
    )


def contract_rows(leading, trailing):
    return lax.dot_general(
        leading, trailing, (((0,), (0,)), ((), ())), preferred_element_type=jnp.float32
    )


def gelu_pair(v):
    sq = v * v
    th = jnp.tanh(GELU_A * v * (1.0 + GELU_B * sq))
    half = 0.5 * (1.0 + th)
    slope = half + 0.5 * v * (1.0 - th * th) * (GELU_A * (1.0 + 3.0 * GELU_B * sq))
    return v * half, slope


def gelu(v):
    return v * (0.5 * (1.0 + jnp.tanh(GELU_A * v * (1.0 + GELU_B * v * v))))


def decay_terms(rate_gate, slope, fresh):
    log_decay = slope * rate_gate
    c = jnp.exp(log_decay)
    y = 2.0 * log_decay
    series = 1.0 + y * (1.0 / 7.0)
    for n in (6, 5, 4, 3, 2):
        series = 1.0 + (y * (1.0 / n)) * series
    sq = c * c
    q = jnp.where(y > -0.5, -y * series, 1.0 - sq)
    rsq = lax.rsqrt(jnp.maximum(q, 1e-37))
    return (
        jnp.where(fresh, 0.0, c),
        jnp.where(fresh, 1.0, q * rsq),
        jnp.where(fresh, 0.0, sq * rsq),
    )


def doc_places(lengths, first, rows):
    spots = first + lax.broadcasted_iota(jnp.int32, (rows, LANES), 0)
    begin = jnp.zeros((rows, LANES), jnp.int32)
    start = jnp.int32(0)
    for k in range(lengths.shape[1] - 1):
        start = start + lengths[0, k]
        begin = jnp.where(spots >= start, start, begin)
    return spots - begin


def rec_fwd_kernel(lengths, pre, wg, par, saved, gated, xbuf, z, carry):
    width = gated.shape[1]
    u_out, r_out, e_out, h_out = (
        saved.at[:, i * width : (i + 1) * width] for i in range(SAVED)
    )
    tiles = width // LANES

    @pl.when(pl.program_id(0) == 0)
    def _():
        xbuf[0:HALO, :] = jnp.zeros((HALO, width), jnp.float32)
        carry[...] = jnp.zeros_like(carry)

    @pl.when(pl.program_id(0) > 0)
    def _():
        xbuf[0:HALO, :] = xbuf[CHUNK : CHUNK + HALO, :]

    xbuf[HALO : HALO + CHUNK, :] = pre[:, width:]

    first = pl.program_id(0) * CHUNK

    def conv_step(i, _):
        row = pl.multiple_of(i * BLOCK, BLOCK)
        place = doc_places(lengths, first + row, BLOCK)
        for t in range(tiles):
            cols = pl.ds(t * LANES, LANES)
            xs = xbuf[pl.ds(row, BLOCK + HALO), cols]
            total = par[BIAS : BIAS + 1, cols] + par[TAP : TAP + 1, cols] * xs[HALO:]
            for k in range(1, CONVW):
                term = par[TAP + k : TAP + k + 1, cols] * xs[HALO - k : HALO - k + BLOCK]
                total = total + jnp.where(place >= k, term, 0.0)
            u_out[pl.ds(row, BLOCK), cols] = total
        return 0

    lax.fori_loop(0, CHUNK // BLOCK, conv_step, 0)
    z[...] = jnp.dot(u_out[...].astype(jnp.bfloat16), wg[...], preferred_element_type=jnp.float32)

    def scan_step(i, _):
        row = pl.multiple_of(i * BLOCK, BLOCK)
        rows = pl.ds(row, BLOCK)
        fresh = doc_places(lengths, first + row, BLOCK) == 0
        inner = lax.broadcasted_iota(jnp.int32, (BLOCK, LANES), 0) % 8
        for t in range(tiles):
            cols = pl.ds(t * LANES, LANES)
            other = pl.ds(width + t * LANES, LANES)
            r = jax.nn.sigmoid(z[rows, cols] + par[RATE_B : RATE_B + 1, cols])
            e = jax.nn.sigmoid(z[rows, other] + par[ENTRY_B : ENTRY_B + 1, cols])
            u = u_out[rows, cols]
            c, m, _ = decay_terms(r, par[DECAY : DECAY + 1, cols], fresh)
            r_out[rows, cols] = r
            e_out[rows, cols] = e
            b = m * e * u
            for d in (1, 2, 4):
                near = inner >= d
                b = b + c * jnp.where(near, pltpu.roll(b, d, 0), 0.0)
                c = c * jnp.where(near, pltpu.roll(c, d, 0), 1.0)
            last = carry[0:1, cols]
            pieces = []
            for g in range(BLOCK // 8):
                part = slice(g * 8, g * 8 + 8)
                state = b[part] + c[part] * last
                last = state[7:8]
                pieces.append(state)
            carry[0:1, cols] = last
            h = jnp.concatenate(pieces, axis=0)
            h_out[rows, cols] = h
            gated[rows, cols] = (h * gelu(pre[rows, cols])).astype(jnp.bfloat16)
        return 0

    lax.fori_loop(0, CHUNK // BLOCK, scan_step, 0)


def rec_fwd(lengths, pre, wg, par):
    length, width = pre.shape[0], pre.shape[1] // 2
    rows = lambda cols: pl.BlockSpec((CHUNK, cols), lambda i: (i, 0))
    whole = lambda a: pl.BlockSpec(a.shape, lambda i: (0,) * a.ndim)
    return pl.pallas_call(
        rec_fwd_kernel,
        grid=(length // CHUNK,),
        out_shape=(
            jax.ShapeDtypeStruct((length, SAVED * width), jnp.float32),
            jax.ShapeDtypeStruct((length, width), jnp.bfloat16),
        ),
        in_specs=[IN_SMEM, rows(2 * width), whole(wg), whole(par)],
        out_specs=[rows(SAVED * width), rows(width)],
        scratch_shapes=[
            pltpu.VMEM((CHUNK + HALO, width), jnp.float32),
            pltpu.VMEM((CHUNK, 2 * width), jnp.float32),
            pltpu.VMEM((8, width), jnp.float32),
        ],
        compiler_params=pltpu.CompilerParams(vmem_limit_bytes=40 * 2**20),
        name="recurrence_forward",
    )(lengths, pre, wg, par)


def each(count, body):
    def step(i, _):
        body(i)
        return 0

    lax.fori_loop(0, count, step, 0)


def line_place():
    return lax.axis_index("head"), lax.axis_size("head")


def peers(axis):
    n = lax.axis_size(axis)
    return [lax.rem(lax.axis_index(axis) + k, n) for k in range(1, n)]


def far_peer(axis):
    return lax.axis_size(axis) - 1 - lax.axis_index(axis)


def near_peers(axis):
    n, me = lax.axis_size(axis), lax.axis_index(axis)
    far = far_peer(axis)
    for k in range(n - 2):
        peer = k + jnp.where(k >= jnp.minimum(me, far), 1, 0)
        peer = peer + jnp.where(k + 1 >= jnp.maximum(me, far), 1, 0)
        ahead = jnp.where(peer < me, 1, 0) + jnp.where(n - 1 - peer < me, 1, 0)
        yield k, peer, me - ahead


def peer_barrier(axes):
    barrier = pltpu.get_barrier_semaphore()
    count = 0
    for axis in axes:
        for peer in peers(axis):
            pl.semaphore_signal(
                barrier, inc=1, device_id={axis: peer}, device_id_type=pl.DeviceIdType.MESH
            )
            count += 1
    pl.semaphore_wait(barrier, count)


def wait_neighbours(sem, j, n):
    inside = (j > 0) & (j < n - 1)

    @pl.when(inside)
    def _():
        pl.semaphore_wait(sem, 2)

    @pl.when(jnp.logical_not(inside))
    def _():
        pl.semaphore_wait(sem, 1)


def line_barrier(j, n):
    barrier = pltpu.get_barrier_semaphore()
    for side in (-1, 1):

        @pl.when((j + side >= 0) & (j + side < n))
        def _():
            pl.semaphore_signal(
                barrier, inc=1, device_id={"head": j + side}, device_id_type=pl.DeviceIdType.MESH
            )

    wait_neighbours(barrier, j, n)


class Gather:
    def __init__(self, j, n, buf, send, recv):
        self.j, self.n, self.buf, self.send, self.recv = j, n, buf, send, recv
        self.span = buf.shape[1] // PARTS

    def copy(self, block, s, side, source=None):
        part = pl.ds(s * self.span, self.span)
        target = self.buf.at[block, part]
        return pltpu.make_async_remote_copy(
            src_ref=target if source is None else source.at[part],
            dst_ref=target,
            send_sem=self.send.at[(side + 1) // 2, block, s],
            recv_sem=self.recv.at[block, s],
            device_id={"head": self.j + side},
            device_id_type=pl.DeviceIdType.MESH,
        )

    def there(self, side):
        return (self.j + side >= 0) & (self.j + side < self.n)

    def flows(self, t):
        for side in (1, -1):
            block = self.j - side * t
            yield side, block, (block >= 0) & (block < self.n)

    def start(self, source):
        for s in range(PARTS):
            for side in (1, -1):

                @pl.when(self.there(side))
                def _():
                    self.copy(self.j, s, side, source).start()

    def step(self, t):
        for s in range(PARTS):
            for side, block, live in self.flows(t):

                @pl.when(live)
                def _():
                    self.copy(block, s, -side).wait_recv()

                @pl.when(live & self.there(side))
                def _():
                    self.copy(block, s, side).start()

    def finish(self):
        def drain(t):
            for s in range(PARTS):
                for side, block, live in self.flows(t):

                    @pl.when(live & self.there(side))
                    def _():
                        self.copy(block, s, side).wait_send()

        each(self.n, drain)


class Scatter:
    def __init__(self, j, n, own, held, send, recv):
        self.j, self.n, self.own, self.held, self.send, self.recv = j, n, own, held, send, recv
        self.span = own.shape[1] // PARTS
        self.compact = own.shape[0] != n

    def place(self, block, side):
        return block if not self.compact else (1 - side) // 2

    def last(self):
        return self.j if not self.compact else 2

    def rows(self, s):
        return pl.ds(s * self.span, self.span)

    def slot(self, block, side, at):
        return block if side == 1 else jnp.where(block == at, self.n, block)

    def arrival(self, slot, s):
        return pltpu.make_async_copy(
            self.held.at[slot, self.rows(s)], self.held.at[slot, self.rows(s)], self.recv.at[slot, s]
        )

    def flows(self, t):
        for side in (1, -1):
            lag = self.j if side == 1 else self.n - 1 - self.j
            block = self.n - 1 - (t - lag) if side == 1 else t - lag
            yield side, block, (t >= lag) & (t <= self.n - 2)

    def copy(self, source, block, s, side):
        slot = self.slot(block, side, self.j + side)
        return pltpu.make_async_remote_copy(
            src_ref=source.at[block, self.rows(s)],
            dst_ref=self.held.at[slot, self.rows(s)],
            send_sem=self.send.at[block, s],
            recv_sem=self.recv.at[slot, s],
            device_id={"head": self.j + side},
            device_id_type=pl.DeviceIdType.MESH,
        )

    def step(self, t):
        for s in range(PARTS):
            for side, block, live in self.flows(t):
                behind = (self.j - side >= 0) & (self.j - side < self.n)

                @pl.when(live & jnp.logical_not(behind))
                def _():
                    if self.compact:
                        self.held[block, self.rows(s), :] = self.own[
                            self.place(block, side), self.rows(s), :
                        ]
                        self.copy(self.held, block, s, side).start()
                    else:
                        self.copy(self.own, block, s, side).start()

                @pl.when(live & behind)
                def _():
                    self.arrival(block, s).wait()
                    self.add(block, s, side)
                    self.copy(self.held, block, s, side).start()

    def add(self, block, s, side):
        def add_rows(i):
            rows = pl.ds(pl.multiple_of(s * self.span + i * STRIP, STRIP), STRIP)
            total = self.own[self.place(block, side), rows, :].astype(jnp.float32) + self.held[
                block, rows, :
            ].astype(jnp.float32)
            self.held[block, rows, :] = total.astype(jnp.bfloat16)

        each(self.span // STRIP, add_rows)

    def arrive(self):
        for s in range(PARTS):

            @pl.when(self.j > 0)
            def _():
                self.arrival(self.j, s).wait()

            @pl.when(self.j < self.n - 1)
            def _():
                self.arrival(self.n, s).wait()

    def result(self, rows):
        total = self.own[self.last(), rows, :].astype(jnp.float32)
        left = self.held[self.j, rows, :].astype(jnp.float32)
        right = self.held[self.n, rows, :].astype(jnp.float32)
        total = total + jnp.where(self.j > 0, left, 0.0)
        return total + jnp.where(self.j < self.n - 1, right, 0.0)

    def finish(self):
        def drain(t):
            for s in range(PARTS):
                for side, block, live in self.flows(t):

                    @pl.when(live)
                    def _():
                        self.copy(self.held, block, s, side).wait_send()

        each(self.n - 1, drain)


class Share:
    def __init__(self, axis, slots, send, recv):
        self.axis, self.slots, self.send, self.recv = axis, slots, send, recv
        self.me = lax.axis_index(axis)

    def copy(self, slot, peer, source=None):
        return pltpu.make_async_remote_copy(
            src_ref=self.slots.at[slot] if source is None else source,
            dst_ref=self.slots.at[slot],
            send_sem=self.send.at[peer],
            recv_sem=self.recv.at[slot],
            device_id={self.axis: peer},
            device_id_type=pl.DeviceIdType.MESH,
        )

    def start(self, sources=None):
        for peer in peers(self.axis):
            source = None if sources is None else sources.at[peer]
            self.copy(self.me, peer, source).start()

    def arrive(self):
        for peer in peers(self.axis):
            self.copy(peer, peer).wait_recv()

    def finish(self):
        for peer in peers(self.axis):
            self.copy(self.me, peer).wait_send()


def share_sems(axis):
    n = lax.axis_size(axis)
    return [pltpu.SemaphoreType.DMA((n,)), pltpu.SemaphoreType.DMA((n,))]


class Sum:
    def __init__(self, terms, slots, total, sems):
        self.terms, self.slots, self.total = terms, slots, total
        self.parts = Share("dp", slots, sems[0], sems[1])
        self.whole = Share("dp", total, sems[2], sems[3])
        self.me, self.sem = self.parts.me, sems[4]

    def start(self):
        self.parts.start(self.terms)

    def keep(self):
        return pltpu.make_async_copy(self.slots.at[self.me], self.total.at[self.me], self.sem)

    def spread(self):
        self.parts.arrive()
        rows = self.slots.shape[1]

        def add(part):
            value = jnp.zeros((STRIP, self.slots.shape[2]), jnp.float32)
            for i in range(self.slots.shape[0]):
                mine = self.terms[i, part, :].astype(jnp.float32)
                other = self.slots[i, part, :].astype(jnp.float32)
                value = value + jnp.where(self.me == i, mine, other)
            self.slots[self.me, part, :] = value.astype(jnp.bfloat16)

        strips(rows, add)
        for peer in peers("dp"):
            self.whole.copy(self.me, peer, self.slots.at[self.me]).start()
        self.keep().start()

    def finish(self):
        self.whole.arrive()
        self.keep().wait()
        self.parts.finish()
        self.whole.finish()


def sum_sems():
    return [*share_sems("dp"), *share_sems("dp"), pltpu.SemaphoreType.DMA]


def gather_sems(n):
    return [pltpu.SemaphoreType.DMA((2, n, PARTS)), pltpu.SemaphoreType.DMA((n, PARTS))]


def scatter_sems(n):
    return [pltpu.SemaphoreType.DMA((n, PARTS)), pltpu.SemaphoreType.DMA((n + 1, PARTS))]


def line_call(kernel, ident, name, out_shape, in_specs, out_specs, scratch, cost=None):
    return pl.pallas_call(
        kernel,
        out_shape=out_shape,
        in_specs=in_specs,
        out_specs=out_specs,
        scratch_shapes=scratch,
        compiler_params=pltpu.CompilerParams(
            collective_id=ident, has_side_effects=True, vmem_limit_bytes=VMEM_BYTES
        ),
        name=name,
    )


STRIP = 16


def strips(rows, body):
    each(rows // STRIP, lambda i: body(pl.ds(pl.multiple_of(i * STRIP, STRIP), STRIP)))


def project_kernel(
    stream, gain, wbi, rows_out, pre, normed, rows, send, recv, keep_sem
):
    j, n = line_place()
    line_barrier(j, n)
    local = stream.shape[0]

    def norm(part):
        _, unit = rms_parts(stream[part, :].astype(jnp.float32))
        normed[part, :] = (unit * gain[...]).astype(jnp.bfloat16)

    strips(local, norm)
    gather = Gather(j, n, rows, send, recv)
    gather.start(normed)

    def project(block, source):
        part = pl.ds(pl.multiple_of(block * local, local), local)
        pre[part, :] = contract_cols(source, wbi[...])

    def keep(source, block):
        return pltpu.make_async_copy(source, rows_out.at[block], keep_sem.at[block])

    keep(normed, j).start()
    project(j, normed[...])

    def visit(v):
        t = v // 2 + 1
        block = jnp.where(v % 2 == 0, j - t, j + t)

        @pl.when(v % 2 == 0)
        def _():
            gather.step(t)

        @pl.when((block >= 0) & (block < n))
        def _():
            keep(rows.at[block], block).start()
            project(block, rows[block])

    each(2 * (n - 1), visit)
    gather.finish()
    keep(normed, j).wait()
    for k in range(1, n):
        other = lax.rem(j + k, n)
        keep(rows.at[other], other).wait()


def project(stream, gain, wbi):
    n = lax.axis_size("head")
    local, depth = stream.shape
    return line_call(
        project_kernel, 0, "gather_project",
        (
            jax.ShapeDtypeStruct((n, local, depth), jnp.bfloat16),
            jax.ShapeDtypeStruct((n * local, wbi.shape[0]), jnp.float32),
        ),
        [IN_VMEM] * 3,
        [IN_ANY, IN_VMEM],
        [
            pltpu.VMEM((local, depth), jnp.bfloat16),
            pltpu.VMEM((n, local, depth), jnp.bfloat16),
            *gather_sems(n),
            pltpu.SemaphoreType.DMA((n,)),
        ],
    )(stream, gain, wbi)


def mixer_out_kernel(
    gated, wo, stream, gain, cot, cot_rows, hidden, low_out, own, held,
    send, recv, gsend, grecv, sem,
):
    j, n = line_place()
    line_barrier(j, n)
    local = stream.shape[0]
    gather = Gather(j, n, cot_rows, gsend, grecv)
    scatter = Scatter(j, n, own, held, send, recv)

    def compute(block):
        part = pl.ds(pl.multiple_of(block * local, local), local)
        own[block] = jnp.dot(
            gated[part, :], wo[...], preferred_element_type=jnp.float32
        ).astype(jnp.bfloat16)

    def ahead(t):
        for _, block, live in scatter.flows(t):
            pl.when(live)(lambda: compute(block))

    ahead(0)
    mine = pltpu.make_async_copy(cot, cot_rows.at[j], sem)
    mine.start()

    def step(t):
        scatter.step(t)

        @pl.when(t == 0)
        def _():
            gather.start(cot)

        ahead(t + 1)

        @pl.when(t == 0)
        def _():
            compute(j)

        @pl.when(t > 0)
        def _():
            gather.step(t)

    each(n - 1, step)
    scatter.arrive()

    def settle(part):
        total = stream[part, :].astype(jnp.float32) + scatter.result(part)
        hidden[part, :] = total
        _, unit = rms_parts(total)
        low_out[part, :] = (unit * gain[...]).astype(jnp.bfloat16)

    strips(local, settle)
    gather.step(n - 1)
    scatter.finish()
    gather.finish()
    mine.wait()


def mixer_out(gated, wo, stream, gain, cot):
    n = lax.axis_size("head")
    local, depth = stream.shape
    return line_call(
        mixer_out_kernel, 1, "mixer_out",
        (
            jax.ShapeDtypeStruct((n, local, depth), jnp.bfloat16),
            jax.ShapeDtypeStruct((local, depth), jnp.float32),
            jax.ShapeDtypeStruct((local, depth), jnp.bfloat16),
        ),
        [IN_VMEM] * 5,
        [IN_ANY, IN_VMEM, IN_VMEM],
        [
            pltpu.VMEM((n, local, depth), jnp.bfloat16),
            pltpu.VMEM((n + 1, local, depth), jnp.bfloat16),
            *scatter_sems(n),
            *gather_sems(n),
            pltpu.SemaphoreType.DMA,
        ],
    )(gated, wo, stream, gain, cot)


def ffn_kernel(
    low, cot_rows, cot, hidden, gain, wg, wu, wd,
    out_part, terms, far_terms, resid, resid_low, gain_grad,
    rows, cot_unit, kept, own, held, stage, wstage, cot_cols,
    gsend, grecv, send, recv, cot_sem, out_sem, col_sem, term_sem, fsend, frecv,
):
    j, n = line_place()
    peer_barrier(("head", "dp"))
    f32, bf16 = jnp.float32, jnp.bfloat16
    local, depth = low.shape
    units = wg.shape[1]
    fstep = 256 if units % 256 == 0 else LANES
    dstep = 512
    gather = Gather(j, n, rows, gsend, grecv)
    scatter = Scatter(j, n, own, held, send, recv)
    gather.start(low)
    rows[j] = low[...]

    def fetch(block):
        return pltpu.make_async_copy(cot_rows.at[block], cot_unit, cot_sem)

    def put(block):
        return pltpu.make_async_copy(stage, out_part.at[block], out_sem)

    def unit(block):
        span = pl.ds(pl.multiple_of(block * local, local), local)
        x = rows.at[block]
        for f in range(0, units, fstep):
            cols = slice(f, f + fstep)
            gate = jnp.dot(x[...], wg[:, cols], preferred_element_type=f32)
            act, slope = gelu_pair(gate)
            up = jnp.dot(x[...], wu[:, cols], preferred_element_type=f32)
            kept[2, span, cols] = (act * up).astype(bf16)
            grad = jnp.dot(cot_unit[...], wd[:, cols], preferred_element_type=f32)
            kept[0, span, cols] = (grad * up * slope).astype(bf16)
            kept[1, span, cols] = (grad * act).astype(bf16)
        for d in range(0, depth, dstep):
            cols = slice(d, d + dstep)
            own[block, :, cols] = (
                contract_cols(kept[0, span, :], wg[cols, :])
                + contract_cols(kept[1, span, :], wu[cols, :])
            ).astype(bf16)
            stage[:, cols] = contract_cols(kept[2, span, :], wd[cols, :]).astype(bf16)

    def visit(v):
        t = (v + 1) // 2
        block = jnp.where(v % 2 == 1, j - t, j + t)
        live = (block >= 0) & (block < n)

        @pl.when(live)
        def _():
            fetch(block).start()

        @pl.when(v % 2 == 1)
        def _():
            gather.step(t)

        @pl.when(live)
        def _():
            fetch(block).wait()

            @pl.when(v > 0)
            def _():
                put(block).wait()

            unit(block)
            put(block).start()

    each(2 * n - 1, visit)
    put(j).wait()

    width = depth // n
    per = depth // terms.shape[0] // width

    far = far_peer("dp")

    def columns(b):
        return pl.ds(pl.multiple_of(lax.rem(b + far * per, n) * width, width), width)

    def take(b):
        return pltpu.make_async_copy(cot_rows.at[:, :, columns(b)], cot_cols, col_sem)

    def give(b):
        owner = lax.rem(b // per + far, n // per)
        spot = pl.ds(pl.multiple_of(lax.rem(b, per) * width, width), width)
        return pltpu.make_async_copy(wstage, terms.at[owner, :, spot, :], term_sem)

    def send_far():
        return pltpu.make_async_remote_copy(
            src_ref=terms.at[far],
            dst_ref=far_terms,
            send_sem=fsend,
            recv_sem=frecv,
            device_id={"dp": far},
            device_id_type=pl.DeviceIdType.MESH,
        )

    def weights(b):
        cols = columns(b)
        xs = rows[:, :, cols].reshape(n * local, width)
        take(b).wait()

        @pl.when(b > 0)
        def _():
            give(b).wait()

        @pl.when(b == per)
        def _():
            send_far().start()

        wstage[0] = contract_rows(xs, kept[0]).astype(bf16)
        wstage[1] = contract_rows(xs, kept[1]).astype(bf16)
        wstage[2] = contract_rows(
            cot_cols[...].reshape(n * local, width), kept[2]
        ).astype(bf16)
        give(b).start()

        @pl.when(b + 1 < n)
        def _():
            take(b + 1).start()

    take(0).start()

    def step(t):
        pl.when(t < n - 1)(lambda: scatter.step(t))
        weights(t)

    each(n, step)
    scatter.arrive()
    gain_grad[...] = jnp.zeros_like(gain_grad)

    def settle(part):
        rinv, u = rms_parts(hidden[part, :])
        grad = scatter.result(part)
        gain_grad[...] += jnp.sum(grad * u, axis=0, keepdims=True)
        total = cot[part, :].astype(f32) + norm_back(u, rinv, gain[...], grad)
        resid[part, :] = total
        resid_low[part, :] = total.astype(bf16)

    strips(local, settle)
    give(0).wait()
    gather.finish()
    scatter.finish()
    send_far().wait()


def feed_forward(low, cot_rows, cot, hidden, gain, wg, wu, wd):
    n, group = lax.axis_size("head"), lax.axis_size("dp")
    local, depth = low.shape
    units = wg.shape[1]
    bf16 = jnp.bfloat16
    return line_call(
        ffn_kernel, 2, "feed_forward",
        (
            jax.ShapeDtypeStruct((n, local, depth), bf16),
            jax.ShapeDtypeStruct((group, 3, depth // group, units), bf16),
            jax.ShapeDtypeStruct((3, depth // group, units), bf16),
            jax.ShapeDtypeStruct((local, depth), jnp.float32),
            jax.ShapeDtypeStruct((local, depth), bf16),
            jax.ShapeDtypeStruct((1, depth), jnp.float32),
        ),
        [IN_VMEM, IN_ANY] + [IN_VMEM] * 6,
        [IN_ANY, IN_ANY, IN_ANY, IN_VMEM, IN_VMEM, IN_VMEM],
        [
            pltpu.VMEM((n, local, depth), bf16),
            pltpu.VMEM((local, depth), bf16),
            pltpu.VMEM((3, n * local, units), bf16),
            pltpu.VMEM((n, local, depth), bf16),
            pltpu.VMEM((n + 1, local, depth), bf16),
            pltpu.VMEM((local, depth), bf16),
            pltpu.VMEM((3, depth // n, units), bf16),
            pltpu.VMEM((n, local, depth // n), bf16),
            *gather_sems(n),
            *scatter_sems(n),
            *[pltpu.SemaphoreType.DMA] * 6,
        ],
    )(low, cot_rows, cot, hidden, gain, wg, wu, wd)


def back_kernel(
    lengths, low, out_part, hidden, terms, gated, wo, wbi, wg, par, pre, saved,
    normed_rows, stream, gain, resid, preffn_grad,
    layer_out, sums, stream_grad, ob_total, i_total, g_total, par_grad, gains,
    rows, own, held, dh, dpre, acc, dgate, dz, du, carry, dpar, wide,
    unit_bp, unit_h, unit_gated, unit_normed,
    obterms, obslots, iterms, islots, gterms, gslots, pslots, dslots, hslots,
    gsend, grecv, send4, recv4, send8, recv8, tsend, trecv, unit_sem, own_sem, chunk_sem,
    row_sem, wide_sem, free, psend, precv, dsend, drecv, hsend, hrecv, *sems,
):
    j, n = line_place()
    f32, bf16 = jnp.float32, jnp.bfloat16
    local, depth = stream.shape
    width = dh.shape[1]
    tiles = width // LANES
    peer_barrier(("head", "dp"))

    def near():
        for k, peer, slot in near_peers("dp"):
            yield pltpu.make_async_remote_copy(
                src_ref=terms.at[peer],
                dst_ref=sums.at[slot],
                send_sem=tsend.at[k],
                recv_sem=trecv.at[slot],
                device_id={"dp": peer},
                device_id_type=pl.DeviceIdType.MESH,
            )

    gather = Gather(j, n, rows, gsend, grecv)
    gather.start(low)
    for copy in near():
        copy.start()
    rows[j] = low[...]
    outs = Scatter(j, n, own, held, send4, recv4)
    acc[...] = jnp.zeros_like(acc)

    def fetch_out(block, slot):
        return pltpu.make_async_copy(out_part.at[block], own.at[slot], own_sem.at[slot])

    def outs_ahead(t):
        for start in (True, False):
            for side, block, live in outs.flows(t):
                copy = fetch_out(block, outs.place(block, side))
                pl.when(live)(copy.start if start else copy.wait)

    def outs_step(t):
        @pl.when((t >= 0) & (t < n - 1))
        def _():
            outs.step(t)
            outs_ahead(t + 1)

    outs_ahead(0)
    fetch_out(j, 2).start()
    fetch_out(j, 2).wait()

    def unit_copies(block):
        span = pl.ds(pl.multiple_of(block * local, local), local)
        return (
            pltpu.make_async_copy(pre.at[span, 0:width], unit_bp, unit_sem.at[0]),
            pltpu.make_async_copy(
                saved.at[span, 3 * width : 4 * width], unit_h, unit_sem.at[1]
            ),
            pltpu.make_async_copy(gated.at[span], unit_gated, unit_sem.at[2]),
            pltpu.make_async_copy(normed_rows.at[block], unit_normed, unit_sem.at[3]),
        )

    def unit(block):
        span = pl.ds(pl.multiple_of(block * local, local), local)
        dh[span, :] = contract_cols(rows[block], wo[...])

        def act(i):
            part = pl.ds(pl.multiple_of(i * BLOCK, BLOCK), BLOCK)
            spot = pl.ds(pl.multiple_of(block * local + i * BLOCK, BLOCK), BLOCK)
            for t in range(tiles):
                cols = pl.ds(t * LANES, LANES)
                grad = dh[spot, cols]
                value, slope = gelu_pair(unit_bp[part, cols])
                dpre[spot, cols] = (grad * unit_h[part, cols] * slope).astype(bf16)
                dh[spot, cols] = grad * value

        each(local // BLOCK, act)
        acc[0:width, :] += contract_rows(unit_gated[...], rows[block])
        acc[width : 2 * width, :] += contract_rows(dpre[span, 0:width], unit_normed[...])

    def visit(v):
        t = (v + 1) // 2
        block = jnp.where(v % 2 == 1, j - t, j + t)
        live = (block >= 0) & (block < n)

        @pl.when(live)
        def _():
            for copy in unit_copies(block):
                copy.start()

        @pl.when(v % 2 == 1)
        def _():
            gather.step(t)
            outs_step(t - 1 - LAG)

        @pl.when(live)
        def _():
            for copy in unit_copies(block):
                copy.wait()
            unit(block)

    each(2 * n - 1, visit)
    gather.finish()

    def pack(target, source, count):
        span = target.shape[1]

        def strip(i):
            row = pl.multiple_of(i * STRIP, STRIP)
            target[row // span, pl.ds(pl.multiple_of(lax.rem(row, span), STRIP), STRIP), :] = source[
                pl.ds(row, STRIP), :
            ].astype(bf16)

        each(count // STRIP, strip)

    obsum = Sum(obterms, obslots, ob_total, sems[0:5])
    isum = Sum(iterms, islots, i_total, sems[5:10])
    gsum = Sum(gterms, gslots, g_total, sems[10:15])
    pack(obterms, acc, 2 * width)
    obsum.start()
    load = pltpu.make_async_copy(normed_rows, rows, row_sem)
    load.start()
    load_hidden = pltpu.make_async_copy(hidden, wide, wide_sem.at[0])
    load_hidden.start()

    count = n * local // CHUNK

    def chunk_copies(i):
        base = lax.rem(i, 2) * (CHUNK + HALO)
        start = pl.multiple_of(i * CHUNK, CHUNK)
        ahead = pl.multiple_of(jnp.maximum(start - HALO, 0), HALO)
        halo, main = pl.ds(pl.multiple_of(base, HALO), HALO), pl.ds(
            pl.multiple_of(base + HALO, HALO), CHUNK
        )
        kept, x = slice(0, SAVED * width), slice(SAVED * width, (SAVED + 1) * width)
        pairs = (
            (saved.at[pl.ds(ahead, HALO)], acc.at[halo, kept]),
            (saved.at[pl.ds(start, CHUNK)], acc.at[main, kept]),
            (pre.at[pl.ds(ahead, HALO), width : 2 * width], acc.at[halo, x]),
            (pre.at[pl.ds(start, CHUNK), width : 2 * width], acc.at[main, x]),
        )
        return [
            pltpu.make_async_copy(a, b, chunk_sem.at[lax.rem(i, 2), k])
            for k, (a, b) in enumerate(pairs)
        ]

    def total(v):
        return jnp.sum(v, axis=0, keepdims=True)

    for copy in chunk_copies(count - 1):
        copy.start()
    du[...] = jnp.zeros_like(du)
    carry[...] = jnp.zeros_like(carry)
    dgate[...] = jnp.zeros_like(dgate)
    dpar[...] = jnp.zeros_like(dpar)

    def chunk(k):
        i = count - 1 - k

        @pl.when(i > 0)
        def _():
            for copy in chunk_copies(i - 1):
                copy.start()

        for copy in chunk_copies(i):
            copy.wait()
        base = lax.rem(i, 2) * (CHUNK + HALO)
        first = i * CHUNK
        du[CHUNK:, :] = du[0:HALO, :]

        def scan_step(b):
            row = pl.multiple_of(CHUNK - BLOCK - b * BLOCK, BLOCK)
            part = pl.ds(row, BLOCK)
            spot = pl.ds(pl.multiple_of(first + row, BLOCK), BLOCK)
            here = pl.ds(pl.multiple_of(base + HALO + row, HALO), BLOCK)
            halo = pl.ds(pl.multiple_of(base + row, HALO), BLOCK + HALO)
            fresh = doc_places(lengths, first + row, BLOCK) == 0
            place = lax.broadcasted_iota(jnp.int32, (BLOCK, LANES), 0)
            inner = place % 8
            for t in range(tiles):
                cols = pl.ds(t * LANES, LANES)
                u, r, e = (acc[here, pl.ds(m * width + t * LANES, LANES)] for m in range(3))
                prior = acc[halo, pl.ds(3 * width + t * LANES, LANES)][HALO - 1 : HALO - 1 + BLOCK]
                near_h = dh[spot, cols]
                decay = par[DECAY : DECAY + 1, cols]
                c, m, ratio = decay_terms(r, decay, fresh)
                b_, a_ = c * near_h, c
                for d in (1, 2, 4):
                    near_row = inner < 8 - d
                    b_ = b_ + a_ * jnp.where(near_row, pltpu.roll(b_, BLOCK - d, 0), 0.0)
                    a_ = a_ * jnp.where(near_row, pltpu.roll(a_, BLOCK - d, 0), 1.0)
                later = carry[0:1, cols]
                pieces = []
                front = later
                for g in reversed(range(BLOCK // 8)):
                    eight = slice(g * 8, g * 8 + 8)
                    state = b_[eight] + a_[eight] * front
                    front = state[0:1]
                    pieces.append(state)
                carry[0:1, cols] = front
                mu = jnp.concatenate(pieces[::-1], axis=0)
                adj = near_h + jnp.where(
                    place == BLOCK - 1, later, pltpu.roll(mu, BLOCK - 1, 0)
                )
                eu = e * u
                dlog = adj * (prior * c - eu * ratio)
                dpar[G_DECAY : G_DECAY + 1, cols] += total(dlog * r)
                dzr = decay * dlog * (r * (1.0 - r))
                dze = adj * m * eu * (1.0 - e)
                dpar[G_RATE : G_RATE + 1, cols] += total(dzr)
                dpar[G_ENTRY : G_ENTRY + 1, cols] += total(dze)
                dz[part, cols] = dzr.astype(bf16)
                dz[part, pl.ds(width + t * LANES, LANES)] = dze.astype(bf16)
                du[part, cols] = adj * m * e

        each(CHUNK // BLOCK, scan_step)
        u_chunk = acc[pl.ds(pl.multiple_of(base + HALO, HALO), CHUNK), 0:width]
        du[0:CHUNK, :] += contract_cols(dz[...], wg[...])
        dgate[...] += contract_rows(u_chunk.astype(bf16), dz[...])

        def conv_step(b):
            row = pl.multiple_of(b * BLOCK, BLOCK)
            spot = pl.ds(pl.multiple_of(first + row, BLOCK), BLOCK)
            halo = pl.ds(pl.multiple_of(base + row, HALO), BLOCK + HALO)
            place = doc_places(lengths, first + row, BLOCK + HALO)
            for t in range(tiles):
                cols = pl.ds(t * LANES, LANES)
                ds = du[pl.ds(row, BLOCK + HALO), cols]
                xs = acc[halo, pl.ds(SAVED * width + t * LANES, LANES)]
                mine = ds[0:BLOCK]
                dx = par[TAP : TAP + 1, cols] * mine
                dpar[G_BIAS : G_BIAS + 1, cols] += total(mine)
                dpar[G_TAP : G_TAP + 1, cols] += total(mine * xs[HALO:])
                for k in range(1, CONVW):
                    inside = jnp.where(place >= k, ds, 0.0)
                    dx = dx + par[TAP + k : TAP + k + 1, cols] * inside[k : k + BLOCK]
                    dpar[G_TAP + k : G_TAP + k + 1, cols] += total(
                        inside[0:BLOCK] * xs[HALO - k : HALO - k + BLOCK]
                    )
                dpre[spot, pl.ds(width + t * LANES, LANES)] = dx.astype(bf16)

        each(CHUNK // BLOCK, conv_step)
        if LAG:
            late = n - 1 - LAG

            @pl.when((k % 2 == 1) & (k // 2 < LAG))
            def _():
                outs_step(late + k // 2)

    each(count, chunk)

    pack(gterms, dgate, width)
    gsum.start()
    pshare = Share("dp", pslots, psend, precv)
    pslots[pshare.me] = dpar[...]
    pshare.start()
    outs.arrive()
    load_hidden.wait()

    def settle_out(part):
        layer_out[part, :] = (wide[part, :] + outs.result(part)).astype(bf16)

    strips(local, settle_out)
    outs.finish()
    load_resid = pltpu.make_async_copy(resid, wide, wide_sem.at[1])
    load_resid.start()
    for side in (-1, 1):

        @pl.when((j + side >= 0) & (j + side < n))
        def _():
            pl.semaphore_signal(
                free, inc=1, device_id={"head": j + side}, device_id_type=pl.DeviceIdType.MESH
            )

    scatter = Scatter(j, n, own, held, send8, recv8)

    def compute(block, slot):
        span = pl.ds(pl.multiple_of(block * local, local), local)
        own[slot] = jnp.dot(dpre[span, :], wbi[...], preferred_element_type=f32).astype(bf16)

    def ahead(t):
        for side, block, live in scatter.flows(t):
            pl.when(live)(functools.partial(compute, block, scatter.place(block, side)))

    ahead(0)
    wait_neighbours(free, j, n)
    scatter.step(0)
    ahead(1)
    load.wait()
    for c in range(0, width, LANES):
        acc[c : c + LANES, :] = contract_rows(
            dpre[:, width + c : width + c + LANES], rows[...].reshape(n * local, depth)
        )
    pack(iterms, acc, width)
    isum.start()
    compute(j, 2)
    obsum.spread()

    def step(t):
        scatter.step(t)
        ahead(t + 1)

        @pl.when(t == n // 2)
        def _():
            gsum.spread()
            isum.spread()

    lax.fori_loop(1, n - 1, lambda t, _: (step(t), 0)[1], 0)
    scatter.arrive()
    load_resid.wait()
    gains[...] = jnp.zeros_like(gains)

    def settle(part):
        rinv, u = rms_parts(stream[part, :].astype(f32))
        grad = scatter.result(part)
        gains[0:1, :] += jnp.sum(grad * u, axis=0, keepdims=True)
        value = wide[part, :] + norm_back(u, rinv, gain[...], grad)
        stream_grad[part, :] = value.astype(bf16)

    strips(local, settle)

    gains[1:2, :] = preffn_grad[...]
    for axis, slots, ssem, rsem in (("dp", dslots, dsend, drecv), ("head", hslots, hsend, hrecv)):
        share = Share(axis, slots, ssem, rsem)
        slots[share.me] = gains[...]
        share.start()
        share.arrive()
        value = slots[0]
        for i in range(1, slots.shape[0]):
            value = value + slots[i]
        gains[...] = value
        share.finish()

    pshare.arrive()
    value = pslots[0]
    for i in range(1, pslots.shape[0]):
        value = value + pslots[i]
    par_grad[...] = value
    pshare.finish()
    for one in (gsum, obsum, isum):
        one.finish()
    scatter.finish()
    for copy in near():
        copy.wait_send()
    for k in range(sums.shape[0]):
        pltpu.make_async_copy(sums.at[k], sums.at[k], trecv.at[k]).wait()


def mixer_back(
    lengths, low, out_part, hidden, terms, gated, wo, wbi, wg, par, pre, saved,
    normed_rows, stream, gain, resid, preffn_grad,
):
    n, group = lax.axis_size("head"), lax.axis_size("dp")
    local, depth = stream.shape
    width, tokens = wo.shape[0], pre.shape[0]
    f32, bf16 = jnp.float32, jnp.bfloat16
    ob = (group, 2 * width // group, depth)
    one = (group, width // group, depth)
    gate = (group, width // group, 2 * width)
    dma = pltpu.SemaphoreType.DMA
    shape = jax.ShapeDtypeStruct
    return line_call(
        back_kernel, 3, "mixer_back",
        (
            shape((local, depth), bf16),
            shape((group - 2, *terms.shape[1:]), bf16),
            shape((local, depth), bf16),
            shape(ob, bf16),
            shape(one, bf16),
            shape(gate, bf16),
            shape((PARAMS, width), f32),
            shape((8, depth), f32),
        ),
        [
            IN_SMEM, IN_VMEM, IN_ANY, IN_ANY, IN_ANY, IN_ANY, *[IN_VMEM] * 4, IN_ANY, IN_ANY,
            IN_ANY, IN_VMEM, IN_VMEM, IN_ANY, IN_VMEM,
        ],
        [IN_VMEM, IN_ANY, IN_VMEM, IN_ANY, IN_ANY, IN_ANY, IN_VMEM, IN_VMEM],
        [
            pltpu.VMEM((n, local, depth), bf16),
            pltpu.VMEM((3, local, depth), bf16),
            pltpu.VMEM((n + 1, local, depth), bf16),
            pltpu.VMEM((tokens, width), f32),
            pltpu.VMEM((tokens, 2 * width), bf16),
            pltpu.VMEM((max(2 * width, 2 * (CHUNK + HALO)), depth), f32),
            pltpu.VMEM((width, 2 * width), f32),
            pltpu.VMEM((CHUNK, 2 * width), bf16),
            pltpu.VMEM((CHUNK + HALO, width), f32),
            pltpu.VMEM((8, width), f32),
            pltpu.VMEM((PARAMS, width), f32),
            pltpu.VMEM((local, depth), f32),
            pltpu.VMEM((local, width), f32),
            pltpu.VMEM((local, width), f32),
            pltpu.VMEM((local, width), bf16),
            pltpu.VMEM((local, depth), bf16),
            pltpu.VMEM(ob, bf16),
            pltpu.VMEM(ob, bf16),
            pltpu.VMEM(one, bf16),
            pltpu.VMEM(one, bf16),
            pltpu.VMEM(gate, bf16),
            pltpu.VMEM(gate, bf16),
            pltpu.VMEM((group, PARAMS, width), f32),
            pltpu.VMEM((group, 8, depth), f32),
            pltpu.VMEM((n, 8, depth), f32),
            *gather_sems(n),
            *scatter_sems(n),
            *scatter_sems(n),
            dma((group,)),
            dma((group,)),
            dma((4,)),
            dma((3,)),
            dma((2, 4)),
            dma,
            dma((2,)),
            pltpu.SemaphoreType.REGULAR,
            *share_sems("dp"),
            *share_sems("dp"),
            *share_sems("head"),
            *sum_sems(),
            *sum_sems(),
            *sum_sems(),
        ],
    )(
        lengths, low, out_part, hidden, terms, gated, wo, wbi, wg, par, pre, saved,
        normed_rows, stream, gain, resid, preffn_grad,
    )


def widen(values, width):
    return jnp.pad(values, ((0, width - values.shape[0]), (0, 0)))


def block_diagonal(weights, width):
    heads, size = weights.shape[0], weights.shape[1]
    placed = [
        jnp.pad(weights[i], ((i * size, width - (i + 1) * size),) * 2) for i in range(heads)
    ]
    return functools.reduce(jnp.add, placed)


def diagonal_blocks(dense, heads, size):
    return jnp.stack(
        [dense[i * size : (i + 1) * size, i * size : (i + 1) * size] for i in range(heads)]
    )


def shards(
    stream, doc_lengths, premix_gain, branch_weight, input_weight, conv_kernel, conv_bias,
    rate_weight, rate_bias, entry_weight, entry_bias, decay_param, output_weight, preffn_gain,
    ffn_gate, ffn_upward, ffn_down, cotangent,
):
    f32, bf16 = jnp.float32, jnp.bfloat16
    heads, size = rate_bias.shape
    chans = branch_weight.shape[1]
    width = -(-chans // LANES) * LANES

    slope = -DECAY_SCALE * jax.nn.softplus(decay_param.astype(f32))
    par = jnp.concatenate(
        [
            conv_bias[None].astype(f32),
            conv_kernel.astype(f32),
            rate_bias.reshape(1, -1).astype(f32),
            entry_bias.reshape(1, -1).astype(f32),
            slope[None],
        ]
    )
    par = jnp.pad(par, ((0, 0), (0, width - chans)), constant_values=-1.0)
    par = jnp.where((jnp.arange(width)[None] < chans) | (jnp.arange(PARAMS)[:, None] == DECAY), par, 0.0)
    wg = jnp.concatenate(
        [block_diagonal(rate_weight, width), block_diagonal(entry_weight, width)], axis=1
    )
    wbi = jnp.concatenate([widen(branch_weight.T, width), widen(input_weight.T, width)])
    wo = widen(output_weight, width)

    premix = premix_gain.astype(f32)[None]
    preffn = preffn_gain.astype(f32)[None]
    normed_rows, pre = project(stream, premix, wbi)
    saved, gated = rec_fwd(doc_lengths, pre, wg, par)
    cot_rows, hidden_in, ffn_low = mixer_out(gated, wo, stream, preffn, cotangent)

    out_part, terms, far_terms, resid_grad, resid_low, preffn_grad = feed_forward(
        ffn_low, cot_rows, cotangent, hidden_in, preffn, ffn_gate, ffn_upward, ffn_down
    )

    layer_out, sums, stream_grad, ob_grad, input_grad, gate_grad, dpar, gains = mixer_back(
        doc_lengths, resid_low, out_part, hidden_in, terms, gated, wo, wbi, wg, par, pre, saved,
        normed_rows, stream, premix, resid_grad, preffn_grad,
    )
    mine = lax.dynamic_index_in_dim(terms, lax.axis_index("dp"), keepdims=False)
    ffn_sums = mine.astype(f32) + far_terms.astype(f32) + jnp.sum(sums.astype(f32), axis=0)
    ob_grad = ob_grad.reshape(2 * width, -1).astype(f32)
    input_grad = input_grad.reshape(width, -1).astype(f32)
    gate_grad = gate_grad.reshape(width, -1).astype(f32)
    dpar = dpar[:, :chans]
    decay_grad = dpar[G_DECAY] * (-DECAY_SCALE * jax.nn.sigmoid(decay_param.astype(f32)))
    return (
        layer_out,
        stream_grad,
        gains[0],
        ob_grad[width : width + chans].T,
        input_grad[:chans].T,
        dpar[G_TAP : G_TAP + CONVW],
        dpar[G_BIAS],
        diagonal_blocks(gate_grad[:, :width], heads, size),
        dpar[G_RATE].reshape(heads, size),
        diagonal_blocks(gate_grad[:, width:], heads, size),
        dpar[G_ENTRY].reshape(heads, size),
        decay_grad,
        ob_grad[:chans],
        gains[1],
        ffn_sums[0],
        ffn_sums[1],
        ffn_sums[2],
    )


def solution(mesh):
    placed = (
        P(("dp", "head"), None),
        P("dp", None),
        P(),
        P(None, "head"),
        P(None, "head"),
        P(None, "head"),
        P("head"),
        P("head", None, None),
        P("head", None),
        P("head", None, None),
        P("head", None),
        P("head"),
        P("head", None),
        P(),
        P(None, "head"),
        P(None, "head"),
        P(None, "head"),
        P(("dp", "head"), None),
    )
    return jax.shard_map(
        shards,
        mesh=mesh,
        in_specs=placed,
        out_specs=(
            P(("dp", "head"), None),
            P(("dp", "head"), None),
            P(),
            P(None, "head"),
            P(None, "head"),
            P(None, "head"),
            P("head"),
            P("head", None, None),
            P("head", None),
            P("head", None, None),
            P("head", None),
            P("head"),
            P("head", None),
            P(),
            P("dp", "head"),
            P("dp", "head"),
            P("dp", "head"),
        ),
        check_vma=False,
    )
```

```python
import functools
import math

import jax
import jax.numpy as jnp
from jax import lax
from jax.experimental import pallas as pl
from jax.experimental.pallas import tpu as pltpu
from jax.sharding import PartitionSpec as P

CONVW = 4
SEQ = 2048
CHUNK = 256
BLOCK = 64
LANES = 128
HALO = 8
PARTS = 2
LAG = 1
FAR_TERMS = 2
VMEM_BYTES = 62 * 2**20
IN_VMEM = pl.BlockSpec(memory_space=pltpu.VMEM)
IN_SMEM = pl.BlockSpec(memory_space=pltpu.SMEM)
IN_ANY = pl.BlockSpec(memory_space=pl.ANY)

EPSILON = 1e-06
DECAY_SCALE = 8.0
GELU_A = math.sqrt(2.0 / math.pi)
GELU_B = 0.044715

BIAS, TAP, RATE_B, ENTRY_B, DECAY = 0, 1, 5, 6, 7
PARAMS = 8
SAVED = 4
G_BIAS, G_TAP, G_RATE, G_ENTRY, G_DECAY = 0, 1, 5, 6, 7


def rms_parts(values):
    rinv = lax.rsqrt(jnp.mean(values * values, axis=-1, keepdims=True) + EPSILON)
    return rinv, values * rinv


def norm_back(unit, rinv, gain, grad):
    q = gain * grad
    return rinv * (q - unit * jnp.mean(q * unit, axis=-1, keepdims=True))


def contract_cols(leading, trailing):
    return lax.dot_general(
        leading, trailing, (((1,), (1,)), ((), ())), preferred_element_type=jnp.float32
    )


def contract_rows(leading, trailing):
    return lax.dot_general(
        leading, trailing, (((0,), (0,)), ((), ())), preferred_element_type=jnp.float32
    )


def gelu_pair(v):
    sq = v * v
    th = jnp.tanh(GELU_A * v * (1.0 + GELU_B * sq))
    half = 0.5 * (1.0 + th)
    slope = half + 0.5 * v * (1.0 - th * th) * (GELU_A * (1.0 + 3.0 * GELU_B * sq))
    return v * half, slope


def gelu(v):
    return v * (0.5 * (1.0 + jnp.tanh(GELU_A * v * (1.0 + GELU_B * v * v))))


def decay_terms(rate_gate, slope, fresh):
    log_decay = slope * rate_gate
    c = jnp.exp(log_decay)
    y = 2.0 * log_decay
    series = 1.0 + y * (1.0 / 7.0)
    for n in (6, 5, 4, 3, 2):
        series = 1.0 + (y * (1.0 / n)) * series
    sq = c * c
    q = jnp.where(y > -0.5, -y * series, 1.0 - sq)
    rsq = lax.rsqrt(jnp.maximum(q, 1e-37))
    return (
        jnp.where(fresh, 0.0, c),
        jnp.where(fresh, 1.0, q * rsq),
        jnp.where(fresh, 0.0, sq * rsq),
    )


def doc_places(lengths, first, rows):
    spots = first + lax.broadcasted_iota(jnp.int32, (rows, LANES), 0)
    begin = jnp.zeros((rows, LANES), jnp.int32)
    start = jnp.int32(0)
    for k in range(lengths.shape[1] - 1):
        start = start + lengths[0, k]
        begin = jnp.where(spots >= start, start, begin)
    return spots - begin


def each(count, body):
    def step(i, _):
        body(i)
        return 0

    lax.fori_loop(0, count, step, 0)


def line_place():
    return lax.axis_index("head"), lax.axis_size("head")


def peers(axis):
    n = lax.axis_size(axis)
    return [lax.rem(lax.axis_index(axis) + k, n) for k in range(1, n)]


def far_peer(axis):
    return lax.axis_size(axis) - 1 - lax.axis_index(axis)


def far_copies(terms, far_terms, sems):
    far = far_peer("dp")
    return [
        pltpu.make_async_remote_copy(
            src_ref=terms.at[far, k],
            dst_ref=far_terms.at[k],
            send_sem=sems.at[0, k],
            recv_sem=sems.at[1, k],
            device_id={"dp": far},
            device_id_type=pl.DeviceIdType.MESH,
        )
        for k in range(far_terms.shape[0])
    ]


def near_copies(terms, near_terms, last_terms, sems):
    n, me, far = lax.axis_size("dp"), lax.axis_index("dp"), far_peer("dp")
    for k in range(n - 2):
        peer = k + jnp.where(k >= jnp.minimum(me, far), 1, 0)
        peer = peer + jnp.where(k + 1 >= jnp.maximum(me, far), 1, 0)
        slot = me - jnp.where(peer < me, 1, 0) - jnp.where(n - 1 - peer < me, 1, 0)
        yield pltpu.make_async_remote_copy(
            src_ref=terms.at[peer],
            dst_ref=near_terms.at[slot],
            send_sem=sems.at[0, k],
            recv_sem=sems.at[1, slot],
            device_id={"dp": peer},
            device_id_type=pl.DeviceIdType.MESH,
        )
    yield pltpu.make_async_remote_copy(
        src_ref=terms.at[far, 2],
        dst_ref=last_terms,
        send_sem=sems.at[0, n - 2],
        recv_sem=sems.at[1, n - 2],
        device_id={"dp": far},
        device_id_type=pl.DeviceIdType.MESH,
    )


def near_arrive(near_terms, last_terms, sems):
    for k in range(near_terms.shape[0]):
        pltpu.make_async_copy(near_terms.at[k], near_terms.at[k], sems.at[1, k]).wait()
    pltpu.make_async_copy(last_terms, last_terms, sems.at[1, near_terms.shape[0]]).wait()


def peer_barrier(axes):
    barrier = pltpu.get_barrier_semaphore()
    count = 0
    for axis in axes:
        for peer in peers(axis):
            pl.semaphore_signal(
                barrier, inc=1, device_id={axis: peer}, device_id_type=pl.DeviceIdType.MESH
            )
            count += 1
    pl.semaphore_wait(barrier, count)


def wait_neighbours(sem, j, n):
    inside = (j > 0) & (j < n - 1)

    @pl.when(inside)
    def _():
        pl.semaphore_wait(sem, 2)

    @pl.when(jnp.logical_not(inside))
    def _():
        pl.semaphore_wait(sem, 1)


def line_barrier(j, n):
    barrier = pltpu.get_barrier_semaphore()
    for side in (-1, 1):

        @pl.when((j + side >= 0) & (j + side < n))
        def _():
            pl.semaphore_signal(
                barrier, inc=1, device_id={"head": j + side}, device_id_type=pl.DeviceIdType.MESH
            )

    wait_neighbours(barrier, j, n)


class Gather:
    def __init__(self, j, n, buf, send, recv):
        self.j, self.n, self.buf, self.send, self.recv = j, n, buf, send, recv
        self.span = buf.shape[1] // PARTS

    def copy(self, block, s, side, source=None):
        part = pl.ds(s * self.span, self.span)
        target = self.buf.at[block, part]
        return pltpu.make_async_remote_copy(
            src_ref=target if source is None else source.at[part],
            dst_ref=target,
            send_sem=self.send.at[(side + 1) // 2, block, s],
            recv_sem=self.recv.at[block, s],
            device_id={"head": self.j + side},
            device_id_type=pl.DeviceIdType.MESH,
        )

    def there(self, side):
        return (self.j + side >= 0) & (self.j + side < self.n)

    def flows(self, t):
        for side in (1, -1):
            block = self.j - side * t
            yield side, block, (block >= 0) & (block < self.n)

    def start(self, source, parts=range(PARTS)):
        for s in parts:
            for side in (1, -1):

                @pl.when(self.there(side))
                def _():
                    self.copy(self.j, s, side, source).start()

    def step(self, t, parts=range(PARTS)):
        for s in parts:
            for side, block, live in self.flows(t):

                @pl.when(live)
                def _():
                    self.copy(block, s, -side).wait_recv()

                @pl.when(live & self.there(side))
                def _():
                    self.copy(block, s, side).start()

    def finish(self):
        def drain(t):
            for s in range(PARTS):
                for side, block, live in self.flows(t):

                    @pl.when(live & self.there(side))
                    def _():
                        self.copy(block, s, side).wait_send()

        each(self.n, drain)


class Scatter:
    def __init__(self, j, n, own, held, send, recv):
        self.j, self.n, self.own, self.held, self.send, self.recv = j, n, own, held, send, recv
        self.span = own.shape[1] // PARTS
        self.compact = own.shape[0] != n

    def place(self, block, side):
        return block if not self.compact else (1 - side) // 2

    def last(self):
        return self.j if not self.compact else 2

    def rows(self, s):
        return pl.ds(s * self.span, self.span)

    def slot(self, block, side, at):
        return block if side == 1 else jnp.where(block == at, self.n, block)

    def arrival(self, slot, s):
        return pltpu.make_async_copy(
            self.held.at[slot, self.rows(s)], self.held.at[slot, self.rows(s)], self.recv.at[slot, s]
        )

    def flows(self, t):
        for side in (1, -1):
            lag = self.j if side == 1 else self.n - 1 - self.j
            block = self.n - 1 - (t - lag) if side == 1 else t - lag
            yield side, block, (t >= lag) & (t <= self.n - 2)

    def copy(self, source, block, s, side):
        slot = self.slot(block, side, self.j + side)
        return pltpu.make_async_remote_copy(
            src_ref=source.at[block, self.rows(s)],
            dst_ref=self.held.at[slot, self.rows(s)],
            send_sem=self.send.at[block, s],
            recv_sem=self.recv.at[slot, s],
            device_id={"head": self.j + side},
            device_id_type=pl.DeviceIdType.MESH,
        )

    def step(self, t, parts=range(PARTS)):
        for s in parts:
            for side, block, live in self.flows(t):
                behind = (self.j - side >= 0) & (self.j - side < self.n)

                @pl.when(live & jnp.logical_not(behind))
                def _():
                    if self.compact:
                        self.held[block, self.rows(s), :] = self.own[
                            self.place(block, side), self.rows(s), :
                        ]
                        self.copy(self.held, block, s, side).start()
                    else:
                        self.copy(self.own, block, s, side).start()

                @pl.when(live & behind)
                def _():
                    self.arrival(block, s).wait()
                    self.add(block, s, side)
                    self.copy(self.held, block, s, side).start()

    def add(self, block, s, side):
        def add_rows(i):
            rows = pl.ds(pl.multiple_of(s * self.span + i * STRIP, STRIP), STRIP)
            total = self.own[self.place(block, side), rows, :].astype(jnp.float32) + self.held[
                block, rows, :
            ].astype(jnp.float32)
            self.held[block, rows, :] = total.astype(jnp.bfloat16)

        each(self.span // STRIP, add_rows)

    def arrive(self):
        for s in range(PARTS):

            @pl.when(self.j > 0)
            def _():
                self.arrival(self.j, s).wait()

            @pl.when(self.j < self.n - 1)
            def _():
                self.arrival(self.n, s).wait()

    def result(self, rows):
        total = self.own[self.last(), rows, :].astype(jnp.float32)
        left = self.held[self.j, rows, :].astype(jnp.float32)
        right = self.held[self.n, rows, :].astype(jnp.float32)
        total = total + jnp.where(self.j > 0, left, 0.0)
        return total + jnp.where(self.j < self.n - 1, right, 0.0)

    def finish(self):
        def drain(t):
            for s in range(PARTS):
                for side, block, live in self.flows(t):

                    @pl.when(live)
                    def _():
                        self.copy(self.held, block, s, side).wait_send()

        each(self.n - 1, drain)


class Share:
    def __init__(self, axis, slots, send, recv):
        self.axis, self.slots, self.send, self.recv = axis, slots, send, recv
        self.me = lax.axis_index(axis)

    def copy(self, slot, peer, source=None):
        return pltpu.make_async_remote_copy(
            src_ref=self.slots.at[slot] if source is None else source,
            dst_ref=self.slots.at[slot],
            send_sem=self.send.at[peer],
            recv_sem=self.recv.at[slot],
            device_id={self.axis: peer},
            device_id_type=pl.DeviceIdType.MESH,
        )

    def start(self, sources=None):
        for peer in peers(self.axis):
            source = None if sources is None else sources.at[peer]
            self.copy(self.me, peer, source).start()

    def arrive(self):
        for peer in peers(self.axis):
            self.copy(peer, peer).wait_recv()

    def finish(self):
        for peer in peers(self.axis):
            self.copy(self.me, peer).wait_send()


def share_sems(axis):
    n = lax.axis_size(axis)
    return [pltpu.SemaphoreType.DMA((n,)), pltpu.SemaphoreType.DMA((n,))]


class Sum:
    def __init__(self, terms, slots, total, sems):
        self.terms, self.slots, self.total = terms, slots, total
        self.parts = Share("dp", slots, sems[0], sems[1])
        self.whole = Share("dp", total, sems[2], sems[3])
        self.me, self.sem = self.parts.me, sems[4]

    def start(self):
        self.parts.start(self.terms)

    def keep(self):
        return pltpu.make_async_copy(self.slots.at[self.me], self.total.at[self.me], self.sem)

    def spread(self):
        self.parts.arrive()
        rows = self.slots.shape[1]

        def add(part):
            value = jnp.zeros((STRIP, self.slots.shape[2]), jnp.float32)
            for i in range(self.slots.shape[0]):
                mine = self.terms[i, part, :].astype(jnp.float32)
                other = self.slots[i, part, :].astype(jnp.float32)
                value = value + jnp.where(self.me == i, mine, other)
            self.slots[self.me, part, :] = value.astype(jnp.bfloat16)

        strips(rows, add)
        for peer in peers("dp"):
            self.whole.copy(self.me, peer, self.slots.at[self.me]).start()
        self.keep().start()

    def finish(self):
        self.whole.arrive()
        self.keep().wait()
        self.parts.finish()
        self.whole.finish()


def sum_sems():
    return [*share_sems("dp"), *share_sems("dp"), pltpu.SemaphoreType.DMA]


def gather_sems(n):
    return [pltpu.SemaphoreType.DMA((2, n, PARTS)), pltpu.SemaphoreType.DMA((n, PARTS))]


def scatter_sems(n):
    return [pltpu.SemaphoreType.DMA((n, PARTS)), pltpu.SemaphoreType.DMA((n + 1, PARTS))]


def line_call(kernel, ident, name, out_shape, in_specs, out_specs, scratch, cost=None):
    return pl.pallas_call(
        kernel,
        out_shape=out_shape,
        in_specs=in_specs,
        out_specs=out_specs,
        scratch_shapes=scratch,
        compiler_params=pltpu.CompilerParams(
            collective_id=ident, has_side_effects=True, vmem_limit_bytes=VMEM_BYTES
        ),
        name=name,
    )


STRIP = 16


def strips(rows, body):
    each(rows // STRIP, lambda i: body(pl.ds(pl.multiple_of(i * STRIP, STRIP), STRIP)))


def front_kernel(
    lengths, stream, premix, wb, wi, wo_in, wg, par, preffn, cot,
    rows_out, pre_out, saved, gated_out, wbi_out, wo_out, cot_rows, hidden, low_out,
    normed, rows, wbi, wo, pre, gated, stage, z, carry, own, held,
    gsend, grecv, csend, crecv, send, recv, keep_sem, pre_sem, stage_sem, one_sem,
):
    j, n = line_place()
    f32, bf16 = jnp.float32, jnp.bfloat16
    local, depth = stream.shape
    width, chans = gated.shape[1], wb.shape[0]
    tiles = width // LANES
    line_barrier(j, n)

    def norm(part):
        _, unit = rms_parts(stream[part, :].astype(f32))
        normed[part, :] = (unit * premix[...]).astype(bf16)

    strips(local, norm)
    gather = Gather(j, n, rows, gsend, grecv)
    gather.start(normed)
    for target, first, source in ((wbi, 0, wb), (wbi, width, wi), (wo, 0, wo_in)):
        whole = chans // STRIP * STRIP
        target[first + whole : first + width, :] = jnp.zeros((width - whole, depth), bf16)
        target[first : first + chans, :] = source[...]
    out_copies = [
        pltpu.make_async_copy(wbi, wbi_out, one_sem.at[0]),
        pltpu.make_async_copy(wo, wo_out, one_sem.at[1]),
    ]
    for copy in out_copies:
        copy.start()

    def span(block):
        return pl.ds(pl.multiple_of(block * local, local), local)

    def shifted(block):
        return pl.ds(pl.multiple_of(block * local + HALO, HALO), local)

    def keep(source, block):
        return pltpu.make_async_copy(source, rows_out.at[block], keep_sem.at[block])

    def keep_pre(block):
        return pltpu.make_async_copy(
            pre.at[shifted(block)], pre_out.at[span(block)], pre_sem.at[block]
        )

    pre[0:HALO, :] = jnp.zeros((HALO, 2 * width), f32)
    keep(normed, j).start()
    pre[shifted(j), :] = contract_cols(normed[...], wbi[...])
    keep_pre(j).start()

    def visit(v):
        t = v // 2 + 1
        block = jnp.where(v % 2 == 0, j - t, j + t)

        @pl.when(v % 2 == 0)
        def _():
            gather.step(t)

        @pl.when((block >= 0) & (block < n))
        def _():
            keep(rows.at[block], block).start()
            pre[shifted(block), :] = contract_cols(rows[block], wbi[...])
            keep_pre(block).start()

    each(2 * (n - 1), visit)
    cots = Gather(j, n, cot_rows, csend, crecv)
    cots.start(cot)
    mine = pltpu.make_async_copy(cot, cot_rows.at[j], one_sem.at[2])
    mine.start()

    carry[...] = jnp.zeros_like(carry)
    count = n * local // CHUNK

    def keep_stage(i):
        return pltpu.make_async_copy(
            stage.at[lax.rem(i, 2)],
            saved.at[pl.ds(pl.multiple_of(i * CHUNK, CHUNK), CHUNK)],
            stage_sem.at[lax.rem(i, 2)],
        )

    def chunk(i):
        first = i * CHUNK

        @pl.when(i >= 2)
        def _():
            keep_stage(i - 2).wait()

        u_out, r_out, e_out, h_out = (
            stage.at[lax.rem(i, 2), :, k * width : (k + 1) * width] for k in range(SAVED)
        )

        def conv_step(b):
            row = pl.multiple_of(b * BLOCK, BLOCK)
            halo = pl.ds(pl.multiple_of(first + row, BLOCK), BLOCK + HALO)
            place = doc_places(lengths, first + row, BLOCK)
            for t in range(tiles):
                cols = pl.ds(t * LANES, LANES)
                xs = pre[halo, pl.ds(width + t * LANES, LANES)]
                total = par[BIAS : BIAS + 1, cols] + par[TAP : TAP + 1, cols] * xs[HALO:]
                for k in range(1, CONVW):
                    term = par[TAP + k : TAP + k + 1, cols] * xs[HALO - k : HALO - k + BLOCK]
                    total = total + jnp.where(place >= k, term, 0.0)
                u_out[pl.ds(row, BLOCK), cols] = total

        each(CHUNK // BLOCK, conv_step)
        z[...] = jnp.dot(u_out[...].astype(bf16), wg[...], preferred_element_type=f32)

        def scan_step(b):
            row = pl.multiple_of(b * BLOCK, BLOCK)
            part = pl.ds(row, BLOCK)
            spot = pl.ds(pl.multiple_of(first + row, BLOCK), BLOCK)
            here = pl.ds(pl.multiple_of(first + row + HALO, HALO), BLOCK)
            fresh = doc_places(lengths, first + row, BLOCK) == 0
            inner = lax.broadcasted_iota(jnp.int32, (BLOCK, LANES), 0) % 8
            for t in range(tiles):
                cols = pl.ds(t * LANES, LANES)
                other = pl.ds(width + t * LANES, LANES)
                r = jax.nn.sigmoid(z[part, cols] + par[RATE_B : RATE_B + 1, cols])
                e = jax.nn.sigmoid(z[part, other] + par[ENTRY_B : ENTRY_B + 1, cols])
                u = u_out[part, cols]
                c, m, _ = decay_terms(r, par[DECAY : DECAY + 1, cols], fresh)
                r_out[part, cols] = r
                e_out[part, cols] = e
                b_ = m * e * u
                for d in (1, 2, 4):
                    near = inner >= d
                    b_ = b_ + c * jnp.where(near, pltpu.roll(b_, d, 0), 0.0)
                    c = c * jnp.where(near, pltpu.roll(c, d, 0), 1.0)
                last = carry[0:1, cols]
                pieces = []
                for g in range(BLOCK // 8):
                    eight = slice(g * 8, g * 8 + 8)
                    state = b_[eight] + c[eight] * last
                    last = state[7:8]
                    pieces.append(state)
                carry[0:1, cols] = last
                h = jnp.concatenate(pieces, axis=0)
                h_out[part, cols] = h
                gated[spot, cols] = (h * gelu(pre[here, cols])).astype(bf16)

        each(CHUNK // BLOCK, scan_step)
        keep_stage(i).start()

        @pl.when(i == count * 5 // 8)
        def _():
            cots.step(1)

    each(count, chunk)
    keep_gated = pltpu.make_async_copy(gated, gated_out, one_sem.at[3])
    keep_gated.start()

    scatter = Scatter(j, n, own, held, send, recv)

    def compute(block, slot):
        own[slot] = jnp.dot(
            gated[span(block), :], wo[...], preferred_element_type=f32
        ).astype(bf16)

    def ahead(t):
        for side, block, live in scatter.flows(t):
            pl.when(live)(functools.partial(compute, block, scatter.place(block, side)))

    ahead(0)

    def step(t):
        scatter.step(t)
        ahead(t + 1)

        @pl.when(t == 0)
        def _():
            compute(j, 2)

        @pl.when(t + 2 < n)
        def _():
            cots.step(t + 2)

    each(n - 1, step)
    scatter.arrive()

    def settle(part):
        total = stream[part, :].astype(f32) + scatter.result(part)
        hidden[part, :] = total
        _, unit = rms_parts(total)
        low_out[part, :] = (unit * preffn[...]).astype(bf16)

    strips(local, settle)
    scatter.finish()
    gather.finish()
    cots.finish()
    mine.wait()
    keep_gated.wait()
    for copy in out_copies:
        copy.wait()
    keep(normed, j).wait()
    keep_pre(j).wait()
    for k in range(1, n):
        other = lax.rem(j + k, n)
        keep(rows.at[other], other).wait()
        keep_pre(other).wait()
    for i in range(max(count - 2, 0), count):
        keep_stage(i).wait()


def mixer_front(lengths, stream, premix, wb, wi, wo, wg, par, preffn, cot):
    n = lax.axis_size("head")
    local, depth = stream.shape
    width, tokens = wg.shape[0], n * local
    f32, bf16 = jnp.float32, jnp.bfloat16
    shape, vmem, dma = jax.ShapeDtypeStruct, pltpu.VMEM, pltpu.SemaphoreType.DMA
    return line_call(
        front_kernel, 0, "mixer_front",
        (
            shape((n, local, depth), bf16),
            shape((tokens, 2 * width), f32),
            shape((tokens, SAVED * width), f32),
            shape((tokens, width), bf16),
            shape((2 * width, depth), bf16),
            shape((width, depth), bf16),
            shape((n, local, depth), bf16),
            shape((local, depth), f32),
            shape((local, depth), bf16),
        ),
        [IN_SMEM] + [IN_VMEM] * 9,
        [IN_ANY] * 7 + [IN_VMEM] * 2,
        [
            vmem((local, depth), bf16),
            vmem((n, local, depth), bf16),
            vmem((2 * width, depth), bf16),
            vmem((width, depth), bf16),
            vmem((HALO + tokens, 2 * width), f32),
            vmem((tokens, width), bf16),
            vmem((2, CHUNK, SAVED * width), f32),
            vmem((CHUNK, 2 * width), f32),
            vmem((8, width), f32),
            vmem((3, local, depth), bf16),
            vmem((n + 1, local, depth), bf16),
            *gather_sems(n),
            *gather_sems(n),
            *scatter_sems(n),
            dma((n,)),
            dma((n,)),
            dma((2,)),
            dma((4,)),
        ],
    )(lengths, stream, premix, wb, wi, wo, wg, par, preffn, cot)


def ffn_kernel(
    low, cot_rows, cot, hidden, gain, wg, wu, wd,
    out_part, terms, far_terms, resid, resid_low, gain_grad,
    rows, cot_pair, kept, own, held, stage, wstage, cot_cols,
    gsend, grecv, send, recv, cot_sem, out_sem, col_sem, term_sem, far_sem,
):
    j, n = line_place()
    peer_barrier(("head", "dp"))
    f32, bf16 = jnp.float32, jnp.bfloat16
    local, depth = low.shape
    units = wg.shape[1]
    half = local // PARTS
    fstep = 256 if units % 256 == 0 else LANES
    dstep = 512
    gather = Gather(j, n, rows, gsend, grecv)
    scatter = Scatter(j, n, own, held, send, recv)
    gather.start(low, [0])
    rows[j] = low[...]

    def pair(chip, q):
        return pl.ds(pl.multiple_of(2 * chip, 2), 2), pl.ds(q * half, half)

    def fetch(chip, q):
        return pltpu.make_async_copy(cot_rows.at[pair(chip, q)], cot_pair, cot_sem)

    def put(chip, q):
        return pltpu.make_async_copy(stage, out_part.at[pair(chip, q)], out_sem)

    def pair_work(chip, q):
        spot = pair(chip, q)

        def flat(v):
            return v.reshape(2 * half, v.shape[-1])

        def fold(v):
            return v.astype(bf16).reshape(2, half, v.shape[-1])

        for f in range(0, units, fstep):
            cols = slice(f, f + fstep)
            gate = jnp.dot(flat(rows[spot]), wg[:, cols], preferred_element_type=f32)
            act, slope = gelu_pair(gate)
            up = jnp.dot(flat(rows[spot]), wu[:, cols], preferred_element_type=f32)
            kept[2, *spot, cols] = fold(act * up)
            grad = jnp.dot(flat(cot_pair[...]), wd[:, cols], preferred_element_type=f32)
            kept[0, *spot, cols] = fold(grad * up * slope)
            kept[1, *spot, cols] = fold(grad * act)
        for d in range(0, depth, dstep):
            cols = slice(d, d + dstep)
            own[*spot, cols] = fold(
                contract_cols(flat(kept[0, *spot]), wg[cols, :])
                + contract_cols(flat(kept[1, *spot]), wu[cols, :])
            )
            stage[:, :, cols] = fold(contract_cols(flat(kept[2, *spot]), wd[cols, :]))

    def gather_half(q):
        def visit(i):
            t = i + 1
            reach = t // 2
            chip = j // 2 + jnp.where((t + j) % 2 == 0, -reach, reach)
            live = (chip >= 0) & (chip < n // 2)

            @pl.when(live)
            def _():
                fetch(chip, q).start()

            gather.step(t, [q])
            if q:
                scatter.step(t - 1, [0])

            @pl.when(live)
            def _():
                fetch(chip, q).wait()

                @pl.when((t > 1) | (q > 0))
                def _():
                    put(chip, q).wait()

                pair_work(chip, q)
                put(chip, q).start()

        each(n - 1, visit)

    gather_half(0)
    gather.start(low, [1])
    gather_half(1)
    put(j // 2, 1).wait()

    width = depth // n
    per = depth // terms.shape[0] // width

    far = far_peer("dp")

    def columns(b):
        return pl.ds(pl.multiple_of(lax.rem(b + far * per, n) * width, width), width)

    def take(b):
        return pltpu.make_async_copy(cot_rows.at[:, :, columns(b)], cot_cols, col_sem)

    def give(b):
        owner = lax.rem(b // per + far, n // per)
        spot = pl.ds(pl.multiple_of(lax.rem(b, per) * width, width), width)
        return pltpu.make_async_copy(wstage, terms.at[owner, :, spot, :], term_sem)

    def weights(b):
        xs = rows[:, :, columns(b)].reshape(n * local, width)
        take(b).wait()

        @pl.when(b > 0)
        def _():
            give(b).wait()

        @pl.when(b == per)
        def _():
            for copy in far_copies(terms, far_terms, far_sem):
                copy.start()

        for k, lead in ((0, xs), (1, xs), (2, cot_cols[...].reshape(n * local, width))):
            wstage[k] = contract_rows(lead, kept[k].reshape(n * local, units)).astype(bf16)
        give(b).start()

        @pl.when(b + 1 < n)
        def _():
            take(b + 1).start()

    take(0).start()

    def step(t):
        pl.when(t < n - 1)(lambda: scatter.step(t, [1]))
        weights(t)

    each(n, step)
    scatter.arrive()
    gain_grad[...] = jnp.zeros_like(gain_grad)

    def settle(part):
        rinv, u = rms_parts(hidden[part, :])
        grad = scatter.result(part)
        gain_grad[...] += jnp.sum(grad * u, axis=0, keepdims=True)
        total = cot[part, :].astype(f32) + norm_back(u, rinv, gain[...], grad)
        resid[part, :] = total
        resid_low[part, :] = total.astype(bf16)

    strips(local, settle)
    give(0).wait()
    gather.finish()
    scatter.finish()
    for copy in far_copies(terms, far_terms, far_sem):
        copy.wait()


def feed_forward(low, cot_rows, cot, hidden, gain, wg, wu, wd):
    n, group = lax.axis_size("head"), lax.axis_size("dp")
    local, depth = low.shape
    units = wg.shape[1]
    bf16 = jnp.bfloat16
    shape, vmem = jax.ShapeDtypeStruct, pltpu.VMEM
    pair = (2, local // PARTS, depth)
    return line_call(
        ffn_kernel, 2, "feed_forward",
        (
            shape((n, local, depth), bf16),
            shape((group, 3, depth // group, units), bf16),
            shape((FAR_TERMS, depth // group, units), bf16),
            shape((local, depth), jnp.float32),
            shape((local, depth), bf16),
            shape((1, depth), jnp.float32),
        ),
        [IN_VMEM, IN_ANY] + [IN_VMEM] * 6,
        [IN_ANY, IN_ANY, IN_ANY, IN_VMEM, IN_VMEM, IN_VMEM],
        [
            vmem((n, local, depth), bf16),
            vmem(pair, bf16),
            vmem((3, n, local, units), bf16),
            vmem((n, local, depth), bf16),
            vmem((n + 1, local, depth), bf16),
            vmem(pair, bf16),
            vmem((3, depth // n, units), bf16),
            vmem((n, local, depth // n), bf16),
            *gather_sems(n),
            *scatter_sems(n),
            *[pltpu.SemaphoreType.DMA] * 4,
            pltpu.SemaphoreType.DMA((2, FAR_TERMS)),
        ],
    )(low, cot_rows, cot, hidden, gain, wg, wu, wd)


def back_kernel(
    lengths, low, out_part, hidden, terms, gated, wo, wbi, wg, par, pre, saved,
    normed_rows, stream, gain, resid, preffn_grad,
    layer_out, sums, last_terms, stream_grad, ob_total, i_total, g_total, par_grad, gains,
    rows, own, held, dh, dpre, acc, dgate, dz, du, carry, dpar, wide,
    unit_bp, unit_h, unit_gated, unit_normed,
    obterms, obslots, iterms, islots, gterms, gslots, pslots, dslots, hslots,
    gsend, grecv, send4, recv4, send8, recv8, tsems, unit_sem, own_sem, chunk_sem,
    row_sem, wide_sem, free, psend, precv, dsend, drecv, hsend, hrecv, *sems,
):
    j, n = line_place()
    f32, bf16 = jnp.float32, jnp.bfloat16
    local, depth = stream.shape
    width = dh.shape[1]
    tiles = width // LANES
    peer_barrier(("head", "dp"))
    gather = Gather(j, n, rows, gsend, grecv)
    gather.start(low)
    for copy in near_copies(terms, sums, last_terms, tsems):
        copy.start()
    rows[j] = low[...]
    outs = Scatter(j, n, own, held, send4, recv4)
    acc[...] = jnp.zeros_like(acc)

    def fetch_out(block, slot):
        return pltpu.make_async_copy(out_part.at[block], own.at[slot], own_sem.at[slot])

    def outs_ahead(t):
        for start in (True, False):
            for side, block, live in outs.flows(t):
                copy = fetch_out(block, outs.place(block, side))
                pl.when(live)(copy.start if start else copy.wait)

    def outs_step(t):
        @pl.when((t >= 0) & (t < n - 1))
        def _():
            outs.step(t)
            outs_ahead(t + 1)

    outs_ahead(0)
    fetch_out(j, 2).start()
    fetch_out(j, 2).wait()

    def unit_copies(block):
        span = pl.ds(pl.multiple_of(block * local, local), local)
        return (
            pltpu.make_async_copy(pre.at[span, 0:width], unit_bp, unit_sem.at[0]),
            pltpu.make_async_copy(
                saved.at[span, 3 * width : 4 * width], unit_h, unit_sem.at[1]
            ),
            pltpu.make_async_copy(gated.at[span], unit_gated, unit_sem.at[2]),
            pltpu.make_async_copy(normed_rows.at[block], unit_normed, unit_sem.at[3]),
        )

    def unit(block):
        span = pl.ds(pl.multiple_of(block * local, local), local)
        dh[span, :] = contract_cols(rows[block], wo[...])

        def act(i):
            part = pl.ds(pl.multiple_of(i * BLOCK, BLOCK), BLOCK)
            spot = pl.ds(pl.multiple_of(block * local + i * BLOCK, BLOCK), BLOCK)
            for t in range(tiles):
                cols = pl.ds(t * LANES, LANES)
                grad = dh[spot, cols]
                value, slope = gelu_pair(unit_bp[part, cols])
                dpre[spot, cols] = (grad * unit_h[part, cols] * slope).astype(bf16)
                dh[spot, cols] = grad * value

        each(local // BLOCK, act)
        acc[0:width, :] += contract_rows(unit_gated[...], rows[block])
        acc[width : 2 * width, :] += contract_rows(dpre[span, 0:width], unit_normed[...])

    def visit(v):
        t = (v + 1) // 2
        block = jnp.where(v % 2 == 1, j - t, j + t)
        live = (block >= 0) & (block < n)

        @pl.when(live)
        def _():
            for copy in unit_copies(block):
                copy.start()

        @pl.when(v % 2 == 1)
        def _():
            gather.step(t)
            outs_step(t - 1 - LAG)

        @pl.when(live)
        def _():
            for copy in unit_copies(block):
                copy.wait()
            unit(block)

    each(2 * n - 1, visit)
    gather.finish()

    def pack(target, source, count):
        span = target.shape[1]

        def strip(i):
            row = pl.multiple_of(i * STRIP, STRIP)
            target[row // span, pl.ds(pl.multiple_of(lax.rem(row, span), STRIP), STRIP), :] = source[
                pl.ds(row, STRIP), :
            ].astype(bf16)

        each(count // STRIP, strip)

    obsum = Sum(obterms, obslots, ob_total, sems[0:5])
    isum = Sum(iterms, islots, i_total, sems[5:10])
    gsum = Sum(gterms, gslots, g_total, sems[10:15])
    pack(obterms, acc, 2 * width)
    obsum.start()
    load = pltpu.make_async_copy(normed_rows, rows, row_sem)
    load.start()
    load_hidden = pltpu.make_async_copy(hidden, wide, wide_sem.at[0])
    load_hidden.start()

    count = n * local // CHUNK

    def chunk_copies(i):
        base = lax.rem(i, 2) * (CHUNK + HALO)
        start = pl.multiple_of(i * CHUNK, CHUNK)
        ahead = pl.multiple_of(jnp.maximum(start - HALO, 0), HALO)
        halo, main = pl.ds(pl.multiple_of(base, HALO), HALO), pl.ds(
            pl.multiple_of(base + HALO, HALO), CHUNK
        )
        kept, x = slice(0, SAVED * width), slice(SAVED * width, (SAVED + 1) * width)
        pairs = (
            (saved.at[pl.ds(ahead, HALO)], acc.at[halo, kept]),
            (saved.at[pl.ds(start, CHUNK)], acc.at[main, kept]),
            (pre.at[pl.ds(ahead, HALO), width : 2 * width], acc.at[halo, x]),
            (pre.at[pl.ds(start, CHUNK), width : 2 * width], acc.at[main, x]),
        )
        return [
            pltpu.make_async_copy(a, b, chunk_sem.at[lax.rem(i, 2), k])
            for k, (a, b) in enumerate(pairs)
        ]

    def total(v):
        return jnp.sum(v, axis=0, keepdims=True)

    for copy in chunk_copies(count - 1):
        copy.start()
    du[...] = jnp.zeros_like(du)
    carry[...] = jnp.zeros_like(carry)
    dgate[...] = jnp.zeros_like(dgate)
    dpar[...] = jnp.zeros_like(dpar)

    def chunk(k):
        i = count - 1 - k

        @pl.when(i > 0)
        def _():
            for copy in chunk_copies(i - 1):
                copy.start()

        for copy in chunk_copies(i):
            copy.wait()
        base = lax.rem(i, 2) * (CHUNK + HALO)
        first = i * CHUNK
        du[CHUNK:, :] = du[0:HALO, :]

        def scan_step(b):
            row = pl.multiple_of(CHUNK - BLOCK - b * BLOCK, BLOCK)
            part = pl.ds(row, BLOCK)
            spot = pl.ds(pl.multiple_of(first + row, BLOCK), BLOCK)
            here = pl.ds(pl.multiple_of(base + HALO + row, HALO), BLOCK)
            halo = pl.ds(pl.multiple_of(base + row, HALO), BLOCK + HALO)
            fresh = doc_places(lengths, first + row, BLOCK) == 0
            place = lax.broadcasted_iota(jnp.int32, (BLOCK, LANES), 0)
            inner = place % 8
            for t in range(tiles):
                cols = pl.ds(t * LANES, LANES)
                u, r, e = (acc[here, pl.ds(m * width + t * LANES, LANES)] for m in range(3))
                prior = acc[halo, pl.ds(3 * width + t * LANES, LANES)][HALO - 1 : HALO - 1 + BLOCK]
                near_h = dh[spot, cols]
                decay = par[DECAY : DECAY + 1, cols]
                c, m, ratio = decay_terms(r, decay, fresh)
                b_, a_ = c * near_h, c
                for d in (1, 2, 4):
                    near_row = inner < 8 - d
                    b_ = b_ + a_ * jnp.where(near_row, pltpu.roll(b_, BLOCK - d, 0), 0.0)
                    a_ = a_ * jnp.where(near_row, pltpu.roll(a_, BLOCK - d, 0), 1.0)
                later = carry[0:1, cols]
                pieces = []
                front = later
                for g in reversed(range(BLOCK // 8)):
                    eight = slice(g * 8, g * 8 + 8)
                    state = b_[eight] + a_[eight] * front
                    front = state[0:1]
                    pieces.append(state)
                carry[0:1, cols] = front
                mu = jnp.concatenate(pieces[::-1], axis=0)
                adj = near_h + jnp.where(
                    place == BLOCK - 1, later, pltpu.roll(mu, BLOCK - 1, 0)
                )
                eu = e * u
                dlog = adj * (prior * c - eu * ratio)
                dpar[G_DECAY : G_DECAY + 1, cols] += total(dlog * r)
                dzr = decay * dlog * (r * (1.0 - r))
                dze = adj * m * eu * (1.0 - e)
                dpar[G_RATE : G_RATE + 1, cols] += total(dzr)
                dpar[G_ENTRY : G_ENTRY + 1, cols] += total(dze)
                dz[part, cols] = dzr.astype(bf16)
                dz[part, pl.ds(width + t * LANES, LANES)] = dze.astype(bf16)
                du[part, cols] = adj * m * e

        each(CHUNK // BLOCK, scan_step)
        u_chunk = acc[pl.ds(pl.multiple_of(base + HALO, HALO), CHUNK), 0:width]
        du[0:CHUNK, :] += contract_cols(dz[...], wg[...])
        dgate[...] += contract_rows(u_chunk.astype(bf16), dz[...])

        def conv_step(b):
            row = pl.multiple_of(b * BLOCK, BLOCK)
            spot = pl.ds(pl.multiple_of(first + row, BLOCK), BLOCK)
            halo = pl.ds(pl.multiple_of(base + row, HALO), BLOCK + HALO)
            place = doc_places(lengths, first + row, BLOCK + HALO)
            for t in range(tiles):
                cols = pl.ds(t * LANES, LANES)
                ds = du[pl.ds(row, BLOCK + HALO), cols]
                xs = acc[halo, pl.ds(SAVED * width + t * LANES, LANES)]
                mine = ds[0:BLOCK]
                dx = par[TAP : TAP + 1, cols] * mine
                dpar[G_BIAS : G_BIAS + 1, cols] += total(mine)
                dpar[G_TAP : G_TAP + 1, cols] += total(mine * xs[HALO:])
                for k in range(1, CONVW):
                    inside = jnp.where(place >= k, ds, 0.0)
                    dx = dx + par[TAP + k : TAP + k + 1, cols] * inside[k : k + BLOCK]
                    dpar[G_TAP + k : G_TAP + k + 1, cols] += total(
                        inside[0:BLOCK] * xs[HALO - k : HALO - k + BLOCK]
                    )
                dpre[spot, pl.ds(width + t * LANES, LANES)] = dx.astype(bf16)

        each(CHUNK // BLOCK, conv_step)
        if LAG:
            late = n - 1 - LAG

            @pl.when((k % 2 == 1) & (k // 2 < LAG))
            def _():
                outs_step(late + k // 2)

    each(count, chunk)

    pack(gterms, dgate, width)
    gsum.start()
    pshare = Share("dp", pslots, psend, precv)
    pslots[pshare.me] = dpar[...]
    pshare.start()
    outs.arrive()
    load_hidden.wait()

    def settle_out(part):
        layer_out[part, :] = (wide[part, :] + outs.result(part)).astype(bf16)

    strips(local, settle_out)
    outs.finish()
    load_resid = pltpu.make_async_copy(resid, wide, wide_sem.at[1])
    load_resid.start()
    for side in (-1, 1):

        @pl.when((j + side >= 0) & (j + side < n))
        def _():
            pl.semaphore_signal(
                free, inc=1, device_id={"head": j + side}, device_id_type=pl.DeviceIdType.MESH
            )

    scatter = Scatter(j, n, own, held, send8, recv8)

    def compute(block, slot):
        span = pl.ds(pl.multiple_of(block * local, local), local)
        own[slot] = jnp.dot(dpre[span, :], wbi[...], preferred_element_type=f32).astype(bf16)

    def ahead(t):
        for side, block, live in scatter.flows(t):
            pl.when(live)(functools.partial(compute, block, scatter.place(block, side)))

    ahead(0)
    wait_neighbours(free, j, n)
    scatter.step(0)
    ahead(1)
    load.wait()
    for c in range(0, width, LANES):
        acc[c : c + LANES, :] = contract_rows(
            dpre[:, width + c : width + c + LANES], rows[...].reshape(n * local, depth)
        )
    pack(iterms, acc, width)
    isum.start()
    compute(j, 2)
    obsum.spread()

    def step(t):
        scatter.step(t)
        ahead(t + 1)

        @pl.when(t == n // 2)
        def _():
            gsum.spread()
            isum.spread()

    lax.fori_loop(1, n - 1, lambda t, _: (step(t), 0)[1], 0)
    scatter.arrive()
    load_resid.wait()
    gains[...] = jnp.zeros_like(gains)

    def settle(part):
        rinv, u = rms_parts(stream[part, :].astype(f32))
        grad = scatter.result(part)
        gains[0:1, :] += jnp.sum(grad * u, axis=0, keepdims=True)
        value = wide[part, :] + norm_back(u, rinv, gain[...], grad)
        stream_grad[part, :] = value.astype(bf16)

    strips(local, settle)

    gains[1:2, :] = preffn_grad[...]
    for axis, slots, ssem, rsem in (("dp", dslots, dsend, drecv), ("head", hslots, hsend, hrecv)):
        share = Share(axis, slots, ssem, rsem)
        slots[share.me] = gains[...]
        share.start()
        share.arrive()
        value = slots[0]
        for i in range(1, slots.shape[0]):
            value = value + slots[i]
        gains[...] = value
        share.finish()

    pshare.arrive()
    value = pslots[0]
    for i in range(1, pslots.shape[0]):
        value = value + pslots[i]
    par_grad[...] = value
    pshare.finish()
    for one in (gsum, obsum, isum):
        one.finish()
    scatter.finish()
    for copy in near_copies(terms, sums, last_terms, tsems):
        copy.wait_send()
    near_arrive(sums, last_terms, tsems)


def mixer_back(
    lengths, low, out_part, hidden, terms, gated, wo, wbi, wg, par, pre, saved,
    normed_rows, stream, gain, resid, preffn_grad,
):
    n, group = lax.axis_size("head"), lax.axis_size("dp")
    local, depth = stream.shape
    width, tokens = wo.shape[0], pre.shape[0]
    f32, bf16 = jnp.float32, jnp.bfloat16
    ob = (group, 2 * width // group, depth)
    one = (group, width // group, depth)
    gate = (group, width // group, 2 * width)
    dma = pltpu.SemaphoreType.DMA
    shape = jax.ShapeDtypeStruct
    return line_call(
        back_kernel, 3, "mixer_back",
        (
            shape((local, depth), bf16),
            shape((group - 2, *terms.shape[1:]), bf16),
            shape(terms.shape[2:], bf16),
            shape((local, depth), bf16),
            shape(ob, bf16),
            shape(one, bf16),
            shape(gate, bf16),
            shape((PARAMS, width), f32),
            shape((8, depth), f32),
        ),
        [
            IN_SMEM, IN_VMEM, IN_ANY, IN_ANY, IN_ANY, IN_ANY, *[IN_VMEM] * 4, IN_ANY, IN_ANY,
            IN_ANY, IN_VMEM, IN_VMEM, IN_ANY, IN_VMEM,
        ],
        [IN_VMEM, IN_ANY, IN_ANY, IN_VMEM, IN_ANY, IN_ANY, IN_ANY, IN_VMEM, IN_VMEM],
        [
            pltpu.VMEM((n, local, depth), bf16),
            pltpu.VMEM((3, local, depth), bf16),
            pltpu.VMEM((n + 1, local, depth), bf16),
            pltpu.VMEM((tokens, width), f32),
            pltpu.VMEM((tokens, 2 * width), bf16),
            pltpu.VMEM((max(2 * width, 2 * (CHUNK + HALO)), depth), f32),
            pltpu.VMEM((width, 2 * width), f32),
            pltpu.VMEM((CHUNK, 2 * width), bf16),
            pltpu.VMEM((CHUNK + HALO, width), f32),
            pltpu.VMEM((8, width), f32),
            pltpu.VMEM((PARAMS, width), f32),
            pltpu.VMEM((local, depth), f32),
            pltpu.VMEM((local, width), f32),
            pltpu.VMEM((local, width), f32),
            pltpu.VMEM((local, width), bf16),
            pltpu.VMEM((local, depth), bf16),
            pltpu.VMEM(ob, bf16),
            pltpu.VMEM(ob, bf16),
            pltpu.VMEM(one, bf16),
            pltpu.VMEM(one, bf16),
            pltpu.VMEM(gate, bf16),
            pltpu.VMEM(gate, bf16),
            pltpu.VMEM((group, PARAMS, width), f32),
            pltpu.VMEM((group, 8, depth), f32),
            pltpu.VMEM((n, 8, depth), f32),
            *gather_sems(n),
            *scatter_sems(n),
            *scatter_sems(n),
            dma((2, group)),
            dma((4,)),
            dma((3,)),
            dma((2, 4)),
            dma,
            dma((2,)),
            pltpu.SemaphoreType.REGULAR,
            *share_sems("dp"),
            *share_sems("dp"),
            *share_sems("head"),
            *sum_sems(),
            *sum_sems(),
            *sum_sems(),
        ],
    )(
        lengths, low, out_part, hidden, terms, gated, wo, wbi, wg, par, pre, saved,
        normed_rows, stream, gain, resid, preffn_grad,
    )


def block_diagonal(weights, width):
    heads, size = weights.shape[0], weights.shape[1]
    placed = [
        jnp.pad(weights[i], ((i * size, width - (i + 1) * size),) * 2) for i in range(heads)
    ]
    return functools.reduce(jnp.add, placed)


def diagonal_blocks(dense, heads, size):
    blocks = [dense[i * size : (i + 1) * size, i * size : (i + 1) * size] for i in range(heads)]
    return jnp.stack(blocks, axis=1).transpose(1, 0, 2)


def shards(
    stream, doc_lengths, premix_gain, branch_weight, input_weight, conv_kernel, conv_bias,
    rate_weight, rate_bias, entry_weight, entry_bias, decay_param, output_weight, preffn_gain,
    ffn_gate, ffn_upward, ffn_down, cotangent,
):
    f32, bf16 = jnp.float32, jnp.bfloat16
    heads, size = rate_bias.shape
    chans = branch_weight.shape[1]
    width = -(-chans // LANES) * LANES

    slope = -DECAY_SCALE * jax.nn.softplus(decay_param.astype(f32))
    par = jnp.concatenate(
        [
            conv_bias[None].astype(f32),
            conv_kernel.astype(f32),
            rate_bias.reshape(1, -1).astype(f32),
            entry_bias.reshape(1, -1).astype(f32),
            slope[None],
        ]
    )
    par = jnp.pad(par, ((0, 0), (0, width - chans)), constant_values=-1.0)
    par = jnp.where((jnp.arange(width)[None] < chans) | (jnp.arange(PARAMS)[:, None] == DECAY), par, 0.0)
    wg = jnp.concatenate(
        [block_diagonal(rate_weight, width), block_diagonal(entry_weight, width)], axis=1
    )

    premix = premix_gain.astype(f32)[None]
    preffn = preffn_gain.astype(f32)[None]
    normed_rows, pre, saved, gated, wbi, wo, cot_rows, hidden_in, ffn_low = mixer_front(
        doc_lengths, stream, premix, branch_weight.T, input_weight.T, output_weight, wg, par,
        preffn, cotangent,
    )

    out_part, terms, far_terms, resid_grad, resid_low, preffn_grad = feed_forward(
        ffn_low, cot_rows, cotangent, hidden_in, preffn, ffn_gate, ffn_upward, ffn_down
    )

    layer_out, sums, last_terms, stream_grad, ob_grad, input_grad, gate_grad, dpar, gains = mixer_back(
        doc_lengths, resid_low, out_part, hidden_in, terms, gated, wo, wbi, wg, par, pre, saved,
        normed_rows, stream, premix, resid_grad, preffn_grad,
    )
    mine = lax.dynamic_index_in_dim(terms, lax.axis_index("dp"), keepdims=False)
    far = [far_terms[0], far_terms[1], last_terms]
    ffn_sums = [
        sum(
            (sums[i, k].astype(f32) for i in range(sums.shape[0])),
            mine[k].astype(f32) + far[k].astype(f32),
        )
        for k in range(3)
    ]
    ob_grad = ob_grad.reshape(2 * width, -1)
    output_grad = ob_grad[:chans].astype(f32)
    branch_grad = ob_grad[width : width + chans].astype(f32).T
    input_grad = input_grad.reshape(width, -1)[:chans].astype(f32).T
    gate_grad = gate_grad.reshape(width, -1).astype(f32)
    dpar = dpar[:, :chans]
    decay_grad = dpar[G_DECAY] * (-DECAY_SCALE * jax.nn.sigmoid(decay_param.astype(f32)))
    return (
        layer_out,
        stream_grad,
        gains[0],
        branch_grad,
        input_grad,
        dpar[G_TAP : G_TAP + CONVW],
        dpar[G_BIAS],
        diagonal_blocks(gate_grad[:, :width], heads, size),
        dpar[G_RATE].reshape(heads, size),
        diagonal_blocks(gate_grad[:, width:], heads, size),
        dpar[G_ENTRY].reshape(heads, size),
        decay_grad,
        output_grad,
        gains[1],
        ffn_sums[0],
        ffn_sums[1],
        ffn_sums[2],
    )


def solution(mesh):
    placed = (
        P(("dp", "head"), None),
        P("dp", None),
        P(),
        P(None, "head"),
        P(None, "head"),
        P(None, "head"),
        P("head"),
        P("head", None, None),
        P("head", None),
        P("head", None, None),
        P("head", None),
        P("head"),
        P("head", None),
        P(),
        P(None, "head"),
        P(None, "head"),
        P(None, "head"),
        P(("dp", "head"), None),
    )
    return jax.shard_map(
        shards,
        mesh=mesh,
        in_specs=placed,
        out_specs=(
            P(("dp", "head"), None),
            P(("dp", "head"), None),
            P(),
            P(None, "head"),
            P(None, "head"),
            P(None, "head"),
            P("head"),
            P("head", None, None),
            P("head", None),
            P("head", None, None),
            P("head", None),
            P("head"),
            P("head", None),
            P(),
            P("dp", "head"),
            P("dp", "head"),
            P("dp", "head"),
        ),
        check_vma=False,
    )
```

```python
import functools
import math

import jax
import jax.numpy as jnp
from jax import lax
from jax.experimental import pallas as pl
from jax.experimental.pallas import tpu as pltpu
from jax.sharding import PartitionSpec as P

CONVW = 4
SEQ = 2048
CHUNK = 256
BLOCK = 64
LANES = 128
HALO = 8
PARTS = 2
LAG = 2
OUT_AT = 2
FAR_TERMS = 2
VMEM_BYTES = 62 * 2**20
IN_VMEM = pl.BlockSpec(memory_space=pltpu.VMEM)
IN_SMEM = pl.BlockSpec(memory_space=pltpu.SMEM)
IN_ANY = pl.BlockSpec(memory_space=pl.ANY)

EPSILON = 1e-06
DECAY_SCALE = 8.0
GELU_A = math.sqrt(2.0 / math.pi)
GELU_B = 0.044715

BIAS, TAP, RATE_B, ENTRY_B, DECAY = 0, 1, 5, 6, 7
PARAMS = 8
SAVED = 4
G_BIAS, G_TAP, G_RATE, G_ENTRY, G_DECAY = 0, 1, 5, 6, 7


def rms_parts(values):
    rinv = lax.rsqrt(jnp.mean(values * values, axis=-1, keepdims=True) + EPSILON)
    return rinv, values * rinv


def norm_back(unit, rinv, gain, grad):
    q = gain * grad
    return rinv * (q - unit * jnp.mean(q * unit, axis=-1, keepdims=True))


def contract_cols(leading, trailing):
    return lax.dot_general(
        leading, trailing, (((1,), (1,)), ((), ())), preferred_element_type=jnp.float32
    )


def contract_rows(leading, trailing):
    return lax.dot_general(
        leading, trailing, (((0,), (0,)), ((), ())), preferred_element_type=jnp.float32
    )


def gelu_pair(v):
    sq = v * v
    th = jnp.tanh(GELU_A * v * (1.0 + GELU_B * sq))
    half = 0.5 * (1.0 + th)
    slope = half + 0.5 * v * (1.0 - th * th) * (GELU_A * (1.0 + 3.0 * GELU_B * sq))
    return v * half, slope


def gelu(v):
    return v * (0.5 * (1.0 + jnp.tanh(GELU_A * v * (1.0 + GELU_B * v * v))))


def decay_terms(rate_gate, slope, fresh):
    log_decay = slope * rate_gate
    c = jnp.exp(log_decay)
    y = 2.0 * log_decay
    series = 1.0 + y * (1.0 / 7.0)
    for n in (6, 5, 4, 3, 2):
        series = 1.0 + (y * (1.0 / n)) * series
    sq = c * c
    q = jnp.where(y > -0.5, -y * series, 1.0 - sq)
    rsq = lax.rsqrt(jnp.maximum(q, 1e-37))
    return (
        jnp.where(fresh, 0.0, c),
        jnp.where(fresh, 1.0, q * rsq),
        jnp.where(fresh, 0.0, sq * rsq),
    )


def doc_places(lengths, first, rows):
    spots = first + lax.broadcasted_iota(jnp.int32, (rows, LANES), 0)
    begin = jnp.zeros((rows, LANES), jnp.int32)
    start = jnp.int32(0)
    for k in range(lengths.shape[1] - 1):
        start = start + lengths[0, k]
        begin = jnp.where(spots >= start, start, begin)
    return spots - begin


def each(count, body):
    def step(i, _):
        body(i)
        return 0

    lax.fori_loop(0, count, step, 0)


def line_place():
    return lax.axis_index("head"), lax.axis_size("head")


def peers(axis):
    n = lax.axis_size(axis)
    return [lax.rem(lax.axis_index(axis) + k, n) for k in range(1, n)]


def far_peer(axis):
    return lax.axis_size(axis) - 1 - lax.axis_index(axis)


def far_copies(terms, far_terms, sems):
    far = far_peer("dp")
    return [
        pltpu.make_async_remote_copy(
            src_ref=terms.at[far, k],
            dst_ref=far_terms.at[k],
            send_sem=sems.at[0, k],
            recv_sem=sems.at[1, k],
            device_id={"dp": far},
            device_id_type=pl.DeviceIdType.MESH,
        )
        for k in range(far_terms.shape[0])
    ]


def near_copies(terms, near_terms, last_terms, sems):
    n, me, far = lax.axis_size("dp"), lax.axis_index("dp"), far_peer("dp")
    for k in range(n - 2):
        peer = k + jnp.where(k >= jnp.minimum(me, far), 1, 0)
        peer = peer + jnp.where(k + 1 >= jnp.maximum(me, far), 1, 0)
        slot = me - jnp.where(peer < me, 1, 0) - jnp.where(n - 1 - peer < me, 1, 0)
        yield pltpu.make_async_remote_copy(
            src_ref=terms.at[peer],
            dst_ref=near_terms.at[slot],
            send_sem=sems.at[0, k],
            recv_sem=sems.at[1, slot],
            device_id={"dp": peer},
            device_id_type=pl.DeviceIdType.MESH,
        )
    yield pltpu.make_async_remote_copy(
        src_ref=terms.at[far, 2],
        dst_ref=last_terms,
        send_sem=sems.at[0, n - 2],
        recv_sem=sems.at[1, n - 2],
        device_id={"dp": far},
        device_id_type=pl.DeviceIdType.MESH,
    )


def near_arrive(near_terms, last_terms, sems):
    for k in range(near_terms.shape[0]):
        pltpu.make_async_copy(near_terms.at[k], near_terms.at[k], sems.at[1, k]).wait()
    pltpu.make_async_copy(last_terms, last_terms, sems.at[1, near_terms.shape[0]]).wait()


def peer_barrier(axes):
    barrier = pltpu.get_barrier_semaphore()
    count = 0
    for axis in axes:
        for peer in peers(axis):
            pl.semaphore_signal(
                barrier, inc=1, device_id={axis: peer}, device_id_type=pl.DeviceIdType.MESH
            )
            count += 1
    pl.semaphore_wait(barrier, count)


def wait_neighbours(sem, j, n):
    inside = (j > 0) & (j < n - 1)

    @pl.when(inside)
    def _():
        pl.semaphore_wait(sem, 2)

    @pl.when(jnp.logical_not(inside))
    def _():
        pl.semaphore_wait(sem, 1)


def line_barrier(j, n):
    barrier = pltpu.get_barrier_semaphore()
    for side in (-1, 1):

        @pl.when((j + side >= 0) & (j + side < n))
        def _():
            pl.semaphore_signal(
                barrier, inc=1, device_id={"head": j + side}, device_id_type=pl.DeviceIdType.MESH
            )

    wait_neighbours(barrier, j, n)


class Gather:
    def __init__(self, j, n, buf, send, recv):
        self.j, self.n, self.buf, self.send, self.recv = j, n, buf, send, recv
        self.span = buf.shape[1] // PARTS

    def copy(self, block, s, side, source=None):
        part = pl.ds(s * self.span, self.span)
        target = self.buf.at[block, part]
        return pltpu.make_async_remote_copy(
            src_ref=target if source is None else source.at[part],
            dst_ref=target,
            send_sem=self.send.at[(side + 1) // 2, block, s],
            recv_sem=self.recv.at[block, s],
            device_id={"head": self.j + side},
            device_id_type=pl.DeviceIdType.MESH,
        )

    def there(self, side):
        return (self.j + side >= 0) & (self.j + side < self.n)

    def flows(self, t):
        for side in (1, -1):
            block = self.j - side * t
            yield side, block, (block >= 0) & (block < self.n)

    def start(self, source, parts=range(PARTS)):
        for s in parts:
            for side in (1, -1):

                @pl.when(self.there(side))
                def _():
                    self.copy(self.j, s, side, source).start()

    def step(self, t, parts=range(PARTS)):
        for s in parts:
            for side, block, live in self.flows(t):

                @pl.when(live)
                def _():
                    self.copy(block, s, -side).wait_recv()

                @pl.when(live & self.there(side))
                def _():
                    self.copy(block, s, side).start()

    def finish(self, parts=range(PARTS)):
        def drain(t):
            for s in parts:
                for side, block, live in self.flows(t):

                    @pl.when(live & self.there(side))
                    def _():
                        self.copy(block, s, side).wait_send()

        each(self.n, drain)


class Scatter:
    def __init__(self, j, n, own, held, send, recv, last=2):
        self.j, self.n, self.own, self.held, self.send, self.recv = j, n, own, held, send, recv
        self.span = own.shape[1] // PARTS
        self.ends = (j, n)
        self.spot = last
        self.compact = own.shape[0] != n

    def place(self, block, side):
        return block if not self.compact else (1 - side) // 2

    def last(self):
        return self.j if not self.compact else self.spot

    def rows(self, s):
        return pl.ds(s * self.span, self.span)

    def slot(self, block, side, at):
        return block if side == 1 else jnp.where(block == at, self.n, block)

    def arrival(self, slot, s):
        return pltpu.make_async_copy(
            self.held.at[slot, self.rows(s)], self.held.at[slot, self.rows(s)], self.recv.at[slot, s]
        )

    def flows(self, t):
        for side in (1, -1):
            lag = self.j if side == 1 else self.n - 1 - self.j
            block = self.n - 1 - (t - lag) if side == 1 else t - lag
            yield side, block, (t >= lag) & (t <= self.n - 2)

    def copy(self, source, block, s, side):
        slot = self.slot(block, side, self.j + side)
        return pltpu.make_async_remote_copy(
            src_ref=source.at[block, self.rows(s)],
            dst_ref=self.held.at[slot, self.rows(s)],
            send_sem=self.send.at[block, s],
            recv_sem=self.recv.at[slot, s],
            device_id={"head": self.j + side},
            device_id_type=pl.DeviceIdType.MESH,
        )

    def step(self, t, parts=range(PARTS)):
        for s in parts:
            for side, block, live in self.flows(t):
                behind = (self.j - side >= 0) & (self.j - side < self.n)

                @pl.when(live & jnp.logical_not(behind))
                def _():
                    if self.compact:
                        self.held[block, self.rows(s), :] = self.own[
                            self.place(block, side), self.rows(s), :
                        ]
                        self.copy(self.held, block, s, side).start()
                    else:
                        self.copy(self.own, block, s, side).start()

                @pl.when(live & behind)
                def _():
                    self.arrival(block, s).wait()
                    self.add(block, s, side)
                    self.copy(self.held, block, s, side).start()

    def add(self, block, s, side):
        def add_rows(i):
            rows = pl.ds(pl.multiple_of(s * self.span + i * STRIP, STRIP), STRIP)
            total = self.own[self.place(block, side), rows, :].astype(jnp.float32) + self.held[
                block, rows, :
            ].astype(jnp.float32)
            self.held[block, rows, :] = total.astype(jnp.bfloat16)

        each(self.span // STRIP, add_rows)

    def arrive(self, parts=range(PARTS)):
        for s in parts:

            @pl.when(self.j > 0)
            def _():
                self.arrival(self.ends[0], s).wait()

            @pl.when(self.j < self.n - 1)
            def _():
                self.arrival(self.ends[1], s).wait()

    def result(self, rows):
        total = self.own[self.last(), rows, :].astype(jnp.float32)
        left = self.held[self.ends[0], rows, :].astype(jnp.float32)
        right = self.held[self.ends[1], rows, :].astype(jnp.float32)
        total = total + jnp.where(self.j > 0, left, 0.0)
        return total + jnp.where(self.j < self.n - 1, right, 0.0)

    def finish(self):
        def drain(t):
            for s in range(PARTS):
                for side, block, live in self.flows(t):

                    @pl.when(live)
                    def _():
                        self.copy(self.held, block, s, side).wait_send()

        each(self.n - 1, drain)


class Share:
    def __init__(self, axis, slots, send, recv):
        self.axis, self.slots, self.send, self.recv = axis, slots, send, recv
        self.me = lax.axis_index(axis)

    def copy(self, slot, peer, source=None):
        return pltpu.make_async_remote_copy(
            src_ref=self.slots.at[slot] if source is None else source,
            dst_ref=self.slots.at[slot],
            send_sem=self.send.at[peer],
            recv_sem=self.recv.at[slot],
            device_id={self.axis: peer},
            device_id_type=pl.DeviceIdType.MESH,
        )

    def start(self, sources=None):
        for peer in peers(self.axis):
            source = None if sources is None else sources.at[peer]
            self.copy(self.me, peer, source).start()

    def arrive(self):
        for peer in peers(self.axis):
            self.copy(peer, peer).wait_recv()

    def finish(self):
        for peer in peers(self.axis):
            self.copy(self.me, peer).wait_send()


def share_sems(axis):
    n = lax.axis_size(axis)
    return [pltpu.SemaphoreType.DMA((n,)), pltpu.SemaphoreType.DMA((n,))]


class Sum:
    def __init__(self, terms, slots, total, sems):
        self.terms, self.slots, self.total = terms, slots, total
        self.parts = Share("dp", slots, sems[0], sems[1])
        self.whole = Share("dp", total, sems[2], sems[3])
        self.me, self.sem = self.parts.me, sems[4]

    def start(self):
        self.parts.start(self.terms)

    def keep(self):
        return pltpu.make_async_copy(self.slots.at[self.me], self.total.at[self.me], self.sem)

    def spread(self):
        self.parts.arrive()
        rows = self.slots.shape[1]

        def add(part):
            value = jnp.zeros((STRIP, self.slots.shape[2]), jnp.float32)
            for i in range(self.slots.shape[0]):
                mine = self.terms[i, part, :].astype(jnp.float32)
                other = self.slots[i, part, :].astype(jnp.float32)
                value = value + jnp.where(self.me == i, mine, other)
            self.slots[self.me, part, :] = value.astype(jnp.bfloat16)

        strips(rows, add)
        for peer in peers("dp"):
            self.whole.copy(self.me, peer, self.slots.at[self.me]).start()
        self.keep().start()

    def finish(self):
        self.whole.arrive()
        self.keep().wait()
        self.parts.finish()
        self.whole.finish()


def sum_sems():
    return [*share_sems("dp"), *share_sems("dp"), pltpu.SemaphoreType.DMA]


def gather_sems(n):
    return [pltpu.SemaphoreType.DMA((2, n, PARTS)), pltpu.SemaphoreType.DMA((n, PARTS))]


def scatter_sems(n):
    return [pltpu.SemaphoreType.DMA((n, PARTS)), pltpu.SemaphoreType.DMA((n + 1, PARTS))]


def line_call(kernel, ident, name, out_shape, in_specs, out_specs, scratch, cost=None):
    return pl.pallas_call(
        kernel,
        out_shape=out_shape,
        in_specs=in_specs,
        out_specs=out_specs,
        scratch_shapes=scratch,
        compiler_params=pltpu.CompilerParams(
            collective_id=ident, has_side_effects=True, vmem_limit_bytes=VMEM_BYTES
        ),
        name=name,
    )


STRIP = 16


def strips(rows, body, first=0):
    each(rows // STRIP, lambda i: body(pl.ds(pl.multiple_of(first + i * STRIP, STRIP), STRIP)))


def front_kernel(
    lengths, stream, premix, wb, wi, wo_in, wg, par, preffn, cot,
    rows_out, pre_out, saved, gated_out, wbi_out, wo_out, cot_rows, hidden, low_out,
    normed, rows, wbi, wo, pre, gated, stage, z, carry, own, held, raw,
    gsend, grecv, csend, crecv, send, recv, keep_sem, pre_sem, stage_sem, one_sem, raw_sem,
):
    j, n = line_place()
    f32, bf16 = jnp.float32, jnp.bfloat16
    local, depth = stream.shape
    width, chans = gated.shape[1], wb.shape[0]
    tiles = width // LANES
    loads = [
        pltpu.make_async_copy(source, raw.at[k], raw_sem.at[k])
        for k, source in enumerate((wb, wi, wo_in))
    ]
    for load in loads:
        load.start()
    line_barrier(j, n)

    def norm(part):
        _, unit = rms_parts(stream[part, :].astype(f32))
        normed[part, :] = (unit * premix[...]).astype(bf16)

    strips(local, norm)
    gather = Gather(j, n, rows, gsend, grecv)
    gather.start(normed)
    for k, (target, first) in enumerate(((wbi, 0), (wbi, width), (wo, 0))):
        loads[k].wait()
        whole = chans // STRIP * STRIP
        target[first + whole : first + width, :] = jnp.zeros((width - whole, depth), bf16)
        target[first : first + chans, :] = raw[k]
    out_copies = [
        pltpu.make_async_copy(wbi, wbi_out, one_sem.at[0]),
        pltpu.make_async_copy(wo, wo_out, one_sem.at[1]),
    ]
    for copy in out_copies:
        copy.start()

    def span(block):
        return pl.ds(pl.multiple_of(block * local, local), local)

    def shifted(block):
        return pl.ds(pl.multiple_of(block * local + HALO, HALO), local)

    def keep(source, block):
        return pltpu.make_async_copy(source, rows_out.at[block], keep_sem.at[block])

    def keep_pre(block):
        return pltpu.make_async_copy(
            pre.at[shifted(block)], pre_out.at[span(block)], pre_sem.at[block]
        )

    pre[0:HALO, :] = jnp.zeros((HALO, 2 * width), f32)
    keep(normed, j).start()
    pre[shifted(j), :] = contract_cols(normed[...], wbi[...])
    keep_pre(j).start()

    def visit(v):
        t = v // 2 + 1
        block = jnp.where(v % 2 == 0, j - t, j + t)

        @pl.when(v % 2 == 0)
        def _():
            gather.step(t)

        @pl.when((block >= 0) & (block < n))
        def _():
            keep(rows.at[block], block).start()
            pre[shifted(block), :] = contract_cols(rows[block], wbi[...])
            keep_pre(block).start()

    each(2 * (n - 1), visit)
    cots = Gather(j, n, cot_rows, csend, crecv)
    cots.start(cot)
    mine = pltpu.make_async_copy(cot, cot_rows.at[j], one_sem.at[2])
    mine.start()

    carry[...] = jnp.zeros_like(carry)
    count = n * local // CHUNK

    def keep_stage(i):
        return pltpu.make_async_copy(
            stage.at[lax.rem(i, 2)],
            saved.at[pl.ds(pl.multiple_of(i * CHUNK, CHUNK), CHUNK)],
            stage_sem.at[lax.rem(i, 2)],
        )

    def chunk(i):
        first = i * CHUNK

        @pl.when(i >= 2)
        def _():
            keep_stage(i - 2).wait()

        u_out, r_out, e_out, h_out = (
            stage.at[lax.rem(i, 2), :, k * width : (k + 1) * width] for k in range(SAVED)
        )

        def conv_step(b):
            row = pl.multiple_of(b * BLOCK, BLOCK)
            halo = pl.ds(pl.multiple_of(first + row, BLOCK), BLOCK + HALO)
            place = doc_places(lengths, first + row, BLOCK)
            for t in range(tiles):
                cols = pl.ds(t * LANES, LANES)
                xs = pre[halo, pl.ds(width + t * LANES, LANES)]
                total = par[BIAS : BIAS + 1, cols] + par[TAP : TAP + 1, cols] * xs[HALO:]
                for k in range(1, CONVW):
                    term = par[TAP + k : TAP + k + 1, cols] * xs[HALO - k : HALO - k + BLOCK]
                    total = total + jnp.where(place >= k, term, 0.0)
                u_out[pl.ds(row, BLOCK), cols] = total

        each(CHUNK // BLOCK, conv_step)
        z[...] = jnp.dot(u_out[...].astype(bf16), wg[...], preferred_element_type=f32)

        def scan_step(b):
            row = pl.multiple_of(b * BLOCK, BLOCK)
            part = pl.ds(row, BLOCK)
            spot = pl.ds(pl.multiple_of(first + row, BLOCK), BLOCK)
            here = pl.ds(pl.multiple_of(first + row + HALO, HALO), BLOCK)
            fresh = doc_places(lengths, first + row, BLOCK) == 0
            inner = lax.broadcasted_iota(jnp.int32, (BLOCK, LANES), 0) % 8
            for t in range(tiles):
                cols = pl.ds(t * LANES, LANES)
                other = pl.ds(width + t * LANES, LANES)
                r = jax.nn.sigmoid(z[part, cols] + par[RATE_B : RATE_B + 1, cols])
                e = jax.nn.sigmoid(z[part, other] + par[ENTRY_B : ENTRY_B + 1, cols])
                u = u_out[part, cols]
                c, m, _ = decay_terms(r, par[DECAY : DECAY + 1, cols], fresh)
                r_out[part, cols] = r
                e_out[part, cols] = e
                b_ = m * e * u
                for d in (1, 2, 4):
                    near = inner >= d
                    b_ = b_ + c * jnp.where(near, pltpu.roll(b_, d, 0), 0.0)
                    c = c * jnp.where(near, pltpu.roll(c, d, 0), 1.0)
                last = carry[0:1, cols]
                pieces = []
                for g in range(BLOCK // 8):
                    eight = slice(g * 8, g * 8 + 8)
                    state = b_[eight] + c[eight] * last
                    last = state[7:8]
                    pieces.append(state)
                carry[0:1, cols] = last
                h = jnp.concatenate(pieces, axis=0)
                h_out[part, cols] = h
                gated[spot, cols] = (h * gelu(pre[here, cols])).astype(bf16)

        each(CHUNK // BLOCK, scan_step)
        keep_stage(i).start()

        @pl.when(i == count * 5 // 8)
        def _():
            cots.step(1)

    each(count, chunk)
    keep_gated = pltpu.make_async_copy(gated, gated_out, one_sem.at[3])
    keep_gated.start()

    scatter = Scatter(j, n, own, held, send, recv)

    def compute(block, slot):
        own[slot] = jnp.dot(
            gated[span(block), :], wo[...], preferred_element_type=f32
        ).astype(bf16)

    def ahead(t):
        for side, block, live in scatter.flows(t):
            pl.when(live)(functools.partial(compute, block, scatter.place(block, side)))

    ahead(0)

    def step(t):
        scatter.step(t)
        ahead(t + 1)

        @pl.when(t == 0)
        def _():
            compute(j, 2)

        @pl.when(t + 2 < n)
        def _():
            cots.step(t + 2)

    each(n - 1, step)
    scatter.arrive()

    def settle(part):
        total = stream[part, :].astype(f32) + scatter.result(part)
        hidden[part, :] = total
        _, unit = rms_parts(total)
        low_out[part, :] = (unit * preffn[...]).astype(bf16)

    strips(local, settle)
    scatter.finish()
    gather.finish()
    cots.finish()
    mine.wait()
    keep_gated.wait()
    for copy in out_copies:
        copy.wait()
    keep(normed, j).wait()
    keep_pre(j).wait()
    for k in range(1, n):
        other = lax.rem(j + k, n)
        keep(rows.at[other], other).wait()
        keep_pre(other).wait()
    for i in range(max(count - 2, 0), count):
        keep_stage(i).wait()


def mixer_front(lengths, stream, premix, wb, wi, wo, wg, par, preffn, cot):
    n = lax.axis_size("head")
    local, depth = stream.shape
    width, tokens = wg.shape[0], n * local
    f32, bf16 = jnp.float32, jnp.bfloat16
    shape, vmem, dma = jax.ShapeDtypeStruct, pltpu.VMEM, pltpu.SemaphoreType.DMA
    return line_call(
        front_kernel, 0, "mixer_front",
        (
            shape((n, local, depth), bf16),
            shape((tokens, 2 * width), f32),
            shape((tokens, SAVED * width), f32),
            shape((tokens, width), bf16),
            shape((2 * width, depth), bf16),
            shape((width, depth), bf16),
            shape((n, local, depth), bf16),
            shape((local, depth), f32),
            shape((local, depth), bf16),
        ),
        [IN_SMEM, IN_VMEM, IN_VMEM, IN_ANY, IN_ANY, IN_ANY, *[IN_VMEM] * 4],
        [IN_ANY] * 7 + [IN_VMEM] * 2,
        [
            vmem((local, depth), bf16),
            vmem((n, local, depth), bf16),
            vmem((2 * width, depth), bf16),
            vmem((width, depth), bf16),
            vmem((HALO + tokens, 2 * width), f32),
            vmem((tokens, width), bf16),
            vmem((2, CHUNK, SAVED * width), f32),
            vmem((CHUNK, 2 * width), f32),
            vmem((8, width), f32),
            vmem((3, local, depth), bf16),
            vmem((n + 1, local, depth), bf16),
            vmem((3, wb.shape[0], depth), bf16),
            *gather_sems(n),
            *gather_sems(n),
            *scatter_sems(n),
            dma((n,)),
            dma((n,)),
            dma((2,)),
            dma((4,)),
            dma((3,)),
        ],
    )(lengths, stream, premix, wb, wi, wo, wg, par, preffn, cot)


def ffn_kernel(
    low, cot_rows, cot_in, hidden_in, gain, wg_in, wu_in, wd_in,
    out_part, terms, far_terms, resid, resid_low, gain_grad,
    rows, cot_pair, kept, own, held, stage, wstage, cot_cols, wg, wu, wd, cot, hidden,
    gsend, grecv, send, recv, cot_sem, out_sem, col_sem, term_sem, far_sem, load_sem,
):
    j, n = line_place()
    peer_barrier(("head", "dp"))
    f32, bf16 = jnp.float32, jnp.bfloat16
    local, depth = low.shape
    units = wg.shape[1]
    half = local // PARTS
    fstep = 256 if units % 256 == 0 else LANES
    dstep = 512
    gather = Gather(j, n, rows, gsend, grecv)
    scatter = Scatter(j, n, own, held, send, recv)
    gather.start(low, [0])
    loads = [
        pltpu.make_async_copy(a, b, load_sem.at[k])
        for k, (a, b) in enumerate(
            ((wg_in, wg), (wu_in, wu), (wd_in, wd), (cot_in, cot), (hidden_in, hidden))
        )
    ]
    for load in loads:
        load.start()
    rows[j] = low[...]
    for load in loads:
        load.wait()

    def pair(chip, q):
        return pl.ds(pl.multiple_of(2 * chip, 2), 2), pl.ds(q * half, half)

    def fetch(chip, q):
        return pltpu.make_async_copy(cot_rows.at[pair(chip, q)], cot_pair, cot_sem)

    def put(chip, q):
        return pltpu.make_async_copy(stage, out_part.at[pair(chip, q)], out_sem)

    def pair_work(chip, q):
        spot = pair(chip, q)

        def flat(v):
            return v.reshape(2 * half, v.shape[-1])

        def fold(v):
            return v.astype(bf16).reshape(2, half, v.shape[-1])

        for f in range(0, units, fstep):
            cols = slice(f, f + fstep)
            gate = jnp.dot(flat(rows[spot]), wg[:, cols], preferred_element_type=f32)
            act, slope = gelu_pair(gate)
            up = jnp.dot(flat(rows[spot]), wu[:, cols], preferred_element_type=f32)
            kept[2, *spot, cols] = fold(act * up)
            grad = jnp.dot(flat(cot_pair[...]), wd[:, cols], preferred_element_type=f32)
            kept[0, *spot, cols] = fold(grad * up * slope)
            kept[1, *spot, cols] = fold(grad * act)
        for d in range(0, depth, dstep):
            cols = slice(d, d + dstep)
            own[*spot, cols] = fold(
                contract_cols(flat(kept[0, *spot]), wg[cols, :])
                + contract_cols(flat(kept[1, *spot]), wu[cols, :])
            )
            stage[:, :, cols] = fold(contract_cols(flat(kept[2, *spot]), wd[cols, :]))

    def gather_half(q):
        def visit(i):
            t = i + 1
            reach = t // 2
            chip = j // 2 + jnp.where((t + j) % 2 == 0, -reach, reach)
            live = (chip >= 0) & (chip < n // 2)

            @pl.when(live)
            def _():
                fetch(chip, q).start()

            gather.step(t, [q])
            if q:
                scatter.step(t - 1, [0])

            @pl.when(live)
            def _():
                fetch(chip, q).wait()

                @pl.when((t > 1) | (q > 0))
                def _():
                    put(chip, q).wait()

                pair_work(chip, q)
                put(chip, q).start()

        each(n - 1, visit)

    gather_half(0)
    gather.start(low, [1])
    gather_half(1)
    put(j // 2, 1).wait()

    width = depth // n
    per = depth // terms.shape[0] // width

    far = far_peer("dp")

    def columns(b):
        return pl.ds(pl.multiple_of(lax.rem(b + far * per, n) * width, width), width)

    def take(b):
        return pltpu.make_async_copy(cot_rows.at[:, :, columns(b)], cot_cols, col_sem)

    def give(b):
        owner = lax.rem(b // per + far, n // per)
        spot = pl.ds(pl.multiple_of(lax.rem(b, per) * width, width), width)
        return pltpu.make_async_copy(wstage, terms.at[owner, :, spot, :], term_sem)

    def weights(b):
        xs = rows[:, :, columns(b)].reshape(n * local, width)
        take(b).wait()

        @pl.when(b > 0)
        def _():
            give(b).wait()

        @pl.when(b == per)
        def _():
            for copy in far_copies(terms, far_terms, far_sem):
                copy.start()

        for k, lead in ((0, xs), (1, xs), (2, cot_cols[...].reshape(n * local, width))):
            wstage[k] = contract_rows(lead, kept[k].reshape(n * local, units)).astype(bf16)
        give(b).start()

        @pl.when(b + 1 < n)
        def _():
            take(b + 1).start()

    take(0).start()

    def step(t):
        pl.when(t < n - 1)(lambda: scatter.step(t, [1]))
        weights(t)

    each(n, step)
    scatter.arrive()
    gain_grad[...] = jnp.zeros_like(gain_grad)

    def settle(part):
        rinv, u = rms_parts(hidden[part, :])
        grad = scatter.result(part)
        gain_grad[...] += jnp.sum(grad * u, axis=0, keepdims=True)
        total = cot[part, :].astype(f32) + norm_back(u, rinv, gain[...], grad)
        resid[part, :] = total
        resid_low[part, :] = total.astype(bf16)

    strips(local, settle)
    give(0).wait()
    gather.finish()
    scatter.finish()
    for copy in far_copies(terms, far_terms, far_sem):
        copy.wait()


def feed_forward(low, cot_rows, cot, hidden, gain, wg, wu, wd):
    n, group = lax.axis_size("head"), lax.axis_size("dp")
    local, depth = low.shape
    units = wg.shape[1]
    bf16 = jnp.bfloat16
    shape, vmem = jax.ShapeDtypeStruct, pltpu.VMEM
    pair = (2, local // PARTS, depth)
    return line_call(
        ffn_kernel, 2, "feed_forward",
        (
            shape((n, local, depth), bf16),
            shape((group, 3, depth // group, units), bf16),
            shape((FAR_TERMS, depth // group, units), bf16),
            shape((local, depth), jnp.float32),
            shape((local, depth), bf16),
            shape((1, depth), jnp.float32),
        ),
        [IN_VMEM, IN_ANY, IN_ANY, IN_ANY, IN_VMEM, IN_ANY, IN_ANY, IN_ANY],
        [IN_ANY, IN_ANY, IN_ANY, IN_VMEM, IN_VMEM, IN_VMEM],
        [
            vmem((n, local, depth), bf16),
            vmem(pair, bf16),
            vmem((3, n, local, units), bf16),
            vmem((n, local, depth), bf16),
            vmem((n + 1, local, depth), bf16),
            vmem(pair, bf16),
            vmem((3, depth // n, units), bf16),
            vmem((n, local, depth // n), bf16),
            *[vmem(wg.shape, bf16)] * 3,
            vmem((local, depth), bf16),
            vmem((local, depth), jnp.float32),
            *gather_sems(n),
            *scatter_sems(n),
            *[pltpu.SemaphoreType.DMA] * 4,
            pltpu.SemaphoreType.DMA((2, FAR_TERMS)),
            pltpu.SemaphoreType.DMA((5,)),
        ],
    )(low, cot_rows, cot, hidden, gain, wg, wu, wd)


def back_kernel(
    lengths, low, out_part, hidden, terms, gated, wo_in, wbi_in, wg, par, pre, saved,
    normed_rows, stream_in, gain, resid, preffn_grad,
    layer_out, sums, last_terms, stream_grad, ob_total, i_total, g_total, par_grad, gains,
    rows, own, held, wo, wbi, dh, dpre, acc, dgate, dz, du, carry, dpar,
    unit_bp, unit_h, unit_gated, unit_normed,
    obterms, obslots, iterms, islots, gterms, gslots, pslots, dslots, hslots,
    gsend, grecv, send4, recv4, send8, recv8, tsems, unit_sem, own_sem, chunk_sem,
    row_sem, wide_sem, load_sem, free, psend, precv, dsend, drecv, hsend, hrecv, *sems,
):
    j, n = line_place()
    f32, bf16 = jnp.float32, jnp.bfloat16
    local, depth = low.shape
    width = dh.shape[1]
    tiles = width // LANES
    stream, wide = unit_normed, acc.at[width : width + local]
    loads = [
        pltpu.make_async_copy(a, b, load_sem.at[k])
        for k, (a, b) in enumerate(((wo_in, wo), (wbi_in, wbi), (stream_in, stream)))
    ]
    for load in loads[:2]:
        load.start()
    peer_barrier(("head", "dp"))
    gather = Gather(j, n, rows, gsend, grecv)
    gather.start(low)
    for copy in near_copies(terms, sums, last_terms, tsems):
        copy.start()
    rows[j] = low[...]
    outs = Scatter(j, n, own, held, send4, recv4)
    acc[...] = jnp.zeros_like(acc)

    def fetch_out(block, slot):
        return pltpu.make_async_copy(out_part.at[block], own.at[slot], own_sem.at[slot])

    def outs_ahead(t):
        for start in (True, False):
            for side, block, live in outs.flows(t):
                copy = fetch_out(block, outs.place(block, side))
                pl.when(live)(copy.start if start else copy.wait)

    def outs_step(t):
        outs.step(t)
        outs_ahead(t + 1)

    def outs_slot(slot):
        t = slot - 1 - LAG

        @pl.when((t >= 0) & (t < n - 1))
        def _():
            outs_step(t)

    outs_ahead(0)
    fetch_out(j, 2).start()
    fetch_out(j, 2).wait()

    def unit_copies(block):
        span = pl.ds(pl.multiple_of(block * local, local), local)
        return (
            pltpu.make_async_copy(pre.at[span, 0:width], unit_bp, unit_sem.at[0]),
            pltpu.make_async_copy(
                saved.at[span, 3 * width : 4 * width], unit_h, unit_sem.at[1]
            ),
            pltpu.make_async_copy(gated.at[span], unit_gated, unit_sem.at[2]),
            pltpu.make_async_copy(normed_rows.at[block], unit_normed, unit_sem.at[3]),
        )

    def unit(block):
        span = pl.ds(pl.multiple_of(block * local, local), local)
        dh[span, :] = contract_cols(rows[block], wo[...])

        def act(i):
            part = pl.ds(pl.multiple_of(i * BLOCK, BLOCK), BLOCK)
            spot = pl.ds(pl.multiple_of(block * local + i * BLOCK, BLOCK), BLOCK)
            for t in range(tiles):
                cols = pl.ds(t * LANES, LANES)
                grad = dh[spot, cols]
                value, slope = gelu_pair(unit_bp[part, cols])
                dpre[spot, cols] = (grad * unit_h[part, cols] * slope).astype(bf16)
                dh[spot, cols] = grad * value

        each(local // BLOCK, act)
        acc[0:width, :] += contract_rows(unit_gated[...], rows[block])
        acc[width : 2 * width, :] += contract_rows(dpre[span, 0:width], unit_normed[...])

    def visit(v):
        t = (v + 1) // 2
        block = jnp.where(v % 2 == 1, j - t, j + t)
        live = (block >= 0) & (block < n)

        @pl.when(live)
        def _():
            for copy in unit_copies(block):
                copy.start()

        @pl.when(v % 2 == 1)
        def _():
            gather.step(t)
            outs_slot(t)

        @pl.when(live)
        def _():
            for copy in unit_copies(block):
                copy.wait()
            unit(block)

    loads[0].wait()
    each(2 * n - 1, visit)
    gather.finish()
    for side in (-1, 1):

        @pl.when((j + side >= 0) & (j + side < n))
        def _():
            pl.semaphore_signal(
                free, inc=1, device_id={"head": j + side}, device_id_type=pl.DeviceIdType.MESH
            )

    def pack(target, source, count):
        span = target.shape[1]

        def strip(i):
            row = pl.multiple_of(i * STRIP, STRIP)
            target[row // span, pl.ds(pl.multiple_of(lax.rem(row, span), STRIP), STRIP), :] = source[
                pl.ds(row, STRIP), :
            ].astype(bf16)

        each(count // STRIP, strip)

    obsum = Sum(obterms, obslots, ob_total, sems[0:5])
    isum = Sum(iterms, islots, i_total, sems[5:10])
    gsum = Sum(gterms, gslots, g_total, sems[10:15])
    pack(obterms, acc, 2 * width)
    obsum.start()
    loads[2].start()

    count = n * local // CHUNK

    def chunk_copies(i):
        base = lax.rem(i, 2) * (CHUNK + HALO)
        start = pl.multiple_of(i * CHUNK, CHUNK)
        ahead = pl.multiple_of(jnp.maximum(start - HALO, 0), HALO)
        halo, main = pl.ds(pl.multiple_of(base, HALO), HALO), pl.ds(
            pl.multiple_of(base + HALO, HALO), CHUNK
        )
        kept, x = slice(0, SAVED * width), slice(SAVED * width, (SAVED + 1) * width)
        pairs = (
            (saved.at[pl.ds(ahead, HALO)], acc.at[halo, kept]),
            (saved.at[pl.ds(start, CHUNK)], acc.at[main, kept]),
            (pre.at[pl.ds(ahead, HALO), width : 2 * width], acc.at[halo, x]),
            (pre.at[pl.ds(start, CHUNK), width : 2 * width], acc.at[main, x]),
        )
        return [
            pltpu.make_async_copy(a, b, chunk_sem.at[lax.rem(i, 2), k])
            for k, (a, b) in enumerate(pairs)
        ]

    def total(v):
        return jnp.sum(v, axis=0, keepdims=True)

    for copy in chunk_copies(count - 1):
        copy.start()
    du[...] = jnp.zeros_like(du)
    carry[...] = jnp.zeros_like(carry)
    dgate[...] = jnp.zeros_like(dgate)
    dpar[...] = jnp.zeros_like(dpar)

    def chunk(k):
        i = count - 1 - k

        @pl.when(i > 0)
        def _():
            for copy in chunk_copies(i - 1):
                copy.start()

        for copy in chunk_copies(i):
            copy.wait()
        base = lax.rem(i, 2) * (CHUNK + HALO)
        first = i * CHUNK
        du[CHUNK:, :] = du[0:HALO, :]

        def scan_step(b):
            row = pl.multiple_of(CHUNK - BLOCK - b * BLOCK, BLOCK)
            part = pl.ds(row, BLOCK)
            spot = pl.ds(pl.multiple_of(first + row, BLOCK), BLOCK)
            here = pl.ds(pl.multiple_of(base + HALO + row, HALO), BLOCK)
            halo = pl.ds(pl.multiple_of(base + row, HALO), BLOCK + HALO)
            fresh = doc_places(lengths, first + row, BLOCK) == 0
            place = lax.broadcasted_iota(jnp.int32, (BLOCK, LANES), 0)
            inner = place % 8
            for t in range(tiles):
                cols = pl.ds(t * LANES, LANES)
                u, r, e = (acc[here, pl.ds(m * width + t * LANES, LANES)] for m in range(3))
                prior = acc[halo, pl.ds(3 * width + t * LANES, LANES)][HALO - 1 : HALO - 1 + BLOCK]
                near_h = dh[spot, cols]
                decay = par[DECAY : DECAY + 1, cols]
                c, m, ratio = decay_terms(r, decay, fresh)
                b_, a_ = c * near_h, c
                for d in (1, 2, 4):
                    near_row = inner < 8 - d
                    b_ = b_ + a_ * jnp.where(near_row, pltpu.roll(b_, BLOCK - d, 0), 0.0)
                    a_ = a_ * jnp.where(near_row, pltpu.roll(a_, BLOCK - d, 0), 1.0)
                later = carry[0:1, cols]
                pieces = []
                front = later
                for g in reversed(range(BLOCK // 8)):
                    eight = slice(g * 8, g * 8 + 8)
                    state = b_[eight] + a_[eight] * front
                    front = state[0:1]
                    pieces.append(state)
                carry[0:1, cols] = front
                mu = jnp.concatenate(pieces[::-1], axis=0)
                adj = near_h + jnp.where(
                    place == BLOCK - 1, later, pltpu.roll(mu, BLOCK - 1, 0)
                )
                eu = e * u
                dlog = adj * (prior * c - eu * ratio)
                dpar[G_DECAY : G_DECAY + 1, cols] += total(dlog * r)
                dzr = decay * dlog * (r * (1.0 - r))
                dze = adj * m * eu * (1.0 - e)
                dpar[G_RATE : G_RATE + 1, cols] += total(dzr)
                dpar[G_ENTRY : G_ENTRY + 1, cols] += total(dze)
                dz[part, cols] = dzr.astype(bf16)
                dz[part, pl.ds(width + t * LANES, LANES)] = dze.astype(bf16)
                du[part, cols] = adj * m * e

        each(CHUNK // BLOCK, scan_step)
        u_chunk = acc[pl.ds(pl.multiple_of(base + HALO, HALO), CHUNK), 0:width]
        du[0:CHUNK, :] += contract_cols(dz[...], wg[...])
        dgate[...] += contract_rows(u_chunk.astype(bf16), dz[...])

        def conv_step(b):
            row = pl.multiple_of(b * BLOCK, BLOCK)
            spot = pl.ds(pl.multiple_of(first + row, BLOCK), BLOCK)
            halo = pl.ds(pl.multiple_of(base + row, HALO), BLOCK + HALO)
            place = doc_places(lengths, first + row, BLOCK + HALO)
            for t in range(tiles):
                cols = pl.ds(t * LANES, LANES)
                ds = du[pl.ds(row, BLOCK + HALO), cols]
                xs = acc[halo, pl.ds(SAVED * width + t * LANES, LANES)]
                mine = ds[0:BLOCK]
                dx = par[TAP : TAP + 1, cols] * mine
                dpar[G_BIAS : G_BIAS + 1, cols] += total(mine)
                dpar[G_TAP : G_TAP + 1, cols] += total(mine * xs[HALO:])
                for k in range(1, CONVW):
                    inside = jnp.where(place >= k, ds, 0.0)
                    dx = dx + par[TAP + k : TAP + k + 1, cols] * inside[k : k + BLOCK]
                    dpar[G_TAP + k : G_TAP + k + 1, cols] += total(
                        inside[0:BLOCK] * xs[HALO - k : HALO - k + BLOCK]
                    )
                dpre[spot, pl.ds(width + t * LANES, LANES)] = dx.astype(bf16)

        each(CHUNK // BLOCK, conv_step)
        pl.when(k % 2 == 0)(lambda: outs_slot(n + k // 2))

    each(count, chunk)
    for t in range(n - 1 - max(0, LAG - (count + 1) // 2), n - 1):
        outs_step(jnp.int32(t))
    pack(gterms, dgate, width)
    gsum.start()
    pshare = Share("dp", pslots, psend, precv)
    pslots[pshare.me] = dpar[...]
    pshare.start()
    load_hidden = pltpu.make_async_copy(hidden, wide, wide_sem.at[0])
    load_hidden.start()
    scatter = Scatter(j, n, own, rows, send8, recv8, last=3)
    loads[1].wait()
    loads[2].wait()

    def compute(block, slot):
        span = pl.ds(pl.multiple_of(block * local, local), local)
        own[slot] = jnp.dot(dpre[span, :], wbi[...], preferred_element_type=f32).astype(bf16)

    def ahead(t):
        for side, block, live in scatter.flows(t):
            pl.when(live)(functools.partial(compute, block, scatter.place(block, side)))

    ahead(0)
    wait_neighbours(free, j, n)
    scatter.step(0)
    ahead(1)
    obsum.spread()

    def settle_out(part):
        layer_out[part, :] = (wide[part, :] + outs.result(part)).astype(bf16)

    load_resid = pltpu.make_async_copy(resid, wide, wide_sem.at[1])

    def step(t):
        scatter.step(t)
        ahead(t + 1)

        @pl.when(t == OUT_AT)
        def _():
            outs.arrive()
            load_hidden.wait()
            strips(local, settle_out)
            outs.finish()
            load_resid.start()
            load.start()
            compute(j, 3)

        @pl.when(t == OUT_AT + 1)
        def _():
            load.wait()
            for c in range(0, width, LANES):
                acc[c : c + LANES, :] = contract_rows(
                    dpre[:, width + c : width + c + LANES],
                    held[0:n].reshape(n * local, depth),
                )
            pack(iterms, acc, width)
            isum.start()

        @pl.when(t == OUT_AT + 2)
        def _():
            gsum.spread()

    load = pltpu.make_async_copy(normed_rows, held.at[pl.ds(0, n)], row_sem)
    lax.fori_loop(1, n - 1, lambda t, _: (step(t), 0)[1], 0)
    isum.spread()
    scatter.arrive()
    load_resid.wait()
    gains[...] = jnp.zeros_like(gains)

    def settle(part):
        rinv, u = rms_parts(stream[part, :].astype(f32))
        grad = scatter.result(part)
        gains[0:1, :] += jnp.sum(grad * u, axis=0, keepdims=True)
        value = wide[part, :] + norm_back(u, rinv, gain[...], grad)
        stream_grad[part, :] = value.astype(bf16)

    strips(local, settle)

    gains[1:2, :] = preffn_grad[...]
    for axis, slots, ssem, rsem in (("dp", dslots, dsend, drecv), ("head", hslots, hsend, hrecv)):
        share = Share(axis, slots, ssem, rsem)
        slots[share.me] = gains[...]
        share.start()
        share.arrive()
        value = slots[0]
        for i in range(1, slots.shape[0]):
            value = value + slots[i]
        gains[...] = value
        share.finish()

    pshare.arrive()
    value = pslots[0]
    for i in range(1, pslots.shape[0]):
        value = value + pslots[i]
    par_grad[...] = value
    pshare.finish()
    for one in (gsum, obsum, isum):
        one.finish()
    scatter.finish()
    for copy in near_copies(terms, sums, last_terms, tsems):
        copy.wait_send()
    near_arrive(sums, last_terms, tsems)


def mixer_back(
    lengths, low, out_part, hidden, terms, gated, wo, wbi, wg, par, pre, saved,
    normed_rows, stream, gain, resid, preffn_grad,
):
    n, group = lax.axis_size("head"), lax.axis_size("dp")
    local, depth = stream.shape
    width, tokens = wo.shape[0], pre.shape[0]
    f32, bf16 = jnp.float32, jnp.bfloat16
    ob = (group, 2 * width // group, depth)
    one = (group, width // group, depth)
    gate = (group, width // group, 2 * width)
    dma = pltpu.SemaphoreType.DMA
    shape = jax.ShapeDtypeStruct
    return line_call(
        back_kernel, 3, "mixer_back",
        (
            shape((local, depth), bf16),
            shape((group - 2, *terms.shape[1:]), bf16),
            shape(terms.shape[2:], bf16),
            shape((local, depth), bf16),
            shape(ob, bf16),
            shape(one, bf16),
            shape(gate, bf16),
            shape((PARAMS, width), f32),
            shape((8, depth), f32),
        ),
        [
            IN_SMEM, IN_VMEM, *[IN_ANY] * 6, IN_VMEM, IN_VMEM, *[IN_ANY] * 4, IN_VMEM, IN_ANY,
            IN_VMEM,
        ],
        [IN_VMEM, IN_ANY, IN_ANY, IN_VMEM, IN_ANY, IN_ANY, IN_ANY, IN_VMEM, IN_VMEM],
        [
            pltpu.VMEM((n + 1, local, depth), bf16),
            pltpu.VMEM((4, local, depth), bf16),
            pltpu.VMEM((n + 1, local, depth), bf16),
            pltpu.VMEM(wo.shape, bf16),
            pltpu.VMEM(wbi.shape, bf16),
            pltpu.VMEM((tokens, width), f32),
            pltpu.VMEM((tokens, 2 * width), bf16),
            pltpu.VMEM((max(2 * width, 2 * (CHUNK + HALO)), depth), f32),
            pltpu.VMEM((width, 2 * width), f32),
            pltpu.VMEM((CHUNK, 2 * width), bf16),
            pltpu.VMEM((CHUNK + HALO, width), f32),
            pltpu.VMEM((8, width), f32),
            pltpu.VMEM((PARAMS, width), f32),
            pltpu.VMEM((local, width), f32),
            pltpu.VMEM((local, width), f32),
            pltpu.VMEM((local, width), bf16),
            pltpu.VMEM((local, depth), bf16),
            pltpu.VMEM(ob, bf16),
            pltpu.VMEM(ob, bf16),
            pltpu.VMEM(one, bf16),
            pltpu.VMEM(one, bf16),
            pltpu.VMEM(gate, bf16),
            pltpu.VMEM(gate, bf16),
            pltpu.VMEM((group, PARAMS, width), f32),
            pltpu.VMEM((group, 8, depth), f32),
            pltpu.VMEM((n, 8, depth), f32),
            *gather_sems(n),
            *scatter_sems(n),
            *scatter_sems(n),
            dma((2, group)),
            dma((4,)),
            dma((3,)),
            dma((2, 4)),
            dma,
            dma((2,)),
            dma((3,)),
            pltpu.SemaphoreType.REGULAR,
            *share_sems("dp"),
            *share_sems("dp"),
            *share_sems("head"),
            *sum_sems(),
            *sum_sems(),
            *sum_sems(),
        ],
    )(
        lengths, low, out_part, hidden, terms, gated, wo, wbi, wg, par, pre, saved,
        normed_rows, stream, gain, resid, preffn_grad,
    )


def block_diagonal(weights, width):
    heads, size = weights.shape[0], weights.shape[1]
    placed = [
        jnp.pad(weights[i], ((i * size, width - (i + 1) * size),) * 2) for i in range(heads)
    ]
    return functools.reduce(jnp.add, placed)


def diagonal_blocks(dense, heads, size):
    blocks = [dense[i * size : (i + 1) * size, i * size : (i + 1) * size] for i in range(heads)]
    return jnp.stack(blocks, axis=1).transpose(1, 0, 2)


def shards(
    stream, doc_lengths, premix_gain, branch_weight, input_weight, conv_kernel, conv_bias,
    rate_weight, rate_bias, entry_weight, entry_bias, decay_param, output_weight, preffn_gain,
    ffn_gate, ffn_upward, ffn_down, cotangent,
):
    f32, bf16 = jnp.float32, jnp.bfloat16
    heads, size = rate_bias.shape
    chans = branch_weight.shape[1]
    width = -(-chans // LANES) * LANES

    slope = -DECAY_SCALE * jax.nn.softplus(decay_param.astype(f32))
    par = jnp.concatenate(
        [
            conv_bias[None].astype(f32),
            conv_kernel.astype(f32),
            rate_bias.reshape(1, -1).astype(f32),
            entry_bias.reshape(1, -1).astype(f32),
            slope[None],
        ]
    )
    par = jnp.pad(par, ((0, 0), (0, width - chans)), constant_values=-1.0)
    par = jnp.where((jnp.arange(width)[None] < chans) | (jnp.arange(PARAMS)[:, None] == DECAY), par, 0.0)
    wg = jnp.concatenate(
        [block_diagonal(rate_weight, width), block_diagonal(entry_weight, width)], axis=1
    )

    premix = premix_gain.astype(f32)[None]
    preffn = preffn_gain.astype(f32)[None]
    normed_rows, pre, saved, gated, wbi, wo, cot_rows, hidden_in, ffn_low = mixer_front(
        doc_lengths, stream, premix, branch_weight.T, input_weight.T, output_weight, wg, par,
        preffn, cotangent,
    )

    out_part, terms, far_terms, resid_grad, resid_low, preffn_grad = feed_forward(
        ffn_low, cot_rows, cotangent, hidden_in, preffn, ffn_gate, ffn_upward, ffn_down
    )

    layer_out, sums, last_terms, stream_grad, ob_grad, input_grad, gate_grad, dpar, gains = mixer_back(
        doc_lengths, resid_low, out_part, hidden_in, terms, gated, wo, wbi, wg, par, pre, saved,
        normed_rows, stream, premix, resid_grad, preffn_grad,
    )
    mine = lax.dynamic_index_in_dim(terms, lax.axis_index("dp"), keepdims=False)
    far = [far_terms[0], far_terms[1], last_terms]
    ffn_sums = [
        sum(
            (sums[i, k].astype(f32) for i in range(sums.shape[0])),
            mine[k].astype(f32) + far[k].astype(f32),
        )
        for k in range(3)
    ]
    ob_grad = ob_grad.reshape(2 * width, -1)
    output_grad = ob_grad[:chans].astype(f32)
    branch_grad = ob_grad[width : width + chans].astype(f32).T
    input_grad = input_grad.reshape(width, -1)[:chans].astype(f32).T
    gate_grad = gate_grad.reshape(width, -1).astype(f32)
    dpar = dpar[:, :chans]
    decay_grad = dpar[G_DECAY] * (-DECAY_SCALE * jax.nn.sigmoid(decay_param.astype(f32)))
    return (
        layer_out,
        stream_grad,
        gains[0],
        branch_grad,
        input_grad,
        dpar[G_TAP : G_TAP + CONVW],
        dpar[G_BIAS],
        diagonal_blocks(gate_grad[:, :width], heads, size),
        dpar[G_RATE].reshape(heads, size),
        diagonal_blocks(gate_grad[:, width:], heads, size),
        dpar[G_ENTRY].reshape(heads, size),
        decay_grad,
        output_grad,
        gains[1],
        ffn_sums[0],
        ffn_sums[1],
        ffn_sums[2],
    )


def solution(mesh):
    placed = (
        P(("dp", "head"), None),
        P("dp", None),
        P(),
        P(None, "head"),
        P(None, "head"),
        P(None, "head"),
        P("head"),
        P("head", None, None),
        P("head", None),
        P("head", None, None),
        P("head", None),
        P("head"),
        P("head", None),
        P(),
        P(None, "head"),
        P(None, "head"),
        P(None, "head"),
        P(("dp", "head"), None),
    )
    return jax.shard_map(
        shards,
        mesh=mesh,
        in_specs=placed,
        out_specs=(
            P(("dp", "head"), None),
            P(("dp", "head"), None),
            P(),
            P(None, "head"),
            P(None, "head"),
            P(None, "head"),
            P("head"),
            P("head", None, None),
            P("head", None),
            P("head", None, None),
            P("head", None),
            P("head"),
            P("head", None),
            P(),
            P("dp", "head"),
            P("dp", "head"),
            P("dp", "head"),
        ),
        check_vma=False,
    )
```

```python
import functools
import math

import jax
import jax.numpy as jnp
from jax import lax
from jax.experimental import pallas as pl
from jax.experimental.pallas import tpu as pltpu
from jax.sharding import PartitionSpec as P

CONVW = 4
SEQ = 2048
CHUNK = 256
BLOCK = 64
LANES = 128
HALO = 8
PARTS = 4
LAG = 2
OUT_AT = 2
FAR_TERMS = 2
VMEM_BYTES = 62 * 2**20
IN_VMEM = pl.BlockSpec(memory_space=pltpu.VMEM)
IN_SMEM = pl.BlockSpec(memory_space=pltpu.SMEM)
IN_ANY = pl.BlockSpec(memory_space=pl.ANY)

EPSILON = 1e-06
DECAY_SCALE = 8.0
GELU_A = math.sqrt(2.0 / math.pi)
GELU_B = 0.044715

BIAS, TAP, RATE_B, ENTRY_B, DECAY = 0, 1, 5, 6, 7
PARAMS = 8
SAVED = 4
G_BIAS, G_TAP, G_RATE, G_ENTRY, G_DECAY = 0, 1, 5, 6, 7


def rms_parts(values):
    rinv = lax.rsqrt(jnp.mean(values * values, axis=-1, keepdims=True) + EPSILON)
    return rinv, values * rinv


def norm_back(unit, rinv, gain, grad):
    q = gain * grad
    return rinv * (q - unit * jnp.mean(q * unit, axis=-1, keepdims=True))


def contract_cols(leading, trailing):
    return lax.dot_general(
        leading, trailing, (((1,), (1,)), ((), ())), preferred_element_type=jnp.float32
    )


def contract_rows(leading, trailing):
    return lax.dot_general(
        leading, trailing, (((0,), (0,)), ((), ())), preferred_element_type=jnp.float32
    )


def gelu_pair(v):
    sq = v * v
    th = jnp.tanh(GELU_A * v * (1.0 + GELU_B * sq))
    half = 0.5 * (1.0 + th)
    slope = half + 0.5 * v * (1.0 - th * th) * (GELU_A * (1.0 + 3.0 * GELU_B * sq))
    return v * half, slope


def gelu(v):
    return v * (0.5 * (1.0 + jnp.tanh(GELU_A * v * (1.0 + GELU_B * v * v))))


def decay_terms(rate_gate, slope, fresh):
    log_decay = slope * rate_gate
    c = jnp.exp(log_decay)
    y = 2.0 * log_decay
    series = 1.0 + y * (1.0 / 7.0)
    for n in (6, 5, 4, 3, 2):
        series = 1.0 + (y * (1.0 / n)) * series
    sq = c * c
    q = jnp.where(y > -0.5, -y * series, 1.0 - sq)
    rsq = lax.rsqrt(jnp.maximum(q, 1e-37))
    return (
        jnp.where(fresh, 0.0, c),
        jnp.where(fresh, 1.0, q * rsq),
        jnp.where(fresh, 0.0, sq * rsq),
    )


def doc_places(lengths, first, rows):
    spots = first + lax.broadcasted_iota(jnp.int32, (rows, LANES), 0)
    begin = jnp.zeros((rows, LANES), jnp.int32)
    start = jnp.int32(0)
    for k in range(lengths.shape[1] - 1):
        start = start + lengths[0, k]
        begin = jnp.where(spots >= start, start, begin)
    return spots - begin


def each(count, body):
    def step(i, _):
        body(i)
        return 0

    lax.fori_loop(0, count, step, 0)


def half_parts(q):
    return range(q * PARTS // 2, (q + 1) * PARTS // 2)


def line_place():
    return lax.axis_index("head"), lax.axis_size("head")


def peers(axis):
    n = lax.axis_size(axis)
    return [lax.rem(lax.axis_index(axis) + k, n) for k in range(1, n)]


def far_peer(axis):
    return lax.axis_size(axis) - 1 - lax.axis_index(axis)


def far_copies(terms, far_terms, sems):
    far = far_peer("dp")
    return [
        pltpu.make_async_remote_copy(
            src_ref=terms.at[far, k],
            dst_ref=far_terms.at[k],
            send_sem=sems.at[0, k],
            recv_sem=sems.at[1, k],
            device_id={"dp": far},
            device_id_type=pl.DeviceIdType.MESH,
        )
        for k in range(far_terms.shape[0])
    ]


def near_copies(terms, near_terms, last_terms, sems):
    n, me, far = lax.axis_size("dp"), lax.axis_index("dp"), far_peer("dp")
    for k in range(n - 2):
        peer = k + jnp.where(k >= jnp.minimum(me, far), 1, 0)
        peer = peer + jnp.where(k + 1 >= jnp.maximum(me, far), 1, 0)
        slot = me - jnp.where(peer < me, 1, 0) - jnp.where(n - 1 - peer < me, 1, 0)
        yield pltpu.make_async_remote_copy(
            src_ref=terms.at[peer],
            dst_ref=near_terms.at[slot],
            send_sem=sems.at[0, k],
            recv_sem=sems.at[1, slot],
            device_id={"dp": peer},
            device_id_type=pl.DeviceIdType.MESH,
        )
    yield pltpu.make_async_remote_copy(
        src_ref=terms.at[far, 2],
        dst_ref=last_terms,
        send_sem=sems.at[0, n - 2],
        recv_sem=sems.at[1, n - 2],
        device_id={"dp": far},
        device_id_type=pl.DeviceIdType.MESH,
    )


def near_arrive(near_terms, last_terms, sems):
    for k in range(near_terms.shape[0]):
        pltpu.make_async_copy(near_terms.at[k], near_terms.at[k], sems.at[1, k]).wait()
    pltpu.make_async_copy(last_terms, last_terms, sems.at[1, near_terms.shape[0]]).wait()


def peer_barrier(axes):
    barrier = pltpu.get_barrier_semaphore()
    count = 0
    for axis in axes:
        for peer in peers(axis):
            pl.semaphore_signal(
                barrier, inc=1, device_id={axis: peer}, device_id_type=pl.DeviceIdType.MESH
            )
            count += 1
    pl.semaphore_wait(barrier, count)


def wait_neighbours(sem, j, n):
    inside = (j > 0) & (j < n - 1)

    @pl.when(inside)
    def _():
        pl.semaphore_wait(sem, 2)

    @pl.when(jnp.logical_not(inside))
    def _():
        pl.semaphore_wait(sem, 1)


def line_barrier(j, n):
    barrier = pltpu.get_barrier_semaphore()
    for side in (-1, 1):

        @pl.when((j + side >= 0) & (j + side < n))
        def _():
            pl.semaphore_signal(
                barrier, inc=1, device_id={"head": j + side}, device_id_type=pl.DeviceIdType.MESH
            )

    wait_neighbours(barrier, j, n)


class Gather:
    def __init__(self, j, n, buf, send, recv):
        self.j, self.n, self.buf, self.send, self.recv = j, n, buf, send, recv
        self.span = buf.shape[1] // PARTS

    def copy(self, block, s, side, source=None):
        part = pl.ds(s * self.span, self.span)
        target = self.buf.at[block, part]
        return pltpu.make_async_remote_copy(
            src_ref=target if source is None else source.at[part],
            dst_ref=target,
            send_sem=self.send.at[(side + 1) // 2, block, s],
            recv_sem=self.recv.at[block, s],
            device_id={"head": self.j + side},
            device_id_type=pl.DeviceIdType.MESH,
        )

    def there(self, side):
        return (self.j + side >= 0) & (self.j + side < self.n)

    def flows(self, t):
        for side in (1, -1):
            block = self.j - side * t
            yield side, block, (block >= 0) & (block < self.n)

    def start(self, source, parts=range(PARTS)):
        for s in parts:
            for side in (1, -1):

                @pl.when(self.there(side))
                def _():
                    self.copy(self.j, s, side, source).start()

    def step(self, t, parts=range(PARTS)):
        for s in parts:
            for side, block, live in self.flows(t):

                @pl.when(live)
                def _():
                    self.copy(block, s, -side).wait_recv()

                @pl.when(live & self.there(side))
                def _():
                    self.copy(block, s, side).start()

    def finish(self, parts=range(PARTS)):
        def drain(t):
            for s in parts:
                for side, block, live in self.flows(t):

                    @pl.when(live & self.there(side))
                    def _():
                        self.copy(block, s, side).wait_send()

        each(self.n, drain)


class Scatter:
    def __init__(self, j, n, own, held, send, recv, last=2):
        self.j, self.n, self.own, self.held, self.send, self.recv = j, n, own, held, send, recv
        self.span = own.shape[1] // PARTS
        self.ends = (j, n)
        self.spot = last
        self.compact = own.shape[0] != n

    def place(self, block, side):
        return block if not self.compact else (1 - side) // 2

    def last(self):
        return self.j if not self.compact else self.spot

    def rows(self, s):
        return pl.ds(s * self.span, self.span)

    def slot(self, block, side, at):
        return block if side == 1 else jnp.where(block == at, self.n, block)

    def arrival(self, slot, s):
        return pltpu.make_async_copy(
            self.held.at[slot, self.rows(s)], self.held.at[slot, self.rows(s)], self.recv.at[slot, s]
        )

    def flows(self, t):
        for side in (1, -1):
            lag = self.j if side == 1 else self.n - 1 - self.j
            block = self.n - 1 - (t - lag) if side == 1 else t - lag
            yield side, block, (t >= lag) & (t <= self.n - 2)

    def copy(self, source, block, s, side):
        slot = self.slot(block, side, self.j + side)
        return pltpu.make_async_remote_copy(
            src_ref=source.at[block, self.rows(s)],
            dst_ref=self.held.at[slot, self.rows(s)],
            send_sem=self.send.at[block, s],
            recv_sem=self.recv.at[slot, s],
            device_id={"head": self.j + side},
            device_id_type=pl.DeviceIdType.MESH,
        )

    def step(self, t, parts=range(PARTS)):
        for s in parts:
            for side, block, live in self.flows(t):
                behind = (self.j - side >= 0) & (self.j - side < self.n)

                @pl.when(live & jnp.logical_not(behind))
                def _():
                    if self.compact:
                        self.held[block, self.rows(s), :] = self.own[
                            self.place(block, side), self.rows(s), :
                        ]
                        self.copy(self.held, block, s, side).start()
                    else:
                        self.copy(self.own, block, s, side).start()

                @pl.when(live & behind)
                def _():
                    self.arrival(block, s).wait()
                    self.add(block, s, side)
                    self.copy(self.held, block, s, side).start()

    def add(self, block, s, side):
        def add_rows(i):
            rows = pl.ds(pl.multiple_of(s * self.span + i * STRIP, STRIP), STRIP)
            total = self.own[self.place(block, side), rows, :].astype(jnp.float32) + self.held[
                block, rows, :
            ].astype(jnp.float32)
            self.held[block, rows, :] = total.astype(jnp.bfloat16)

        each(self.span // STRIP, add_rows)

    def arrive(self, parts=range(PARTS)):
        for s in parts:

            @pl.when(self.j > 0)
            def _():
                self.arrival(self.ends[0], s).wait()

            @pl.when(self.j < self.n - 1)
            def _():
                self.arrival(self.ends[1], s).wait()

    def result(self, rows):
        total = self.own[self.last(), rows, :].astype(jnp.float32)
        left = self.held[self.ends[0], rows, :].astype(jnp.float32)
        right = self.held[self.ends[1], rows, :].astype(jnp.float32)
        total = total + jnp.where(self.j > 0, left, 0.0)
        return total + jnp.where(self.j < self.n - 1, right, 0.0)

    def finish(self):
        def drain(t):
            for s in range(PARTS):
                for side, block, live in self.flows(t):

                    @pl.when(live)
                    def _():
                        self.copy(self.held, block, s, side).wait_send()

        each(self.n - 1, drain)


class Share:
    def __init__(self, axis, slots, send, recv):
        self.axis, self.slots, self.send, self.recv = axis, slots, send, recv
        self.me = lax.axis_index(axis)

    def copy(self, slot, peer, source=None):
        return pltpu.make_async_remote_copy(
            src_ref=self.slots.at[slot] if source is None else source,
            dst_ref=self.slots.at[slot],
            send_sem=self.send.at[peer],
            recv_sem=self.recv.at[slot],
            device_id={self.axis: peer},
            device_id_type=pl.DeviceIdType.MESH,
        )

    def start(self, sources=None):
        for peer in peers(self.axis):
            source = None if sources is None else sources.at[peer]
            self.copy(self.me, peer, source).start()

    def arrive(self):
        for peer in peers(self.axis):
            self.copy(peer, peer).wait_recv()

    def finish(self):
        for peer in peers(self.axis):
            self.copy(self.me, peer).wait_send()


def share_sems(axis):
    n = lax.axis_size(axis)
    return [pltpu.SemaphoreType.DMA((n,)), pltpu.SemaphoreType.DMA((n,))]


class Sum:
    def __init__(self, terms, slots, total, sems):
        self.terms, self.slots, self.total = terms, slots, total
        self.parts = Share("dp", slots, sems[0], sems[1])
        self.whole = Share("dp", total, sems[2], sems[3])
        self.me, self.sem = self.parts.me, sems[4]

    def start(self):
        self.parts.start(self.terms)

    def keep(self):
        return pltpu.make_async_copy(self.slots.at[self.me], self.total.at[self.me], self.sem)

    def spread(self):
        self.parts.arrive()
        rows = self.slots.shape[1]

        def add(part):
            value = jnp.zeros((STRIP, self.slots.shape[2]), jnp.float32)
            for i in range(self.slots.shape[0]):
                mine = self.terms[i, part, :].astype(jnp.float32)
                other = self.slots[i, part, :].astype(jnp.float32)
                value = value + jnp.where(self.me == i, mine, other)
            self.slots[self.me, part, :] = value.astype(jnp.bfloat16)

        strips(rows, add)
        for peer in peers("dp"):
            self.whole.copy(self.me, peer, self.slots.at[self.me]).start()
        self.keep().start()

    def finish(self):
        self.whole.arrive()
        self.keep().wait()
        self.parts.finish()
        self.whole.finish()


def sum_sems():
    return [*share_sems("dp"), *share_sems("dp"), pltpu.SemaphoreType.DMA]


def gather_sems(n):
    return [pltpu.SemaphoreType.DMA((2, n, PARTS)), pltpu.SemaphoreType.DMA((n, PARTS))]


def scatter_sems(n):
    return [pltpu.SemaphoreType.DMA((n, PARTS)), pltpu.SemaphoreType.DMA((n + 1, PARTS))]


def line_call(kernel, ident, name, out_shape, in_specs, out_specs, scratch, cost=None):
    return pl.pallas_call(
        kernel,
        out_shape=out_shape,
        in_specs=in_specs,
        out_specs=out_specs,
        scratch_shapes=scratch,
        compiler_params=pltpu.CompilerParams(
            collective_id=ident, has_side_effects=True, vmem_limit_bytes=VMEM_BYTES
        ),
        name=name,
    )


STRIP = 16


def strips(rows, body, first=0):
    each(rows // STRIP, lambda i: body(pl.ds(pl.multiple_of(first + i * STRIP, STRIP), STRIP)))


def front_kernel(
    lengths, stream, premix, wb, wi, wo_in, wg, par, preffn, cot,
    rows_out, pre_out, saved, gated_out, wbi_out, wo_out, cot_rows, hidden, low_out,
    normed, rows, wbi, wo, pre, gated, stage, z, carry, own, held, raw,
    gsend, grecv, csend, crecv, send, recv, keep_sem, pre_sem, stage_sem, one_sem, raw_sem,
):
    j, n = line_place()
    f32, bf16 = jnp.float32, jnp.bfloat16
    local, depth = stream.shape
    width, chans = gated.shape[1], wb.shape[0]
    tiles = width // LANES
    loads = [
        pltpu.make_async_copy(source, raw.at[k], raw_sem.at[k])
        for k, source in enumerate((wb, wi, wo_in))
    ]
    for load in loads:
        load.start()
    line_barrier(j, n)

    def norm(part):
        _, unit = rms_parts(stream[part, :].astype(f32))
        normed[part, :] = (unit * premix[...]).astype(bf16)

    strips(local, norm)
    gather = Gather(j, n, rows, gsend, grecv)
    gather.start(normed)
    for k, (target, first) in enumerate(((wbi, 0), (wbi, width), (wo, 0))):
        loads[k].wait()
        whole = chans // STRIP * STRIP
        target[first + whole : first + width, :] = jnp.zeros((width - whole, depth), bf16)
        target[first : first + chans, :] = raw[k]
    out_copies = [
        pltpu.make_async_copy(wbi, wbi_out, one_sem.at[0]),
        pltpu.make_async_copy(wo, wo_out, one_sem.at[1]),
    ]
    for copy in out_copies:
        copy.start()

    def span(block):
        return pl.ds(pl.multiple_of(block * local, local), local)

    def shifted(block):
        return pl.ds(pl.multiple_of(block * local + HALO, HALO), local)

    def keep(source, block):
        return pltpu.make_async_copy(source, rows_out.at[block], keep_sem.at[block])

    def keep_pre(block):
        return pltpu.make_async_copy(
            pre.at[shifted(block)], pre_out.at[span(block)], pre_sem.at[block]
        )

    pre[0:HALO, :] = jnp.zeros((HALO, 2 * width), f32)
    keep(normed, j).start()
    pre[shifted(j), :] = contract_cols(normed[...], wbi[...])
    keep_pre(j).start()

    def visit(v):
        t = v // 2 + 1
        block = jnp.where(v % 2 == 0, j - t, j + t)

        @pl.when(v % 2 == 0)
        def _():
            gather.step(t)

        @pl.when((block >= 0) & (block < n))
        def _():
            keep(rows.at[block], block).start()
            pre[shifted(block), :] = contract_cols(rows[block], wbi[...])
            keep_pre(block).start()

    each(2 * (n - 1), visit)
    cots = Gather(j, n, cot_rows, csend, crecv)
    cots.start(cot)
    mine = pltpu.make_async_copy(cot, cot_rows.at[j], one_sem.at[2])
    mine.start()

    carry[...] = jnp.zeros_like(carry)
    count = n * local // CHUNK

    def keep_stage(i):
        return pltpu.make_async_copy(
            stage.at[lax.rem(i, 2)],
            saved.at[pl.ds(pl.multiple_of(i * CHUNK, CHUNK), CHUNK)],
            stage_sem.at[lax.rem(i, 2)],
        )

    def chunk(i):
        first = i * CHUNK

        @pl.when(i >= 2)
        def _():
            keep_stage(i - 2).wait()

        u_out, r_out, e_out, h_out = (
            stage.at[lax.rem(i, 2), :, k * width : (k + 1) * width] for k in range(SAVED)
        )

        def conv_step(b):
            row = pl.multiple_of(b * BLOCK, BLOCK)
            halo = pl.ds(pl.multiple_of(first + row, BLOCK), BLOCK + HALO)
            place = doc_places(lengths, first + row, BLOCK)
            for t in range(tiles):
                cols = pl.ds(t * LANES, LANES)
                xs = pre[halo, pl.ds(width + t * LANES, LANES)]
                total = par[BIAS : BIAS + 1, cols] + par[TAP : TAP + 1, cols] * xs[HALO:]
                for k in range(1, CONVW):
                    term = par[TAP + k : TAP + k + 1, cols] * xs[HALO - k : HALO - k + BLOCK]
                    total = total + jnp.where(place >= k, term, 0.0)
                u_out[pl.ds(row, BLOCK), cols] = total

        each(CHUNK // BLOCK, conv_step)
        z[...] = jnp.dot(u_out[...].astype(bf16), wg[...], preferred_element_type=f32)

        def scan_step(b):
            row = pl.multiple_of(b * BLOCK, BLOCK)
            part = pl.ds(row, BLOCK)
            spot = pl.ds(pl.multiple_of(first + row, BLOCK), BLOCK)
            here = pl.ds(pl.multiple_of(first + row + HALO, HALO), BLOCK)
            fresh = doc_places(lengths, first + row, BLOCK) == 0
            inner = lax.broadcasted_iota(jnp.int32, (BLOCK, LANES), 0) % 8
            for t in range(tiles):
                cols = pl.ds(t * LANES, LANES)
                other = pl.ds(width + t * LANES, LANES)
                r = jax.nn.sigmoid(z[part, cols] + par[RATE_B : RATE_B + 1, cols])
                e = jax.nn.sigmoid(z[part, other] + par[ENTRY_B : ENTRY_B + 1, cols])
                u = u_out[part, cols]
                c, m, _ = decay_terms(r, par[DECAY : DECAY + 1, cols], fresh)
                r_out[part, cols] = r
                e_out[part, cols] = e
                b_ = m * e * u
                for d in (1, 2, 4):
                    near = inner >= d
                    b_ = b_ + c * jnp.where(near, pltpu.roll(b_, d, 0), 0.0)
                    c = c * jnp.where(near, pltpu.roll(c, d, 0), 1.0)
                last = carry[0:1, cols]
                pieces = []
                for g in range(BLOCK // 8):
                    eight = slice(g * 8, g * 8 + 8)
                    state = b_[eight] + c[eight] * last
                    last = state[7:8]
                    pieces.append(state)
                carry[0:1, cols] = last
                h = jnp.concatenate(pieces, axis=0)
                h_out[part, cols] = h
                gated[spot, cols] = (h * gelu(pre[here, cols])).astype(bf16)

        each(CHUNK // BLOCK, scan_step)
        keep_stage(i).start()

        @pl.when(i == count * 5 // 8)
        def _():
            cots.step(1)

    each(count, chunk)
    keep_gated = pltpu.make_async_copy(gated, gated_out, one_sem.at[3])
    keep_gated.start()

    scatter = Scatter(j, n, own, held, send, recv)

    def compute(block, slot):
        own[slot] = jnp.dot(
            gated[span(block), :], wo[...], preferred_element_type=f32
        ).astype(bf16)

    def ahead(t):
        for side, block, live in scatter.flows(t):
            pl.when(live)(functools.partial(compute, block, scatter.place(block, side)))

    ahead(0)

    def step(t):
        scatter.step(t)
        ahead(t + 1)

        @pl.when(t == 0)
        def _():
            compute(j, 2)

        @pl.when(t + 2 < n)
        def _():
            cots.step(t + 2)

    each(n - 1, step)
    scatter.arrive()

    def settle(part):
        total = stream[part, :].astype(f32) + scatter.result(part)
        hidden[part, :] = total
        _, unit = rms_parts(total)
        low_out[part, :] = (unit * preffn[...]).astype(bf16)

    strips(local, settle)
    scatter.finish()
    gather.finish()
    cots.finish()
    mine.wait()
    keep_gated.wait()
    for copy in out_copies:
        copy.wait()
    keep(normed, j).wait()
    keep_pre(j).wait()
    for k in range(1, n):
        other = lax.rem(j + k, n)
        keep(rows.at[other], other).wait()
        keep_pre(other).wait()
    for i in range(max(count - 2, 0), count):
        keep_stage(i).wait()


def mixer_front(lengths, stream, premix, wb, wi, wo, wg, par, preffn, cot):
    n = lax.axis_size("head")
    local, depth = stream.shape
    width, tokens = wg.shape[0], n * local
    f32, bf16 = jnp.float32, jnp.bfloat16
    shape, vmem, dma = jax.ShapeDtypeStruct, pltpu.VMEM, pltpu.SemaphoreType.DMA
    return line_call(
        front_kernel, 0, "mixer_front",
        (
            shape((n, local, depth), bf16),
            shape((tokens, 2 * width), f32),
            shape((tokens, SAVED * width), f32),
            shape((tokens, width), bf16),
            shape((2 * width, depth), bf16),
            shape((width, depth), bf16),
            shape((n, local, depth), bf16),
            shape((local, depth), f32),
            shape((local, depth), bf16),
        ),
        [IN_SMEM, IN_VMEM, IN_VMEM, IN_ANY, IN_ANY, IN_ANY, *[IN_VMEM] * 4],
        [IN_ANY] * 7 + [IN_VMEM] * 2,
        [
            vmem((local, depth), bf16),
            vmem((n, local, depth), bf16),
            vmem((2 * width, depth), bf16),
            vmem((width, depth), bf16),
            vmem((HALO + tokens, 2 * width), f32),
            vmem((tokens, width), bf16),
            vmem((2, CHUNK, SAVED * width), f32),
            vmem((CHUNK, 2 * width), f32),
            vmem((8, width), f32),
            vmem((3, local, depth), bf16),
            vmem((n + 1, local, depth), bf16),
            vmem((3, wb.shape[0], depth), bf16),
            *gather_sems(n),
            *gather_sems(n),
            *scatter_sems(n),
            dma((n,)),
            dma((n,)),
            dma((2,)),
            dma((4,)),
            dma((3,)),
        ],
    )(lengths, stream, premix, wb, wi, wo, wg, par, preffn, cot)


def ffn_kernel(
    low, cot_rows, cot_in, hidden_in, gain, wg_in, wu_in, wd_in,
    out_part, terms, far_terms, resid, resid_low, gain_grad,
    rows, cot_pair, kept, own, held, stage, wstage, cot_cols, wg, wu, wd, cot, hidden,
    gsend, grecv, send, recv, cot_sem, out_sem, col_sem, term_sem, far_sem, load_sem,
):
    j, n = line_place()
    peer_barrier(("head", "dp"))
    f32, bf16 = jnp.float32, jnp.bfloat16
    local, depth = low.shape
    units = wg.shape[1]
    half = local // 2
    fstep = 256 if units % 256 == 0 else LANES
    dstep = 512
    gather = Gather(j, n, rows, gsend, grecv)
    scatter = Scatter(j, n, own, held, send, recv)
    gather.start(low, half_parts(0))
    loads = [
        pltpu.make_async_copy(a, b, load_sem.at[k])
        for k, (a, b) in enumerate(
            ((wg_in, wg), (wu_in, wu), (wd_in, wd), (cot_in, cot), (hidden_in, hidden))
        )
    ]
    for load in loads:
        load.start()
    rows[j] = low[...]
    for load in loads:
        load.wait()

    def pair(chip, q):
        return pl.ds(pl.multiple_of(2 * chip, 2), 2), pl.ds(q * half, half)

    def fetch(chip, q):
        return pltpu.make_async_copy(cot_rows.at[pair(chip, q)], cot_pair, cot_sem)

    def put(chip, q):
        return pltpu.make_async_copy(stage, out_part.at[pair(chip, q)], out_sem)

    def pair_work(chip, q):
        spot = pair(chip, q)

        def flat(v):
            return v.reshape(2 * half, v.shape[-1])

        def fold(v):
            return v.astype(bf16).reshape(2, half, v.shape[-1])

        for f in range(0, units, fstep):
            cols = slice(f, f + fstep)
            gate = jnp.dot(flat(rows[spot]), wg[:, cols], preferred_element_type=f32)
            act, slope = gelu_pair(gate)
            up = jnp.dot(flat(rows[spot]), wu[:, cols], preferred_element_type=f32)
            kept[2, *spot, cols] = fold(act * up)
            grad = jnp.dot(flat(cot_pair[...]), wd[:, cols], preferred_element_type=f32)
            kept[0, *spot, cols] = fold(grad * up * slope)
            kept[1, *spot, cols] = fold(grad * act)
        for d in range(0, depth, dstep):
            cols = slice(d, d + dstep)
            own[*spot, cols] = fold(
                contract_cols(flat(kept[0, *spot]), wg[cols, :])
                + contract_cols(flat(kept[1, *spot]), wu[cols, :])
            )
            stage[:, :, cols] = fold(contract_cols(flat(kept[2, *spot]), wd[cols, :]))

    def gather_half(q):
        def visit(i):
            t = i + 1
            reach = t // 2
            chip = j // 2 + jnp.where((t + j) % 2 == 0, -reach, reach)
            live = (chip >= 0) & (chip < n // 2)

            @pl.when(live)
            def _():
                fetch(chip, q).start()

            gather.step(t, half_parts(q))
            if q:
                scatter.step(t - 1, half_parts(0))

            @pl.when(live)
            def _():
                fetch(chip, q).wait()

                @pl.when((t > 1) | (q > 0))
                def _():
                    put(chip, q).wait()

                pair_work(chip, q)
                put(chip, q).start()

        each(n - 1, visit)

    gather_half(0)
    gather.start(low, half_parts(1))
    gather_half(1)
    put(j // 2, 1).wait()

    width = depth // n
    per = depth // terms.shape[0] // width

    far = far_peer("dp")

    def columns(b):
        return pl.ds(pl.multiple_of(lax.rem(b + far * per, n) * width, width), width)

    def take(b):
        return pltpu.make_async_copy(cot_rows.at[:, :, columns(b)], cot_cols, col_sem)

    def give(b):
        owner = lax.rem(b // per + far, n // per)
        spot = pl.ds(pl.multiple_of(lax.rem(b, per) * width, width), width)
        return pltpu.make_async_copy(wstage, terms.at[owner, :, spot, :], term_sem)

    def weights(b):
        xs = rows[:, :, columns(b)].reshape(n * local, width)
        take(b).wait()

        @pl.when(b > 0)
        def _():
            give(b).wait()

        @pl.when(b == per)
        def _():
            for copy in far_copies(terms, far_terms, far_sem):
                copy.start()

        for k, lead in ((0, xs), (1, xs), (2, cot_cols[...].reshape(n * local, width))):
            wstage[k] = contract_rows(lead, kept[k].reshape(n * local, units)).astype(bf16)
        give(b).start()

        @pl.when(b + 1 < n)
        def _():
            take(b + 1).start()

    take(0).start()

    def step(t):
        pl.when(t < n - 1)(lambda: scatter.step(t, half_parts(1)))
        weights(t)

    each(n, step)
    scatter.arrive()
    gain_grad[...] = jnp.zeros_like(gain_grad)

    def settle(part):
        rinv, u = rms_parts(hidden[part, :])
        grad = scatter.result(part)
        gain_grad[...] += jnp.sum(grad * u, axis=0, keepdims=True)
        total = cot[part, :].astype(f32) + norm_back(u, rinv, gain[...], grad)
        resid[part, :] = total
        resid_low[part, :] = total.astype(bf16)

    strips(local, settle)
    give(0).wait()
    gather.finish()
    scatter.finish()
    for copy in far_copies(terms, far_terms, far_sem):
        copy.wait()


def feed_forward(low, cot_rows, cot, hidden, gain, wg, wu, wd):
    n, group = lax.axis_size("head"), lax.axis_size("dp")
    local, depth = low.shape
    units = wg.shape[1]
    bf16 = jnp.bfloat16
    shape, vmem = jax.ShapeDtypeStruct, pltpu.VMEM
    pair = (2, local // 2, depth)
    return line_call(
        ffn_kernel, 2, "feed_forward",
        (
            shape((n, local, depth), bf16),
            shape((group, 3, depth // group, units), bf16),
            shape((FAR_TERMS, depth // group, units), bf16),
            shape((local, depth), jnp.float32),
            shape((local, depth), bf16),
            shape((1, depth), jnp.float32),
        ),
        [IN_VMEM, IN_ANY, IN_ANY, IN_ANY, IN_VMEM, IN_ANY, IN_ANY, IN_ANY],
        [IN_ANY, IN_ANY, IN_ANY, IN_VMEM, IN_VMEM, IN_VMEM],
        [
            vmem((n, local, depth), bf16),
            vmem(pair, bf16),
            vmem((3, n, local, units), bf16),
            vmem((n, local, depth), bf16),
            vmem((n + 1, local, depth), bf16),
            vmem(pair, bf16),
            vmem((3, depth // n, units), bf16),
            vmem((n, local, depth // n), bf16),
            *[vmem(wg.shape, bf16)] * 3,
            vmem((local, depth), bf16),
            vmem((local, depth), jnp.float32),
            *gather_sems(n),
            *scatter_sems(n),
            *[pltpu.SemaphoreType.DMA] * 4,
            pltpu.SemaphoreType.DMA((2, FAR_TERMS)),
            pltpu.SemaphoreType.DMA((5,)),
        ],
    )(low, cot_rows, cot, hidden, gain, wg, wu, wd)


def back_kernel(
    lengths, low, out_part, hidden, terms, gated, wo_in, wbi_in, wg, par, pre, saved,
    normed_rows, stream_in, gain, resid, preffn_grad,
    layer_out, sums, last_terms, stream_grad, ob_total, i_total, g_total, par_grad, gains,
    rows, own, held, wo, wbi, dh, dpre, acc, dgate, dz, du, carry, dpar,
    unit_bp, unit_h, unit_gated, unit_normed,
    obterms, obslots, iterms, islots, gterms, gslots, pslots, dslots, hslots,
    gsend, grecv, send4, recv4, send8, recv8, tsems, unit_sem, own_sem, chunk_sem,
    row_sem, wide_sem, load_sem, free, psend, precv, dsend, drecv, hsend, hrecv, *sems,
):
    j, n = line_place()
    f32, bf16 = jnp.float32, jnp.bfloat16
    local, depth = low.shape
    width = dh.shape[1]
    tiles = width // LANES
    stream, wide = unit_normed, acc.at[width : width + local]
    loads = [
        pltpu.make_async_copy(a, b, load_sem.at[k])
        for k, (a, b) in enumerate(((wo_in, wo), (wbi_in, wbi), (stream_in, stream)))
    ]
    for load in loads[:2]:
        load.start()
    peer_barrier(("head", "dp"))
    gather = Gather(j, n, rows, gsend, grecv)
    gather.start(low)
    for copy in near_copies(terms, sums, last_terms, tsems):
        copy.start()
    rows[j] = low[...]
    outs = Scatter(j, n, own, held, send4, recv4)
    acc[...] = jnp.zeros_like(acc)

    def fetch_out(block, slot):
        return pltpu.make_async_copy(out_part.at[block], own.at[slot], own_sem.at[slot])

    def outs_ahead(t):
        for start in (True, False):
            for side, block, live in outs.flows(t):
                copy = fetch_out(block, outs.place(block, side))
                pl.when(live)(copy.start if start else copy.wait)

    def outs_step(t):
        outs.step(t)
        outs_ahead(t + 1)

    def outs_slot(slot):
        t = slot - 1 - LAG

        @pl.when((t >= 0) & (t < n - 1))
        def _():
            outs_step(t)

    outs_ahead(0)
    fetch_out(j, 2).start()
    fetch_out(j, 2).wait()

    def unit_copies(block):
        span = pl.ds(pl.multiple_of(block * local, local), local)
        return (
            pltpu.make_async_copy(pre.at[span, 0:width], unit_bp, unit_sem.at[0]),
            pltpu.make_async_copy(
                saved.at[span, 3 * width : 4 * width], unit_h, unit_sem.at[1]
            ),
            pltpu.make_async_copy(gated.at[span], unit_gated, unit_sem.at[2]),
            pltpu.make_async_copy(normed_rows.at[block], unit_normed, unit_sem.at[3]),
        )

    def unit(block):
        span = pl.ds(pl.multiple_of(block * local, local), local)
        dh[span, :] = contract_cols(rows[block], wo[...])

        def act(i):
            part = pl.ds(pl.multiple_of(i * BLOCK, BLOCK), BLOCK)
            spot = pl.ds(pl.multiple_of(block * local + i * BLOCK, BLOCK), BLOCK)
            for t in range(tiles):
                cols = pl.ds(t * LANES, LANES)
                grad = dh[spot, cols]
                value, slope = gelu_pair(unit_bp[part, cols])
                dpre[spot, cols] = (grad * unit_h[part, cols] * slope).astype(bf16)
                dh[spot, cols] = grad * value

        each(local // BLOCK, act)
        acc[0:width, :] += contract_rows(unit_gated[...], rows[block])
        acc[width : 2 * width, :] += contract_rows(dpre[span, 0:width], unit_normed[...])

    def visit(v):
        t = (v + 1) // 2
        block = jnp.where(v % 2 == 1, j - t, j + t)
        live = (block >= 0) & (block < n)

        @pl.when(live)
        def _():
            for copy in unit_copies(block):
                copy.start()

        @pl.when(v % 2 == 1)
        def _():
            gather.step(t)
            outs_slot(t)

        @pl.when(live)
        def _():
            for copy in unit_copies(block):
                copy.wait()
            unit(block)

    loads[0].wait()
    each(2 * n - 1, visit)
    gather.finish()
    for side in (-1, 1):

        @pl.when((j + side >= 0) & (j + side < n))
        def _():
            pl.semaphore_signal(
                free, inc=1, device_id={"head": j + side}, device_id_type=pl.DeviceIdType.MESH
            )

    def pack(target, source, count):
        span = target.shape[1]

        def strip(i):
            row = pl.multiple_of(i * STRIP, STRIP)
            target[row // span, pl.ds(pl.multiple_of(lax.rem(row, span), STRIP), STRIP), :] = source[
                pl.ds(row, STRIP), :
            ].astype(bf16)

        each(count // STRIP, strip)

    obsum = Sum(obterms, obslots, ob_total, sems[0:5])
    isum = Sum(iterms, islots, i_total, sems[5:10])
    gsum = Sum(gterms, gslots, g_total, sems[10:15])
    pack(obterms, acc, 2 * width)
    obsum.start()
    loads[2].start()

    count = n * local // CHUNK

    def chunk_copies(i):
        base = lax.rem(i, 2) * (CHUNK + HALO)
        start = pl.multiple_of(i * CHUNK, CHUNK)
        ahead = pl.multiple_of(jnp.maximum(start - HALO, 0), HALO)
        halo, main = pl.ds(pl.multiple_of(base, HALO), HALO), pl.ds(
            pl.multiple_of(base + HALO, HALO), CHUNK
        )
        kept, x = slice(0, SAVED * width), slice(SAVED * width, (SAVED + 1) * width)
        pairs = (
            (saved.at[pl.ds(ahead, HALO)], acc.at[halo, kept]),
            (saved.at[pl.ds(start, CHUNK)], acc.at[main, kept]),
            (pre.at[pl.ds(ahead, HALO), width : 2 * width], acc.at[halo, x]),
            (pre.at[pl.ds(start, CHUNK), width : 2 * width], acc.at[main, x]),
        )
        return [
            pltpu.make_async_copy(a, b, chunk_sem.at[lax.rem(i, 2), k])
            for k, (a, b) in enumerate(pairs)
        ]

    def total(v):
        return jnp.sum(v, axis=0, keepdims=True)

    for copy in chunk_copies(count - 1):
        copy.start()
    du[...] = jnp.zeros_like(du)
    carry[...] = jnp.zeros_like(carry)
    dgate[...] = jnp.zeros_like(dgate)
    dpar[...] = jnp.zeros_like(dpar)

    def chunk(k):
        i = count - 1 - k

        @pl.when(i > 0)
        def _():
            for copy in chunk_copies(i - 1):
                copy.start()

        for copy in chunk_copies(i):
            copy.wait()
        base = lax.rem(i, 2) * (CHUNK + HALO)
        first = i * CHUNK
        du[CHUNK:, :] = du[0:HALO, :]

        def scan_step(b):
            row = pl.multiple_of(CHUNK - BLOCK - b * BLOCK, BLOCK)
            part = pl.ds(row, BLOCK)
            spot = pl.ds(pl.multiple_of(first + row, BLOCK), BLOCK)
            here = pl.ds(pl.multiple_of(base + HALO + row, HALO), BLOCK)
            halo = pl.ds(pl.multiple_of(base + row, HALO), BLOCK + HALO)
            fresh = doc_places(lengths, first + row, BLOCK) == 0
            place = lax.broadcasted_iota(jnp.int32, (BLOCK, LANES), 0)
            inner = place % 8
            for t in range(tiles):
                cols = pl.ds(t * LANES, LANES)
                u, r, e = (acc[here, pl.ds(m * width + t * LANES, LANES)] for m in range(3))
                prior = acc[halo, pl.ds(3 * width + t * LANES, LANES)][HALO - 1 : HALO - 1 + BLOCK]
                near_h = dh[spot, cols]
                decay = par[DECAY : DECAY + 1, cols]
                c, m, ratio = decay_terms(r, decay, fresh)
                b_, a_ = c * near_h, c
                for d in (1, 2, 4):
                    near_row = inner < 8 - d
                    b_ = b_ + a_ * jnp.where(near_row, pltpu.roll(b_, BLOCK - d, 0), 0.0)
                    a_ = a_ * jnp.where(near_row, pltpu.roll(a_, BLOCK - d, 0), 1.0)
                later = carry[0:1, cols]
                pieces = []
                front = later
                for g in reversed(range(BLOCK // 8)):
                    eight = slice(g * 8, g * 8 + 8)
                    state = b_[eight] + a_[eight] * front
                    front = state[0:1]
                    pieces.append(state)
                carry[0:1, cols] = front
                mu = jnp.concatenate(pieces[::-1], axis=0)
                adj = near_h + jnp.where(
                    place == BLOCK - 1, later, pltpu.roll(mu, BLOCK - 1, 0)
                )
                eu = e * u
                dlog = adj * (prior * c - eu * ratio)
                dpar[G_DECAY : G_DECAY + 1, cols] += total(dlog * r)
                dzr = decay * dlog * (r * (1.0 - r))
                dze = adj * m * eu * (1.0 - e)
                dpar[G_RATE : G_RATE + 1, cols] += total(dzr)
                dpar[G_ENTRY : G_ENTRY + 1, cols] += total(dze)
                dz[part, cols] = dzr.astype(bf16)
                dz[part, pl.ds(width + t * LANES, LANES)] = dze.astype(bf16)
                du[part, cols] = adj * m * e

        each(CHUNK // BLOCK, scan_step)
        u_chunk = acc[pl.ds(pl.multiple_of(base + HALO, HALO), CHUNK), 0:width]
        du[0:CHUNK, :] += contract_cols(dz[...], wg[...])
        dgate[...] += contract_rows(u_chunk.astype(bf16), dz[...])

        def conv_step(b):
            row = pl.multiple_of(b * BLOCK, BLOCK)
            spot = pl.ds(pl.multiple_of(first + row, BLOCK), BLOCK)
            halo = pl.ds(pl.multiple_of(base + row, HALO), BLOCK + HALO)
            place = doc_places(lengths, first + row, BLOCK + HALO)
            for t in range(tiles):
                cols = pl.ds(t * LANES, LANES)
                ds = du[pl.ds(row, BLOCK + HALO), cols]
                xs = acc[halo, pl.ds(SAVED * width + t * LANES, LANES)]
                mine = ds[0:BLOCK]
                dx = par[TAP : TAP + 1, cols] * mine
                dpar[G_BIAS : G_BIAS + 1, cols] += total(mine)
                dpar[G_TAP : G_TAP + 1, cols] += total(mine * xs[HALO:])
                for k in range(1, CONVW):
                    inside = jnp.where(place >= k, ds, 0.0)
                    dx = dx + par[TAP + k : TAP + k + 1, cols] * inside[k : k + BLOCK]
                    dpar[G_TAP + k : G_TAP + k + 1, cols] += total(
                        inside[0:BLOCK] * xs[HALO - k : HALO - k + BLOCK]
                    )
                dpre[spot, pl.ds(width + t * LANES, LANES)] = dx.astype(bf16)

        each(CHUNK // BLOCK, conv_step)
        pl.when(k % 2 == 0)(lambda: outs_slot(n + k // 2))

    each(count, chunk)
    for t in range(n - 1 - max(0, LAG - (count + 1) // 2), n - 1):
        outs_step(jnp.int32(t))
    pack(gterms, dgate, width)
    gsum.start()
    pshare = Share("dp", pslots, psend, precv)
    pslots[pshare.me] = dpar[...]
    pshare.start()
    load_hidden = pltpu.make_async_copy(hidden, wide, wide_sem.at[0])
    load_hidden.start()
    scatter = Scatter(j, n, own, rows, send8, recv8, last=3)
    loads[1].wait()
    loads[2].wait()

    def compute(block, slot):
        span = pl.ds(pl.multiple_of(block * local, local), local)
        own[slot] = jnp.dot(dpre[span, :], wbi[...], preferred_element_type=f32).astype(bf16)

    def ahead(t):
        for side, block, live in scatter.flows(t):
            pl.when(live)(functools.partial(compute, block, scatter.place(block, side)))

    ahead(0)
    wait_neighbours(free, j, n)
    scatter.step(0)
    ahead(1)
    obsum.spread()

    def settle_out(part):
        layer_out[part, :] = (wide[part, :] + outs.result(part)).astype(bf16)

    load_resid = pltpu.make_async_copy(resid, wide, wide_sem.at[1])

    def step(t):
        scatter.step(t)
        ahead(t + 1)

        @pl.when(t == OUT_AT)
        def _():
            outs.arrive()
            load_hidden.wait()
            strips(local, settle_out)
            outs.finish()
            load_resid.start()
            load.start()
            compute(j, 3)

        @pl.when(t == OUT_AT + 1)
        def _():
            load.wait()
            for c in range(0, width, LANES):
                acc[c : c + LANES, :] = contract_rows(
                    dpre[:, width + c : width + c + LANES],
                    held[0:n].reshape(n * local, depth),
                )
            pack(iterms, acc, width)
            isum.start()

        @pl.when(t == OUT_AT + 2)
        def _():
            gsum.spread()

    load = pltpu.make_async_copy(normed_rows, held.at[pl.ds(0, n)], row_sem)
    lax.fori_loop(1, n - 1, lambda t, _: (step(t), 0)[1], 0)
    isum.spread()
    scatter.arrive()
    load_resid.wait()
    gains[...] = jnp.zeros_like(gains)

    def settle(part):
        rinv, u = rms_parts(stream[part, :].astype(f32))
        grad = scatter.result(part)
        gains[0:1, :] += jnp.sum(grad * u, axis=0, keepdims=True)
        value = wide[part, :] + norm_back(u, rinv, gain[...], grad)
        stream_grad[part, :] = value.astype(bf16)

    strips(local, settle)

    gains[1:2, :] = preffn_grad[...]
    for axis, slots, ssem, rsem in (("dp", dslots, dsend, drecv), ("head", hslots, hsend, hrecv)):
        share = Share(axis, slots, ssem, rsem)
        slots[share.me] = gains[...]
        share.start()
        share.arrive()
        value = slots[0]
        for i in range(1, slots.shape[0]):
            value = value + slots[i]
        gains[...] = value
        share.finish()

    pshare.arrive()
    value = pslots[0]
    for i in range(1, pslots.shape[0]):
        value = value + pslots[i]
    par_grad[...] = value
    pshare.finish()
    for one in (gsum, obsum, isum):
        one.finish()
    scatter.finish()
    for copy in near_copies(terms, sums, last_terms, tsems):
        copy.wait_send()
    near_arrive(sums, last_terms, tsems)


def mixer_back(
    lengths, low, out_part, hidden, terms, gated, wo, wbi, wg, par, pre, saved,
    normed_rows, stream, gain, resid, preffn_grad,
):
    n, group = lax.axis_size("head"), lax.axis_size("dp")
    local, depth = stream.shape
    width, tokens = wo.shape[0], pre.shape[0]
    f32, bf16 = jnp.float32, jnp.bfloat16
    ob = (group, 2 * width // group, depth)
    one = (group, width // group, depth)
    gate = (group, width // group, 2 * width)
    dma = pltpu.SemaphoreType.DMA
    shape = jax.ShapeDtypeStruct
    return line_call(
        back_kernel, 3, "mixer_back",
        (
            shape((local, depth), bf16),
            shape((group - 2, *terms.shape[1:]), bf16),
            shape(terms.shape[2:], bf16),
            shape((local, depth), bf16),
            shape(ob, bf16),
            shape(one, bf16),
            shape(gate, bf16),
            shape((PARAMS, width), f32),
            shape((2, depth), f32),
        ),
        [
            IN_SMEM, IN_VMEM, *[IN_ANY] * 6, IN_VMEM, IN_VMEM, *[IN_ANY] * 4, IN_VMEM, IN_ANY,
            IN_VMEM,
        ],
        [IN_VMEM, IN_ANY, IN_ANY, IN_VMEM, IN_ANY, IN_ANY, IN_ANY, IN_VMEM, IN_VMEM],
        [
            pltpu.VMEM((n + 1, local, depth), bf16),
            pltpu.VMEM((4, local, depth), bf16),
            pltpu.VMEM((n + 1, local, depth), bf16),
            pltpu.VMEM(wo.shape, bf16),
            pltpu.VMEM(wbi.shape, bf16),
            pltpu.VMEM((tokens, width), f32),
            pltpu.VMEM((tokens, 2 * width), bf16),
            pltpu.VMEM((max(2 * width, 2 * (CHUNK + HALO)), depth), f32),
            pltpu.VMEM((width, 2 * width), f32),
            pltpu.VMEM((CHUNK, 2 * width), bf16),
            pltpu.VMEM((CHUNK + HALO, width), f32),
            pltpu.VMEM((8, width), f32),
            pltpu.VMEM((PARAMS, width), f32),
            pltpu.VMEM((local, width), f32),
            pltpu.VMEM((local, width), f32),
            pltpu.VMEM((local, width), bf16),
            pltpu.VMEM((local, depth), bf16),
            pltpu.VMEM(ob, bf16),
            pltpu.VMEM(ob, bf16),
            pltpu.VMEM(one, bf16),
            pltpu.VMEM(one, bf16),
            pltpu.VMEM(gate, bf16),
            pltpu.VMEM(gate, bf16),
            pltpu.VMEM((group, PARAMS, width), f32),
            pltpu.VMEM((group, 2, depth), f32),
            pltpu.VMEM((n, 2, depth), f32),
            *gather_sems(n),
            *scatter_sems(n),
            *scatter_sems(n),
            dma((2, group)),
            dma((4,)),
            dma((3,)),
            dma((2, 4)),
            dma,
            dma((2,)),
            dma((3,)),
            pltpu.SemaphoreType.REGULAR,
            *share_sems("dp"),
            *share_sems("dp"),
            *share_sems("head"),
            *sum_sems(),
            *sum_sems(),
            *sum_sems(),
        ],
    )(
        lengths, low, out_part, hidden, terms, gated, wo, wbi, wg, par, pre, saved,
        normed_rows, stream, gain, resid, preffn_grad,
    )


def block_diagonal(weights, width):
    heads, size = weights.shape[0], weights.shape[1]
    placed = [
        jnp.pad(weights[i], ((i * size, width - (i + 1) * size),) * 2) for i in range(heads)
    ]
    return functools.reduce(jnp.add, placed)


def diagonal_blocks(dense, heads, size):
    blocks = [dense[i * size : (i + 1) * size, i * size : (i + 1) * size] for i in range(heads)]
    return jnp.stack(blocks, axis=1).transpose(1, 0, 2)


def shards(
    stream, doc_lengths, premix_gain, branch_weight, input_weight, conv_kernel, conv_bias,
    rate_weight, rate_bias, entry_weight, entry_bias, decay_param, output_weight, preffn_gain,
    ffn_gate, ffn_upward, ffn_down, cotangent,
):
    f32, bf16 = jnp.float32, jnp.bfloat16
    heads, size = rate_bias.shape
    chans = branch_weight.shape[1]
    width = -(-chans // LANES) * LANES

    slope = -DECAY_SCALE * jax.nn.softplus(decay_param.astype(f32))
    par = jnp.concatenate(
        [
            conv_bias[None].astype(f32),
            conv_kernel.astype(f32),
            rate_bias.reshape(1, -1).astype(f32),
            entry_bias.reshape(1, -1).astype(f32),
            slope[None],
        ]
    )
    par = jnp.pad(par, ((0, 0), (0, width - chans)), constant_values=-1.0)
    par = jnp.where((jnp.arange(width)[None] < chans) | (jnp.arange(PARAMS)[:, None] == DECAY), par, 0.0)
    wg = jnp.concatenate(
        [block_diagonal(rate_weight, width), block_diagonal(entry_weight, width)], axis=1
    )

    premix = premix_gain.astype(f32)[None]
    preffn = preffn_gain.astype(f32)[None]
    normed_rows, pre, saved, gated, wbi, wo, cot_rows, hidden_in, ffn_low = mixer_front(
        doc_lengths, stream, premix, branch_weight.T, input_weight.T, output_weight, wg, par,
        preffn, cotangent,
    )

    out_part, terms, far_terms, resid_grad, resid_low, preffn_grad = feed_forward(
        ffn_low, cot_rows, cotangent, hidden_in, preffn, ffn_gate, ffn_upward, ffn_down
    )

    layer_out, sums, last_terms, stream_grad, ob_grad, input_grad, gate_grad, dpar, gains = mixer_back(
        doc_lengths, resid_low, out_part, hidden_in, terms, gated, wo, wbi, wg, par, pre, saved,
        normed_rows, stream, premix, resid_grad, preffn_grad,
    )
    mine = lax.dynamic_index_in_dim(terms, lax.axis_index("dp"), keepdims=False)
    far = [far_terms[0], far_terms[1], last_terms]
    ffn_sums = [
        sum(
            (sums[i, k].astype(f32) for i in range(sums.shape[0])),
            mine[k].astype(f32) + far[k].astype(f32),
        )
        for k in range(3)
    ]
    ob_grad = ob_grad.reshape(2 * width, -1)
    output_grad = ob_grad[:chans].astype(f32)
    branch_grad = ob_grad[width : width + chans].astype(f32).T
    input_grad = input_grad.reshape(width, -1)[:chans].astype(f32).T
    gate_grad = gate_grad.reshape(width, -1).astype(f32)
    dpar = dpar[:, :chans]
    decay_grad = dpar[G_DECAY] * (-DECAY_SCALE * jax.nn.sigmoid(decay_param.astype(f32)))
    return (
        layer_out,
        stream_grad,
        gains[0],
        branch_grad,
        input_grad,
        dpar[G_TAP : G_TAP + CONVW],
        dpar[G_BIAS],
        diagonal_blocks(gate_grad[:, :width], heads, size),
        dpar[G_RATE].reshape(heads, size),
        diagonal_blocks(gate_grad[:, width:], heads, size),
        dpar[G_ENTRY].reshape(heads, size),
        decay_grad,
        output_grad,
        gains[1],
        ffn_sums[0],
        ffn_sums[1],
        ffn_sums[2],
    )


def solution(mesh):
    placed = (
        P(("dp", "head"), None),
        P("dp", None),
        P(),
        P(None, "head"),
        P(None, "head"),
        P(None, "head"),
        P("head"),
        P("head", None, None),
        P("head", None),
        P("head", None, None),
        P("head", None),
        P("head"),
        P("head", None),
        P(),
        P(None, "head"),
        P(None, "head"),
        P(None, "head"),
        P(("dp", "head"), None),
    )
    return jax.shard_map(
        shards,
        mesh=mesh,
        in_specs=placed,
        out_specs=(
            P(("dp", "head"), None),
            P(("dp", "head"), None),
            P(),
            P(None, "head"),
            P(None, "head"),
            P(None, "head"),
            P("head"),
            P("head", None, None),
            P("head", None),
            P("head", None, None),
            P("head", None),
            P("head"),
            P("head", None),
            P(),
            P("dp", "head"),
            P("dp", "head"),
            P("dp", "head"),
        ),
        check_vma=False,
    )
```

```python
import functools
import math

import jax
import jax.numpy as jnp
from jax import lax
from jax.experimental import pallas as pl
from jax.experimental.pallas import tpu as pltpu
from jax.sharding import PartitionSpec as P

CONVW = 4
SEQ = 2048
CHUNK = 256
BLOCK = 64
LANES = 128
HALO = 8
PARTS = 4
LAG = 2
OUT_AT = 2
FAR_TERMS = 2
VMEM_BYTES = 62 * 2**20
IN_VMEM = pl.BlockSpec(memory_space=pltpu.VMEM)
IN_SMEM = pl.BlockSpec(memory_space=pltpu.SMEM)
IN_ANY = pl.BlockSpec(memory_space=pl.ANY)

EPSILON = 1e-06
DECAY_SCALE = 8.0
GELU_A = math.sqrt(2.0 / math.pi)
GELU_B = 0.044715

BIAS, TAP, RATE_B, ENTRY_B, DECAY = 0, 1, 5, 6, 7
PARAMS = 8
SAVED = 4
G_BIAS, G_TAP, G_RATE, G_ENTRY, G_DECAY = 0, 1, 5, 6, 7


def rms_parts(values):
    rinv = lax.rsqrt(jnp.mean(values * values, axis=-1, keepdims=True) + EPSILON)
    return rinv, values * rinv


def norm_back(unit, rinv, gain, grad):
    q = gain * grad
    return rinv * (q - unit * jnp.mean(q * unit, axis=-1, keepdims=True))


def contract_cols(leading, trailing):
    return lax.dot_general(
        leading, trailing, (((1,), (1,)), ((), ())), preferred_element_type=jnp.float32
    )


def contract_rows(leading, trailing):
    return lax.dot_general(
        leading, trailing, (((0,), (0,)), ((), ())), preferred_element_type=jnp.float32
    )


def gelu_pair(v):
    sq = v * v
    th = jnp.tanh(GELU_A * v * (1.0 + GELU_B * sq))
    half = 0.5 * (1.0 + th)
    slope = half + 0.5 * v * (1.0 - th * th) * (GELU_A * (1.0 + 3.0 * GELU_B * sq))
    return v * half, slope


def gelu(v):
    return v * (0.5 * (1.0 + jnp.tanh(GELU_A * v * (1.0 + GELU_B * v * v))))


def decay_terms(rate_gate, slope, fresh):
    log_decay = slope * rate_gate
    c = jnp.exp(log_decay)
    y = 2.0 * log_decay
    series = 1.0 + y * (1.0 / 7.0)
    for n in (6, 5, 4, 3, 2):
        series = 1.0 + (y * (1.0 / n)) * series
    sq = c * c
    q = jnp.where(y > -0.5, -y * series, 1.0 - sq)
    rsq = lax.rsqrt(jnp.maximum(q, 1e-37))
    return (
        jnp.where(fresh, 0.0, c),
        jnp.where(fresh, 1.0, q * rsq),
        jnp.where(fresh, 0.0, sq * rsq),
    )


def doc_places(lengths, first, rows):
    spots = first + lax.broadcasted_iota(jnp.int32, (rows, LANES), 0)
    begin = jnp.zeros((rows, LANES), jnp.int32)
    start = jnp.int32(0)
    for k in range(lengths.shape[1] - 1):
        start = start + lengths[0, k]
        begin = jnp.where(spots >= start, start, begin)
    return spots - begin


def each(count, body):
    def step(i, _):
        body(i)
        return 0

    lax.fori_loop(0, count, step, 0)


def half_parts(q):
    return range(q * PARTS // 2, (q + 1) * PARTS // 2)


def line_place():
    return lax.axis_index("head"), lax.axis_size("head")


def peers(axis):
    n = lax.axis_size(axis)
    return [lax.rem(lax.axis_index(axis) + k, n) for k in range(1, n)]


def far_peer(axis):
    return lax.axis_size(axis) - 1 - lax.axis_index(axis)


def far_copies(terms, far_terms, sems):
    far = far_peer("dp")
    return [
        pltpu.make_async_remote_copy(
            src_ref=terms.at[far, k],
            dst_ref=far_terms.at[k],
            send_sem=sems.at[0, k],
            recv_sem=sems.at[1, k],
            device_id={"dp": far},
            device_id_type=pl.DeviceIdType.MESH,
        )
        for k in range(far_terms.shape[0])
    ]


def near_copies(terms, near_terms, last_terms, sems):
    n, me, far = lax.axis_size("dp"), lax.axis_index("dp"), far_peer("dp")
    for k in range(n - 2):
        peer = k + jnp.where(k >= jnp.minimum(me, far), 1, 0)
        peer = peer + jnp.where(k + 1 >= jnp.maximum(me, far), 1, 0)
        slot = me - jnp.where(peer < me, 1, 0) - jnp.where(n - 1 - peer < me, 1, 0)
        yield pltpu.make_async_remote_copy(
            src_ref=terms.at[peer],
            dst_ref=near_terms.at[slot],
            send_sem=sems.at[0, k],
            recv_sem=sems.at[1, slot],
            device_id={"dp": peer},
            device_id_type=pl.DeviceIdType.MESH,
        )
    yield pltpu.make_async_remote_copy(
        src_ref=terms.at[far, 2],
        dst_ref=last_terms,
        send_sem=sems.at[0, n - 2],
        recv_sem=sems.at[1, n - 2],
        device_id={"dp": far},
        device_id_type=pl.DeviceIdType.MESH,
    )


def near_arrive(near_terms, last_terms, sems):
    for k in range(near_terms.shape[0]):
        pltpu.make_async_copy(near_terms.at[k], near_terms.at[k], sems.at[1, k]).wait()
    pltpu.make_async_copy(last_terms, last_terms, sems.at[1, near_terms.shape[0]]).wait()


def peer_barrier(axes):
    barrier = pltpu.get_barrier_semaphore()
    count = 0
    for axis in axes:
        for peer in peers(axis):
            pl.semaphore_signal(
                barrier, inc=1, device_id={axis: peer}, device_id_type=pl.DeviceIdType.MESH
            )
            count += 1
    pl.semaphore_wait(barrier, count)


def wait_neighbours(sem, j, n):
    inside = (j > 0) & (j < n - 1)

    @pl.when(inside)
    def _():
        pl.semaphore_wait(sem, 2)

    @pl.when(jnp.logical_not(inside))
    def _():
        pl.semaphore_wait(sem, 1)


def line_barrier(j, n):
    barrier = pltpu.get_barrier_semaphore()
    for side in (-1, 1):

        @pl.when((j + side >= 0) & (j + side < n))
        def _():
            pl.semaphore_signal(
                barrier, inc=1, device_id={"head": j + side}, device_id_type=pl.DeviceIdType.MESH
            )

    wait_neighbours(barrier, j, n)


class Gather:
    def __init__(self, j, n, buf, send, recv):
        self.j, self.n, self.buf, self.send, self.recv = j, n, buf, send, recv
        self.span = buf.shape[1] // PARTS

    def copy(self, block, s, side, source=None):
        part = pl.ds(s * self.span, self.span)
        target = self.buf.at[block, part]
        return pltpu.make_async_remote_copy(
            src_ref=target if source is None else source.at[part],
            dst_ref=target,
            send_sem=self.send.at[(side + 1) // 2, block, s],
            recv_sem=self.recv.at[block, s],
            device_id={"head": self.j + side},
            device_id_type=pl.DeviceIdType.MESH,
        )

    def there(self, side):
        return (self.j + side >= 0) & (self.j + side < self.n)

    def flows(self, t):
        for side in (1, -1):
            block = self.j - side * t
            yield side, block, (block >= 0) & (block < self.n)

    def start(self, source, parts=range(PARTS)):
        for s in parts:
            for side in (1, -1):

                @pl.when(self.there(side))
                def _():
                    self.copy(self.j, s, side, source).start()

    def step(self, t, parts=range(PARTS)):
        for s in parts:
            for side, block, live in self.flows(t):

                @pl.when(live)
                def _():
                    self.copy(block, s, -side).wait_recv()

                @pl.when(live & self.there(side))
                def _():
                    self.copy(block, s, side).start()

    def finish(self, parts=range(PARTS)):
        def drain(t):
            for s in parts:
                for side, block, live in self.flows(t):

                    @pl.when(live & self.there(side))
                    def _():
                        self.copy(block, s, side).wait_send()

        each(self.n, drain)


class Scatter:
    def __init__(self, j, n, own, held, send, recv, last=2):
        self.j, self.n, self.own, self.held, self.send, self.recv = j, n, own, held, send, recv
        self.span = own.shape[1] // PARTS
        self.ends = (j, n)
        self.spot = last
        self.compact = own.shape[0] != n

    def place(self, block, side):
        return block if not self.compact else (1 - side) // 2

    def last(self):
        return self.j if not self.compact else self.spot

    def rows(self, s):
        return pl.ds(s * self.span, self.span)

    def slot(self, block, side, at):
        return block if side == 1 else jnp.where(block == at, self.n, block)

    def arrival(self, slot, s):
        return pltpu.make_async_copy(
            self.held.at[slot, self.rows(s)], self.held.at[slot, self.rows(s)], self.recv.at[slot, s]
        )

    def flows(self, t):
        for side in (1, -1):
            lag = self.j if side == 1 else self.n - 1 - self.j
            block = self.n - 1 - (t - lag) if side == 1 else t - lag
            yield side, block, (t >= lag) & (t <= self.n - 2)

    def copy(self, source, block, s, side):
        slot = self.slot(block, side, self.j + side)
        return pltpu.make_async_remote_copy(
            src_ref=source.at[block, self.rows(s)],
            dst_ref=self.held.at[slot, self.rows(s)],
            send_sem=self.send.at[block, s],
            recv_sem=self.recv.at[slot, s],
            device_id={"head": self.j + side},
            device_id_type=pl.DeviceIdType.MESH,
        )

    def step(self, t, parts=range(PARTS)):
        for s in parts:
            for side, block, live in self.flows(t):
                behind = (self.j - side >= 0) & (self.j - side < self.n)

                @pl.when(live & jnp.logical_not(behind))
                def _():
                    if self.compact:
                        self.held[block, self.rows(s), :] = self.own[
                            self.place(block, side), self.rows(s), :
                        ]
                        self.copy(self.held, block, s, side).start()
                    else:
                        self.copy(self.own, block, s, side).start()

                @pl.when(live & behind)
                def _():
                    self.arrival(block, s).wait()
                    self.add(block, s, side)
                    self.copy(self.held, block, s, side).start()

    def add(self, block, s, side):
        def add_rows(i):
            rows = pl.ds(pl.multiple_of(s * self.span + i * STRIP, STRIP), STRIP)
            total = self.own[self.place(block, side), rows, :].astype(jnp.float32) + self.held[
                block, rows, :
            ].astype(jnp.float32)
            self.held[block, rows, :] = total.astype(jnp.bfloat16)

        each(self.span // STRIP, add_rows)

    def arrive(self, parts=range(PARTS)):
        for s in parts:

            @pl.when(self.j > 0)
            def _():
                self.arrival(self.ends[0], s).wait()

            @pl.when(self.j < self.n - 1)
            def _():
                self.arrival(self.ends[1], s).wait()

    def result(self, rows):
        total = self.own[self.last(), rows, :].astype(jnp.float32)
        left = self.held[self.ends[0], rows, :].astype(jnp.float32)
        right = self.held[self.ends[1], rows, :].astype(jnp.float32)
        total = total + jnp.where(self.j > 0, left, 0.0)
        return total + jnp.where(self.j < self.n - 1, right, 0.0)

    def finish(self):
        def drain(t):
            for s in range(PARTS):
                for side, block, live in self.flows(t):

                    @pl.when(live)
                    def _():
                        self.copy(self.held, block, s, side).wait_send()

        each(self.n - 1, drain)


class Share:
    def __init__(self, axis, slots, send, recv):
        self.axis, self.slots, self.send, self.recv = axis, slots, send, recv
        self.me = lax.axis_index(axis)

    def copy(self, slot, peer, source=None):
        return pltpu.make_async_remote_copy(
            src_ref=self.slots.at[slot] if source is None else source,
            dst_ref=self.slots.at[slot],
            send_sem=self.send.at[peer],
            recv_sem=self.recv.at[slot],
            device_id={self.axis: peer},
            device_id_type=pl.DeviceIdType.MESH,
        )

    def start(self, sources=None):
        for peer in peers(self.axis):
            source = None if sources is None else sources.at[peer]
            self.copy(self.me, peer, source).start()

    def arrive(self):
        for peer in peers(self.axis):
            self.copy(peer, peer).wait_recv()

    def finish(self):
        for peer in peers(self.axis):
            self.copy(self.me, peer).wait_send()


def share_sems(axis):
    n = lax.axis_size(axis)
    return [pltpu.SemaphoreType.DMA((n,)), pltpu.SemaphoreType.DMA((n,))]


class Sum:
    def __init__(self, terms, slots, total, sems):
        self.terms, self.slots, self.total = terms, slots, total
        self.parts = Share("dp", slots, sems[0], sems[1])
        self.whole = Share("dp", total, sems[2], sems[3])
        self.me, self.sem = self.parts.me, sems[4]

    def start(self):
        self.parts.start(self.terms)

    def keep(self):
        return pltpu.make_async_copy(self.slots.at[self.me], self.total.at[self.me], self.sem)

    def spread(self):
        self.parts.arrive()
        rows = self.slots.shape[1]

        def add(part):
            value = jnp.zeros((STRIP, self.slots.shape[2]), jnp.float32)
            for i in range(self.slots.shape[0]):
                mine = self.terms[i, part, :].astype(jnp.float32)
                other = self.slots[i, part, :].astype(jnp.float32)
                value = value + jnp.where(self.me == i, mine, other)
            self.slots[self.me, part, :] = value.astype(jnp.bfloat16)

        strips(rows, add)
        for peer in peers("dp"):
            self.whole.copy(self.me, peer, self.slots.at[self.me]).start()
        self.keep().start()

    def finish(self):
        self.whole.arrive()
        self.keep().wait()
        self.parts.finish()
        self.whole.finish()


def sum_sems():
    return [*share_sems("dp"), *share_sems("dp"), pltpu.SemaphoreType.DMA]


def gather_sems(n):
    return [pltpu.SemaphoreType.DMA((2, n, PARTS)), pltpu.SemaphoreType.DMA((n, PARTS))]


def scatter_sems(n):
    return [pltpu.SemaphoreType.DMA((n, PARTS)), pltpu.SemaphoreType.DMA((n + 1, PARTS))]


def line_call(kernel, ident, name, out_shape, in_specs, out_specs, scratch, cost=None):
    return pl.pallas_call(
        kernel,
        out_shape=out_shape,
        in_specs=in_specs,
        out_specs=out_specs,
        scratch_shapes=scratch,
        compiler_params=pltpu.CompilerParams(
            collective_id=ident, has_side_effects=True, vmem_limit_bytes=VMEM_BYTES
        ),
        name=name,
    )


STRIP = 16


def strips(rows, body, first=0):
    each(rows // STRIP, lambda i: body(pl.ds(pl.multiple_of(first + i * STRIP, STRIP), STRIP)))


def front_kernel(
    lengths, stream, premix, wb, wi, wo_in, wg, par, preffn, cot,
    rows_out, pre_out, saved, gated_out, wbi_out, wo_out, cot_rows, hidden, low_out,
    normed, rows, wbi, wo, pre, gated, stage, z, carry, own, held, raw,
    gsend, grecv, csend, crecv, send, recv, keep_sem, pre_sem, stage_sem, one_sem, raw_sem,
):
    j, n = line_place()
    f32, bf16 = jnp.float32, jnp.bfloat16
    local, depth = stream.shape
    width, chans = gated.shape[1], wb.shape[0]
    tiles = width // LANES
    loads = [
        pltpu.make_async_copy(source, raw.at[k], raw_sem.at[k])
        for k, source in enumerate((wb, wi, wo_in))
    ]
    for load in loads:
        load.start()
    line_barrier(j, n)

    def norm(part):
        _, unit = rms_parts(stream[part, :].astype(f32))
        normed[part, :] = (unit * premix[...]).astype(bf16)

    strips(local, norm)
    gather = Gather(j, n, rows, gsend, grecv)
    gather.start(normed)
    for k, (target, first) in enumerate(((wbi, 0), (wbi, width), (wo, 0))):
        loads[k].wait()
        whole = chans // STRIP * STRIP
        target[first + whole : first + width, :] = jnp.zeros((width - whole, depth), bf16)
        target[first : first + chans, :] = raw[k]
    out_copies = [
        pltpu.make_async_copy(wbi, wbi_out, one_sem.at[0]),
        pltpu.make_async_copy(wo, wo_out, one_sem.at[1]),
    ]
    for copy in out_copies:
        copy.start()

    def span(block):
        return pl.ds(pl.multiple_of(block * local, local), local)

    def shifted(block):
        return pl.ds(pl.multiple_of(block * local + HALO, HALO), local)

    def keep(source, block):
        return pltpu.make_async_copy(source, rows_out.at[block], keep_sem.at[block])

    def keep_pre(block):
        return pltpu.make_async_copy(
            pre.at[shifted(block)], pre_out.at[span(block)], pre_sem.at[block]
        )

    pre[0:HALO, :] = jnp.zeros((HALO, 2 * width), f32)
    keep(normed, j).start()
    pre[shifted(j), :] = contract_cols(normed[...], wbi[...])
    keep_pre(j).start()

    def visit(v):
        t = v // 2 + 1
        block = jnp.where(v % 2 == 0, j - t, j + t)

        @pl.when(v % 2 == 0)
        def _():
            gather.step(t)

        @pl.when((block >= 0) & (block < n))
        def _():
            keep(rows.at[block], block).start()
            pre[shifted(block), :] = contract_cols(rows[block], wbi[...])
            keep_pre(block).start()

    each(2 * (n - 1), visit)
    cots = Gather(j, n, cot_rows, csend, crecv)
    cots.start(cot)
    mine = pltpu.make_async_copy(cot, cot_rows.at[j], one_sem.at[2])
    mine.start()

    carry[...] = jnp.zeros_like(carry)
    count = n * local // CHUNK

    def keep_stage(i):
        return pltpu.make_async_copy(
            stage.at[lax.rem(i, 2)],
            saved.at[pl.ds(pl.multiple_of(i * CHUNK, CHUNK), CHUNK)],
            stage_sem.at[lax.rem(i, 2)],
        )

    def chunk(i):
        first = i * CHUNK

        @pl.when(i >= 2)
        def _():
            keep_stage(i - 2).wait()

        u_out, r_out, e_out, h_out = (
            stage.at[lax.rem(i, 2), :, k * width : (k + 1) * width] for k in range(SAVED)
        )

        def conv_step(b):
            row = pl.multiple_of(b * BLOCK, BLOCK)
            halo = pl.ds(pl.multiple_of(first + row, BLOCK), BLOCK + HALO)
            place = doc_places(lengths, first + row, BLOCK)
            for t in range(tiles):
                cols = pl.ds(t * LANES, LANES)
                xs = pre[halo, pl.ds(width + t * LANES, LANES)]
                total = par[BIAS : BIAS + 1, cols] + par[TAP : TAP + 1, cols] * xs[HALO:]
                for k in range(1, CONVW):
                    term = par[TAP + k : TAP + k + 1, cols] * xs[HALO - k : HALO - k + BLOCK]
                    total = total + jnp.where(place >= k, term, 0.0)
                u_out[pl.ds(row, BLOCK), cols] = total

        each(CHUNK // BLOCK, conv_step)
        z[...] = jnp.dot(u_out[...].astype(bf16), wg[...], preferred_element_type=f32)

        def scan_step(b):
            row = pl.multiple_of(b * BLOCK, BLOCK)
            part = pl.ds(row, BLOCK)
            spot = pl.ds(pl.multiple_of(first + row, BLOCK), BLOCK)
            here = pl.ds(pl.multiple_of(first + row + HALO, HALO), BLOCK)
            fresh = doc_places(lengths, first + row, BLOCK) == 0
            inner = lax.broadcasted_iota(jnp.int32, (BLOCK, LANES), 0) % 8
            for t in range(tiles):
                cols = pl.ds(t * LANES, LANES)
                other = pl.ds(width + t * LANES, LANES)
                r = jax.nn.sigmoid(z[part, cols] + par[RATE_B : RATE_B + 1, cols])
                e = jax.nn.sigmoid(z[part, other] + par[ENTRY_B : ENTRY_B + 1, cols])
                u = u_out[part, cols]
                c, m, _ = decay_terms(r, par[DECAY : DECAY + 1, cols], fresh)
                r_out[part, cols] = r
                e_out[part, cols] = e
                b_ = m * e * u
                for d in (1, 2, 4):
                    near = inner >= d
                    b_ = b_ + c * jnp.where(near, pltpu.roll(b_, d, 0), 0.0)
                    c = c * jnp.where(near, pltpu.roll(c, d, 0), 1.0)
                last = carry[0:1, cols]
                pieces = []
                for g in range(BLOCK // 8):
                    eight = slice(g * 8, g * 8 + 8)
                    state = b_[eight] + c[eight] * last
                    last = state[7:8]
                    pieces.append(state)
                carry[0:1, cols] = last
                h = jnp.concatenate(pieces, axis=0)
                h_out[part, cols] = h
                gated[spot, cols] = (h * gelu(pre[here, cols])).astype(bf16)

        each(CHUNK // BLOCK, scan_step)
        keep_stage(i).start()

        @pl.when(i == count * 5 // 8)
        def _():
            cots.step(1)

    each(count, chunk)
    keep_gated = pltpu.make_async_copy(gated, gated_out, one_sem.at[3])
    keep_gated.start()

    scatter = Scatter(j, n, own, held, send, recv)

    def compute(block, slot):
        own[slot] = jnp.dot(
            gated[span(block), :], wo[...], preferred_element_type=f32
        ).astype(bf16)

    def ahead(t):
        for side, block, live in scatter.flows(t):
            pl.when(live)(functools.partial(compute, block, scatter.place(block, side)))

    ahead(0)

    def step(t):
        scatter.step(t)
        ahead(t + 1)

        @pl.when(t == 0)
        def _():
            compute(j, 2)

        @pl.when(t + 2 < n)
        def _():
            cots.step(t + 2)

    each(n - 1, step)
    scatter.arrive()

    def settle(part):
        total = stream[part, :].astype(f32) + scatter.result(part)
        hidden[part, :] = total
        _, unit = rms_parts(total)
        low_out[part, :] = (unit * preffn[...]).astype(bf16)

    strips(local, settle)
    scatter.finish()
    gather.finish()
    cots.finish()
    mine.wait()
    keep_gated.wait()
    for copy in out_copies:
        copy.wait()
    keep(normed, j).wait()
    keep_pre(j).wait()
    for k in range(1, n):
        other = lax.rem(j + k, n)
        keep(rows.at[other], other).wait()
        keep_pre(other).wait()
    for i in range(max(count - 2, 0), count):
        keep_stage(i).wait()


def mixer_front(lengths, stream, premix, wb, wi, wo, wg, par, preffn, cot):
    n = lax.axis_size("head")
    local, depth = stream.shape
    width, tokens = wg.shape[0], n * local
    f32, bf16 = jnp.float32, jnp.bfloat16
    shape, vmem, dma = jax.ShapeDtypeStruct, pltpu.VMEM, pltpu.SemaphoreType.DMA
    return line_call(
        front_kernel, 0, "mixer_front",
        (
            shape((n, local, depth), bf16),
            shape((tokens, 2 * width), f32),
            shape((tokens, SAVED * width), f32),
            shape((tokens, width), bf16),
            shape((2 * width, depth), bf16),
            shape((width, depth), bf16),
            shape((n, local, depth), bf16),
            shape((local, depth), f32),
            shape((local, depth), bf16),
        ),
        [IN_SMEM, IN_VMEM, IN_VMEM, IN_ANY, IN_ANY, IN_ANY, *[IN_VMEM] * 4],
        [IN_ANY] * 7 + [IN_VMEM] * 2,
        [
            vmem((local, depth), bf16),
            vmem((n, local, depth), bf16),
            vmem((2 * width, depth), bf16),
            vmem((width, depth), bf16),
            vmem((HALO + tokens, 2 * width), f32),
            vmem((tokens, width), bf16),
            vmem((2, CHUNK, SAVED * width), f32),
            vmem((CHUNK, 2 * width), f32),
            vmem((8, width), f32),
            vmem((3, local, depth), bf16),
            vmem((n + 1, local, depth), bf16),
            vmem((3, wb.shape[0], depth), bf16),
            *gather_sems(n),
            *gather_sems(n),
            *scatter_sems(n),
            dma((n,)),
            dma((n,)),
            dma((2,)),
            dma((4,)),
            dma((3,)),
        ],
    )(lengths, stream, premix, wb, wi, wo, wg, par, preffn, cot)


def ffn_kernel(
    low, cot_rows, cot_in, hidden_in, gain, wg_in, wu_in, wd_in,
    out_part, terms, far_terms, resid, resid_low, gain_grad,
    rows, cot_pair, kept, own, held, stage, wstage, cot_cols, wg, wu, wd, cot, hidden,
    gsend, grecv, send, recv, cot_sem, out_sem, col_sem, term_sem, far_sem, load_sem,
):
    j, n = line_place()
    peer_barrier(("head", "dp"))
    f32, bf16 = jnp.float32, jnp.bfloat16
    local, depth = low.shape
    units = wg.shape[1]
    half = local // 2
    fstep = 256 if units % 256 == 0 else LANES
    dstep = 512
    gather = Gather(j, n, rows, gsend, grecv)
    scatter = Scatter(j, n, own, held, send, recv)
    gather.start(low, half_parts(0))
    loads = [
        pltpu.make_async_copy(a, b, load_sem.at[k])
        for k, (a, b) in enumerate(
            ((wg_in, wg), (wu_in, wu), (wd_in, wd), (cot_in, cot), (hidden_in, hidden))
        )
    ]
    for load in loads:
        load.start()
    rows[j] = low[...]
    for load in loads:
        load.wait()

    def pair(chip, q):
        return pl.ds(pl.multiple_of(2 * chip, 2), 2), pl.ds(q * half, half)

    def fetch(chip, q):
        return pltpu.make_async_copy(cot_rows.at[pair(chip, q)], cot_pair, cot_sem)

    def put(chip, q):
        return pltpu.make_async_copy(stage, out_part.at[pair(chip, q)], out_sem)

    def pair_work(chip, q):
        spot = pair(chip, q)

        def flat(v):
            return v.reshape(2 * half, v.shape[-1])

        def fold(v):
            return v.astype(bf16).reshape(2, half, v.shape[-1])

        for f in range(0, units, fstep):
            cols = slice(f, f + fstep)
            gate = jnp.dot(flat(rows[spot]), wg[:, cols], preferred_element_type=f32)
            act, slope = gelu_pair(gate)
            up = jnp.dot(flat(rows[spot]), wu[:, cols], preferred_element_type=f32)
            kept[2, *spot, cols] = fold(act * up)
            grad = jnp.dot(flat(cot_pair[...]), wd[:, cols], preferred_element_type=f32)
            kept[0, *spot, cols] = fold(grad * up * slope)
            kept[1, *spot, cols] = fold(grad * act)
        for d in range(0, depth, dstep):
            cols = slice(d, d + dstep)
            own[*spot, cols] = fold(
                contract_cols(flat(kept[0, *spot]), wg[cols, :])
                + contract_cols(flat(kept[1, *spot]), wu[cols, :])
            )
            stage[:, :, cols] = fold(contract_cols(flat(kept[2, *spot]), wd[cols, :]))

    def gather_half(q):
        def visit(i):
            t = i + 1
            reach = t // 2
            chip = j // 2 + jnp.where((t + j) % 2 == 0, -reach, reach)
            live = (chip >= 0) & (chip < n // 2)

            @pl.when(live)
            def _():
                fetch(chip, q).start()

            gather.step(t, half_parts(q))
            if q:
                scatter.step(t - 1, half_parts(0))

            @pl.when(live)
            def _():
                fetch(chip, q).wait()

                @pl.when((t > 1) | (q > 0))
                def _():
                    put(chip, q).wait()

                pair_work(chip, q)
                put(chip, q).start()

        each(n - 1, visit)

    gather_half(0)
    gather.start(low, half_parts(1))
    gather_half(1)
    put(j // 2, 1).wait()

    width = depth // n
    per = depth // terms.shape[0] // width

    far = far_peer("dp")

    def columns(b):
        return pl.ds(pl.multiple_of(lax.rem(b + far * per, n) * width, width), width)

    def take(b):
        return pltpu.make_async_copy(cot_rows.at[:, :, columns(b)], cot_cols, col_sem)

    def give(b):
        owner = lax.rem(b // per + far, n // per)
        spot = pl.ds(pl.multiple_of(lax.rem(b, per) * width, width), width)
        return pltpu.make_async_copy(wstage, terms.at[owner, :, spot, :], term_sem)

    def weights(b):
        xs = rows[:, :, columns(b)].reshape(n * local, width)
        take(b).wait()

        @pl.when(b > 0)
        def _():
            give(b).wait()

        @pl.when(b == per)
        def _():
            for copy in far_copies(terms, far_terms, far_sem):
                copy.start()

        for k, lead in ((0, xs), (1, xs), (2, cot_cols[...].reshape(n * local, width))):
            wstage[k] = contract_rows(lead, kept[k].reshape(n * local, units)).astype(bf16)
        give(b).start()

        @pl.when(b + 1 < n)
        def _():
            take(b + 1).start()

    take(0).start()

    def step(t):
        pl.when(t < n - 1)(lambda: scatter.step(t, half_parts(1)))
        weights(t)

    each(n, step)
    scatter.arrive()
    gain_grad[...] = jnp.zeros_like(gain_grad)

    def settle(part):
        rinv, u = rms_parts(hidden[part, :])
        grad = scatter.result(part)
        gain_grad[...] += jnp.sum(grad * u, axis=0, keepdims=True)
        total = cot[part, :].astype(f32) + norm_back(u, rinv, gain[...], grad)
        resid[part, :] = total
        resid_low[part, :] = total.astype(bf16)

    strips(local, settle)
    give(0).wait()
    gather.finish()
    scatter.finish()
    for copy in far_copies(terms, far_terms, far_sem):
        copy.wait()


def feed_forward(low, cot_rows, cot, hidden, gain, wg, wu, wd):
    n, group = lax.axis_size("head"), lax.axis_size("dp")
    local, depth = low.shape
    units = wg.shape[1]
    bf16 = jnp.bfloat16
    shape, vmem = jax.ShapeDtypeStruct, pltpu.VMEM
    pair = (2, local // 2, depth)
    return line_call(
        ffn_kernel, 2, "feed_forward",
        (
            shape((n, local, depth), bf16),
            shape((group, 3, depth // group, units), bf16),
            shape((FAR_TERMS, depth // group, units), bf16),
            shape((local, depth), jnp.float32),
            shape((local, depth), bf16),
            shape((1, depth), jnp.float32),
        ),
        [IN_VMEM, IN_ANY, IN_ANY, IN_ANY, IN_VMEM, IN_ANY, IN_ANY, IN_ANY],
        [IN_ANY, IN_ANY, IN_ANY, IN_VMEM, IN_VMEM, IN_VMEM],
        [
            vmem((n, local, depth), bf16),
            vmem(pair, bf16),
            vmem((3, n, local, units), bf16),
            vmem((n, local, depth), bf16),
            vmem((n + 1, local, depth), bf16),
            vmem(pair, bf16),
            vmem((3, depth // n, units), bf16),
            vmem((n, local, depth // n), bf16),
            *[vmem(wg.shape, bf16)] * 3,
            vmem((local, depth), bf16),
            vmem((local, depth), jnp.float32),
            *gather_sems(n),
            *scatter_sems(n),
            *[pltpu.SemaphoreType.DMA] * 4,
            pltpu.SemaphoreType.DMA((2, FAR_TERMS)),
            pltpu.SemaphoreType.DMA((5,)),
        ],
    )(low, cot_rows, cot, hidden, gain, wg, wu, wd)


def back_kernel(
    lengths, low, out_part, hidden, terms, gated, wo_in, wbi_in, wg, par, pre, saved,
    normed_rows, stream_in, gain, resid, preffn_grad,
    layer_out, sums, last_terms, stream_grad, ob_total, i_total, g_total, par_grad, gains,
    rows, own, held, wo, wbi, dh, dpre, acc, dgate, dz, du, carry, dpar,
    unit_bp, unit_h, unit_gated, unit_normed,
    obterms, obslots, iterms, islots, gterms, gslots, pslots, dslots, hslots,
    gsend, grecv, send4, recv4, send8, recv8, tsems, unit_sem, own_sem, chunk_sem,
    row_sem, wide_sem, load_sem, free, psend, precv, dsend, drecv, hsend, hrecv, *sems,
):
    j, n = line_place()
    f32, bf16 = jnp.float32, jnp.bfloat16
    local, depth = low.shape
    width = dh.shape[1]
    tiles = width // LANES
    stream, wide = unit_normed, acc.at[width : width + local]
    loads = [
        pltpu.make_async_copy(a, b, load_sem.at[k])
        for k, (a, b) in enumerate(((wo_in, wo), (wbi_in, wbi), (stream_in, stream)))
    ]
    for load in loads[:2]:
        load.start()
    peer_barrier(("head", "dp"))
    gather = Gather(j, n, rows, gsend, grecv)
    gather.start(low)
    for copy in near_copies(terms, sums, last_terms, tsems):
        copy.start()
    rows[j] = low[...]
    outs = Scatter(j, n, own, held, send4, recv4)
    acc[...] = jnp.zeros_like(acc)

    def fetch_out(block, slot):
        return pltpu.make_async_copy(out_part.at[block], own.at[slot], own_sem.at[slot])

    def outs_ahead(t):
        for start in (True, False):
            for side, block, live in outs.flows(t):
                copy = fetch_out(block, outs.place(block, side))
                pl.when(live)(copy.start if start else copy.wait)

    def outs_step(t):
        outs.step(t)
        outs_ahead(t + 1)

    def outs_slot(slot):
        t = slot - 1 - LAG

        @pl.when((t >= 0) & (t < n - 1))
        def _():
            outs_step(t)

    outs_ahead(0)
    fetch_out(j, 2).start()
    fetch_out(j, 2).wait()

    def unit_copies(block):
        span = pl.ds(pl.multiple_of(block * local, local), local)
        return (
            pltpu.make_async_copy(pre.at[span, 0:width], unit_bp, unit_sem.at[0]),
            pltpu.make_async_copy(
                saved.at[span, 3 * width : 4 * width], unit_h, unit_sem.at[1]
            ),
            pltpu.make_async_copy(gated.at[span], unit_gated, unit_sem.at[2]),
            pltpu.make_async_copy(normed_rows.at[block], unit_normed, unit_sem.at[3]),
        )

    def unit(block):
        span = pl.ds(pl.multiple_of(block * local, local), local)
        dh[span, :] = contract_cols(rows[block], wo[...])

        def act(i):
            part = pl.ds(pl.multiple_of(i * BLOCK, BLOCK), BLOCK)
            spot = pl.ds(pl.multiple_of(block * local + i * BLOCK, BLOCK), BLOCK)
            for t in range(tiles):
                cols = pl.ds(t * LANES, LANES)
                grad = dh[spot, cols]
                value, slope = gelu_pair(unit_bp[part, cols])
                dpre[spot, cols] = (grad * unit_h[part, cols] * slope).astype(bf16)
                dh[spot, cols] = grad * value

        each(local // BLOCK, act)
        acc[0:width, :] += contract_rows(unit_gated[...], rows[block])
        acc[width : 2 * width, :] += contract_rows(dpre[span, 0:width], unit_normed[...])

    def visit(v):
        t = (v + 1) // 2
        block = jnp.where(v % 2 == 1, j - t, j + t)
        live = (block >= 0) & (block < n)

        @pl.when(live)
        def _():
            for copy in unit_copies(block):
                copy.start()

        @pl.when(v % 2 == 1)
        def _():
            gather.step(t)
            outs_slot(t)

        @pl.when(live)
        def _():
            for copy in unit_copies(block):
                copy.wait()
            unit(block)

    loads[0].wait()
    each(2 * n - 1, visit)
    gather.finish()
    for side in (-1, 1):

        @pl.when((j + side >= 0) & (j + side < n))
        def _():
            pl.semaphore_signal(
                free, inc=1, device_id={"head": j + side}, device_id_type=pl.DeviceIdType.MESH
            )

    def pack(target, source, count):
        span = target.shape[1]

        def strip(i):
            row = pl.multiple_of(i * STRIP, STRIP)
            target[row // span, pl.ds(pl.multiple_of(lax.rem(row, span), STRIP), STRIP), :] = source[
                pl.ds(row, STRIP), :
            ].astype(bf16)

        each(count // STRIP, strip)

    obsum = Sum(obterms, obslots, ob_total, sems[0:5])
    isum = Sum(iterms, islots, i_total, sems[5:10])
    gsum = Sum(gterms, gslots, g_total, sems[10:15])
    pack(obterms, acc, 2 * width)
    obsum.start()
    loads[2].start()

    count = n * local // CHUNK

    def chunk_copies(i):
        base = lax.rem(i, 2) * (CHUNK + HALO)
        start = pl.multiple_of(i * CHUNK, CHUNK)
        ahead = pl.multiple_of(jnp.maximum(start - HALO, 0), HALO)
        halo, main = pl.ds(pl.multiple_of(base, HALO), HALO), pl.ds(
            pl.multiple_of(base + HALO, HALO), CHUNK
        )
        kept, x = slice(0, SAVED * width), slice(SAVED * width, (SAVED + 1) * width)
        pairs = (
            (saved.at[pl.ds(ahead, HALO)], acc.at[halo, kept]),
            (saved.at[pl.ds(start, CHUNK)], acc.at[main, kept]),
            (pre.at[pl.ds(ahead, HALO), width : 2 * width], acc.at[halo, x]),
            (pre.at[pl.ds(start, CHUNK), width : 2 * width], acc.at[main, x]),
        )
        return [
            pltpu.make_async_copy(a, b, chunk_sem.at[lax.rem(i, 2), k])
            for k, (a, b) in enumerate(pairs)
        ]

    def total(v):
        return jnp.sum(v, axis=0, keepdims=True)

    for copy in chunk_copies(count - 1):
        copy.start()
    du[...] = jnp.zeros_like(du)
    carry[...] = jnp.zeros_like(carry)
    dgate[...] = jnp.zeros_like(dgate)
    dpar[...] = jnp.zeros_like(dpar)

    def chunk(k):
        i = count - 1 - k

        @pl.when(i > 0)
        def _():
            for copy in chunk_copies(i - 1):
                copy.start()

        for copy in chunk_copies(i):
            copy.wait()
        base = lax.rem(i, 2) * (CHUNK + HALO)
        first = i * CHUNK
        du[CHUNK:, :] = du[0:HALO, :]

        def scan_step(b):
            row = pl.multiple_of(CHUNK - BLOCK - b * BLOCK, BLOCK)
            part = pl.ds(row, BLOCK)
            spot = pl.ds(pl.multiple_of(first + row, BLOCK), BLOCK)
            here = pl.ds(pl.multiple_of(base + HALO + row, HALO), BLOCK)
            halo = pl.ds(pl.multiple_of(base + row, HALO), BLOCK + HALO)
            fresh = doc_places(lengths, first + row, BLOCK) == 0
            place = lax.broadcasted_iota(jnp.int32, (BLOCK, LANES), 0)
            inner = place % 8
            for t in range(tiles):
                cols = pl.ds(t * LANES, LANES)
                u, r, e = (acc[here, pl.ds(m * width + t * LANES, LANES)] for m in range(3))
                prior = acc[halo, pl.ds(3 * width + t * LANES, LANES)][HALO - 1 : HALO - 1 + BLOCK]
                near_h = dh[spot, cols]
                decay = par[DECAY : DECAY + 1, cols]
                c, m, ratio = decay_terms(r, decay, fresh)
                b_, a_ = c * near_h, c
                for d in (1, 2, 4):
                    near_row = inner < 8 - d
                    b_ = b_ + a_ * jnp.where(near_row, pltpu.roll(b_, BLOCK - d, 0), 0.0)
                    a_ = a_ * jnp.where(near_row, pltpu.roll(a_, BLOCK - d, 0), 1.0)
                later = carry[0:1, cols]
                pieces = []
                front = later
                for g in reversed(range(BLOCK // 8)):
                    eight = slice(g * 8, g * 8 + 8)
                    state = b_[eight] + a_[eight] * front
                    front = state[0:1]
                    pieces.append(state)
                carry[0:1, cols] = front
                mu = jnp.concatenate(pieces[::-1], axis=0)
                adj = near_h + jnp.where(
                    place == BLOCK - 1, later, pltpu.roll(mu, BLOCK - 1, 0)
                )
                eu = e * u
                dlog = adj * (prior * c - eu * ratio)
                dpar[G_DECAY : G_DECAY + 1, cols] += total(dlog * r)
                dzr = decay * dlog * (r * (1.0 - r))
                dze = adj * m * eu * (1.0 - e)
                dpar[G_RATE : G_RATE + 1, cols] += total(dzr)
                dpar[G_ENTRY : G_ENTRY + 1, cols] += total(dze)
                dz[part, cols] = dzr.astype(bf16)
                dz[part, pl.ds(width + t * LANES, LANES)] = dze.astype(bf16)
                du[part, cols] = adj * m * e

        each(CHUNK // BLOCK, scan_step)
        u_chunk = acc[pl.ds(pl.multiple_of(base + HALO, HALO), CHUNK), 0:width]
        du[0:CHUNK, :] += contract_cols(dz[...], wg[...])
        dgate[...] += contract_rows(u_chunk.astype(bf16), dz[...])

        def conv_step(b):
            row = pl.multiple_of(b * BLOCK, BLOCK)
            spot = pl.ds(pl.multiple_of(first + row, BLOCK), BLOCK)
            halo = pl.ds(pl.multiple_of(base + row, HALO), BLOCK + HALO)
            place = doc_places(lengths, first + row, BLOCK + HALO)
            for t in range(tiles):
                cols = pl.ds(t * LANES, LANES)
                ds = du[pl.ds(row, BLOCK + HALO), cols]
                xs = acc[halo, pl.ds(SAVED * width + t * LANES, LANES)]
                mine = ds[0:BLOCK]
                dx = par[TAP : TAP + 1, cols] * mine
                dpar[G_BIAS : G_BIAS + 1, cols] += total(mine)
                dpar[G_TAP : G_TAP + 1, cols] += total(mine * xs[HALO:])
                for k in range(1, CONVW):
                    inside = jnp.where(place >= k, ds, 0.0)
                    dx = dx + par[TAP + k : TAP + k + 1, cols] * inside[k : k + BLOCK]
                    dpar[G_TAP + k : G_TAP + k + 1, cols] += total(
                        inside[0:BLOCK] * xs[HALO - k : HALO - k + BLOCK]
                    )
                dpre[spot, pl.ds(width + t * LANES, LANES)] = dx.astype(bf16)

        each(CHUNK // BLOCK, conv_step)
        pl.when(k % 2 == 0)(lambda: outs_slot(n + k // 2))

    each(count, chunk)
    for t in range(n - 1 - max(0, LAG - (count + 1) // 2), n - 1):
        outs_step(jnp.int32(t))
    pack(gterms, dgate, width)
    gsum.start()
    pshare = Share("dp", pslots, psend, precv)
    pslots[pshare.me] = dpar[...]
    pshare.start()
    load_hidden = pltpu.make_async_copy(hidden, wide, wide_sem.at[0])
    load_hidden.start()
    scatter = Scatter(j, n, own, rows, send8, recv8, last=3)
    loads[1].wait()
    loads[2].wait()

    def compute(block, slot):
        span = pl.ds(pl.multiple_of(block * local, local), local)
        own[slot] = jnp.dot(dpre[span, :], wbi[...], preferred_element_type=f32).astype(bf16)

    def ahead(t):
        for side, block, live in scatter.flows(t):
            pl.when(live)(functools.partial(compute, block, scatter.place(block, side)))

    ahead(0)
    wait_neighbours(free, j, n)
    scatter.step(0)
    ahead(1)
    obsum.spread()

    def settle_out(part):
        layer_out[part, :] = (wide[part, :] + outs.result(part)).astype(bf16)

    load_resid = pltpu.make_async_copy(resid, wide, wide_sem.at[1])

    def step(t):
        @pl.when(t == OUT_AT + 1)
        def _():
            load.wait()
            for c in range(0, width, LANES):
                acc[c : c + LANES, :] = contract_rows(
                    dpre[:, width + c : width + c + LANES],
                    held[0:n].reshape(n * local, depth),
                )
            pack(iterms, acc, width)
            isum.start()

        scatter.step(t)
        ahead(t + 1)

        @pl.when(t == OUT_AT)
        def _():
            outs.arrive()
            load_hidden.wait()
            strips(local, settle_out)
            outs.finish()
            load_resid.start()
            load.start()
            compute(j, 3)

        @pl.when(t == OUT_AT + 2)
        def _():
            gsum.spread()

    load = pltpu.make_async_copy(normed_rows, held.at[pl.ds(0, n)], row_sem)
    lax.fori_loop(1, n - 1, lambda t, _: (step(t), 0)[1], 0)
    isum.spread()
    scatter.arrive()
    load_resid.wait()
    gains[...] = jnp.zeros_like(gains)

    def settle(part):
        rinv, u = rms_parts(stream[part, :].astype(f32))
        grad = scatter.result(part)
        gains[0:1, :] += jnp.sum(grad * u, axis=0, keepdims=True)
        value = wide[part, :] + norm_back(u, rinv, gain[...], grad)
        stream_grad[part, :] = value.astype(bf16)

    strips(local, settle)

    gains[1:2, :] = preffn_grad[...]
    for axis, slots, ssem, rsem in (("dp", dslots, dsend, drecv), ("head", hslots, hsend, hrecv)):
        share = Share(axis, slots, ssem, rsem)
        slots[share.me] = gains[...]
        share.start()
        share.arrive()
        value = slots[0]
        for i in range(1, slots.shape[0]):
            value = value + slots[i]
        gains[...] = value
        share.finish()

    pshare.arrive()
    value = pslots[0]
    for i in range(1, pslots.shape[0]):
        value = value + pslots[i]
    par_grad[...] = value
    pshare.finish()
    for one in (gsum, obsum, isum):
        one.finish()
    scatter.finish()
    for copy in near_copies(terms, sums, last_terms, tsems):
        copy.wait_send()
    near_arrive(sums, last_terms, tsems)


def mixer_back(
    lengths, low, out_part, hidden, terms, gated, wo, wbi, wg, par, pre, saved,
    normed_rows, stream, gain, resid, preffn_grad,
):
    n, group = lax.axis_size("head"), lax.axis_size("dp")
    local, depth = stream.shape
    width, tokens = wo.shape[0], pre.shape[0]
    f32, bf16 = jnp.float32, jnp.bfloat16
    ob = (group, 2 * width // group, depth)
    one = (group, width // group, depth)
    gate = (group, width // group, 2 * width)
    dma = pltpu.SemaphoreType.DMA
    shape = jax.ShapeDtypeStruct
    return line_call(
        back_kernel, 3, "mixer_back",
        (
            shape((local, depth), bf16),
            shape((group - 2, *terms.shape[1:]), bf16),
            shape(terms.shape[2:], bf16),
            shape((local, depth), bf16),
            shape(ob, bf16),
            shape(one, bf16),
            shape(gate, bf16),
            shape((PARAMS, width), f32),
            shape((2, depth), f32),
        ),
        [
            IN_SMEM, IN_VMEM, *[IN_ANY] * 6, IN_VMEM, IN_VMEM, *[IN_ANY] * 4, IN_VMEM, IN_ANY,
            IN_VMEM,
        ],
        [IN_VMEM, IN_ANY, IN_ANY, IN_VMEM, IN_ANY, IN_ANY, IN_ANY, IN_VMEM, IN_VMEM],
        [
            pltpu.VMEM((n + 1, local, depth), bf16),
            pltpu.VMEM((4, local, depth), bf16),
            pltpu.VMEM((n + 1, local, depth), bf16),
            pltpu.VMEM(wo.shape, bf16),
            pltpu.VMEM(wbi.shape, bf16),
            pltpu.VMEM((tokens, width), f32),
            pltpu.VMEM((tokens, 2 * width), bf16),
            pltpu.VMEM((max(2 * width, 2 * (CHUNK + HALO)), depth), f32),
            pltpu.VMEM((width, 2 * width), f32),
            pltpu.VMEM((CHUNK, 2 * width), bf16),
            pltpu.VMEM((CHUNK + HALO, width), f32),
            pltpu.VMEM((8, width), f32),
            pltpu.VMEM((PARAMS, width), f32),
            pltpu.VMEM((local, width), f32),
            pltpu.VMEM((local, width), f32),
            pltpu.VMEM((local, width), bf16),
            pltpu.VMEM((local, depth), bf16),
            pltpu.VMEM(ob, bf16),
            pltpu.VMEM(ob, bf16),
            pltpu.VMEM(one, bf16),
            pltpu.VMEM(one, bf16),
            pltpu.VMEM(gate, bf16),
            pltpu.VMEM(gate, bf16),
            pltpu.VMEM((group, PARAMS, width), f32),
            pltpu.VMEM((group, 2, depth), f32),
            pltpu.VMEM((n, 2, depth), f32),
            *gather_sems(n),
            *scatter_sems(n),
            *scatter_sems(n),
            dma((2, group)),
            dma((4,)),
            dma((3,)),
            dma((2, 4)),
            dma,
            dma((2,)),
            dma((3,)),
            pltpu.SemaphoreType.REGULAR,
            *share_sems("dp"),
            *share_sems("dp"),
            *share_sems("head"),
            *sum_sems(),
            *sum_sems(),
            *sum_sems(),
        ],
    )(
        lengths, low, out_part, hidden, terms, gated, wo, wbi, wg, par, pre, saved,
        normed_rows, stream, gain, resid, preffn_grad,
    )


def block_diagonal(weights, width):
    heads, size = weights.shape[0], weights.shape[1]
    placed = [
        jnp.pad(weights[i], ((i * size, width - (i + 1) * size),) * 2) for i in range(heads)
    ]
    return functools.reduce(jnp.add, placed)


def diagonal_blocks(dense, heads, size):
    blocks = [dense[i * size : (i + 1) * size, i * size : (i + 1) * size] for i in range(heads)]
    return jnp.stack(blocks, axis=1).transpose(1, 0, 2)


def shards(
    stream, doc_lengths, premix_gain, branch_weight, input_weight, conv_kernel, conv_bias,
    rate_weight, rate_bias, entry_weight, entry_bias, decay_param, output_weight, preffn_gain,
    ffn_gate, ffn_upward, ffn_down, cotangent,
):
    f32, bf16 = jnp.float32, jnp.bfloat16
    heads, size = rate_bias.shape
    chans = branch_weight.shape[1]
    width = -(-chans // LANES) * LANES

    slope = -DECAY_SCALE * jax.nn.softplus(decay_param.astype(f32))
    par = jnp.concatenate(
        [
            conv_bias[None].astype(f32),
            conv_kernel.astype(f32),
            rate_bias.reshape(1, -1).astype(f32),
            entry_bias.reshape(1, -1).astype(f32),
            slope[None],
        ]
    )
    par = jnp.pad(par, ((0, 0), (0, width - chans)), constant_values=-1.0)
    par = jnp.where((jnp.arange(width)[None] < chans) | (jnp.arange(PARAMS)[:, None] == DECAY), par, 0.0)
    wg = jnp.concatenate(
        [block_diagonal(rate_weight, width), block_diagonal(entry_weight, width)], axis=1
    )

    premix = premix_gain.astype(f32)[None]
    preffn = preffn_gain.astype(f32)[None]
    normed_rows, pre, saved, gated, wbi, wo, cot_rows, hidden_in, ffn_low = mixer_front(
        doc_lengths, stream, premix, branch_weight.T, input_weight.T, output_weight, wg, par,
        preffn, cotangent,
    )

    out_part, terms, far_terms, resid_grad, resid_low, preffn_grad = feed_forward(
        ffn_low, cot_rows, cotangent, hidden_in, preffn, ffn_gate, ffn_upward, ffn_down
    )

    layer_out, sums, last_terms, stream_grad, ob_grad, input_grad, gate_grad, dpar, gains = mixer_back(
        doc_lengths, resid_low, out_part, hidden_in, terms, gated, wo, wbi, wg, par, pre, saved,
        normed_rows, stream, premix, resid_grad, preffn_grad,
    )
    mine = lax.dynamic_index_in_dim(terms, lax.axis_index("dp"), keepdims=False)
    far = [far_terms[0], far_terms[1], last_terms]
    ffn_sums = [
        sum(
            (sums[i, k].astype(f32) for i in range(sums.shape[0])),
            mine[k].astype(f32) + far[k].astype(f32),
        )
        for k in range(3)
    ]
    ob_grad = ob_grad.reshape(2 * width, -1)
    output_grad = ob_grad[:chans].astype(f32)
    branch_grad = ob_grad[width : width + chans].astype(f32).T
    input_grad = input_grad.reshape(width, -1)[:chans].astype(f32).T
    gate_grad = gate_grad.reshape(width, -1).astype(f32)
    dpar = dpar[:, :chans]
    decay_grad = dpar[G_DECAY] * (-DECAY_SCALE * jax.nn.sigmoid(decay_param.astype(f32)))
    return (
        layer_out,
        stream_grad,
        gains[0],
        branch_grad,
        input_grad,
        dpar[G_TAP : G_TAP + CONVW],
        dpar[G_BIAS],
        diagonal_blocks(gate_grad[:, :width], heads, size),
        dpar[G_RATE].reshape(heads, size),
        diagonal_blocks(gate_grad[:, width:], heads, size),
        dpar[G_ENTRY].reshape(heads, size),
        decay_grad,
        output_grad,
        gains[1],
        ffn_sums[0],
        ffn_sums[1],
        ffn_sums[2],
    )


def solution(mesh):
    placed = (
        P(("dp", "head"), None),
        P("dp", None),
        P(),
        P(None, "head"),
        P(None, "head"),
        P(None, "head"),
        P("head"),
        P("head", None, None),
        P("head", None),
        P("head", None, None),
        P("head", None),
        P("head"),
        P("head", None),
        P(),
        P(None, "head"),
        P(None, "head"),
        P(None, "head"),
        P(("dp", "head"), None),
    )
    return jax.shard_map(
        shards,
        mesh=mesh,
        in_specs=placed,
        out_specs=(
            P(("dp", "head"), None),
            P(("dp", "head"), None),
            P(),
            P(None, "head"),
            P(None, "head"),
            P(None, "head"),
            P("head"),
            P("head", None, None),
            P("head", None),
            P("head", None, None),
            P("head", None),
            P("head"),
            P("head", None),
            P(),
            P("dp", "head"),
            P("dp", "head"),
            P("dp", "head"),
        ),
        check_vma=False,
    )
```
